32 devices in a mesh: groups: 2 (over y), replica: 4 (over z), tensor: 4 (over x, core).
Axes of the slice: x: 2, y: 2, z: 4, core: 2. Of those that a mesh axis runs over, the one named last changes fastest.
Arguments:
- queries: bfloat16 [512, 64, 128], P(('groups', 'replica'), 'tensor'), parts along dimension 0, may hold values from -256 to 256
- prefix_pool: bfloat16 [16, 64, 2, 8, 128], P(('groups', 'replica'), None, None, 'tensor'), parts along dimension 0, may hold values from -8 to 8
- page_table: int32 [12], P('groups'), parts along dimension 0, may hold values from 0 to 7, as said below
- suffix_kv: bfloat16 [512, 24, 2, 8, 128], P(('groups', 'replica'), None, None, 'tensor'), parts along dimension 0, may hold values from -9 to 9
- new_kv: bfloat16 [512, 2, 8, 128], P(('groups', 'replica'), None, 'tensor'), parts along dimension 0, may hold values from -10 to 10
- suffix_len: int32 [512], P(('groups', 'replica')), parts along dimension 0, may hold values from 0 to 24
- counts: int32 [8], P(('groups', 'replica')), parts along dimension 0, may hold values from 0 to 64, as said below
Outputs:
- attended: bfloat16 [512, 64, 128], P(('groups', 'replica'), 'tensor'), parts along dimension 0
The draws below stay inside these ranges and needn't reach their ends.
There are 2 independent parts, one for each index of `groups`. The reference program is written for one: setup_inputs(seed, part) draws one part's arguments, and reference() takes and returns one part's arrays. A program takes and returns all parts, laid end to end along the dimension named above; each array names one. Nothing has to cross between parts.
Inputs may be any that keep to these rules, and one draw needn't show every extreme that they name: `page_table`: 6 distinct pool slots, among them slots 0 and 7. The counts of replicas 2i and 2i + 1 sum to 64.
All inputs are finite; a program needn't handle non-finite values.
Results may differ from the reference program's by a relative error of at most 0.013.
Values may be sent and summed in bfloat16 or wider, within the bound.
No kernel may reach another device: no remote copies, remote signals or barrier semaphores. Data moves between devices by JAX's collectives and lax.ppermute only.
A program may use at most 64 MiB of HBM per device.

```python
import jax
import jax.numpy as jnp
from jax import lax

QH = 64
KVH = 8
HD = 128
PAGE = 64
BAL = 32
SUF = 24
CAP = 64
REQ = 256
SLOTS = 8
PAGES = 6
N_REPLICA = 4


def make_pool(pool_key):
    normal_base = jax.random.normal(pool_key, (SLOTS, PAGE, 2, KVH, HD), jnp.float32)
    return jnp.clip(normal_base, -6.0, 6.0)


def draw_prefix_pool(key, part):
    normal_base = make_pool(jax.random.fold_in(key, 11))
    return normal_base.astype(jnp.bfloat16)


def draw_queries(key, part):
    drawn_draw = jnp.clip(jax.random.normal(jax.random.fold_in(key, 23), (REQ, QH, HD), jnp.float32) * 2.5, -15.0, 15.0)
    return drawn_draw.astype(jnp.bfloat16)


def draw_page_table(key, part):
    first_key, second_key = jax.random.split(jax.random.fold_in(key, 37))
    middle_slots = 1 + jax.random.permutation(first_key, SLOTS - 2)[:PAGES - 2]
    chosen = jnp.concatenate([jnp.array([0, SLOTS - 1], jnp.int32), middle_slots.astype(jnp.int32)])
    return jax.random.permutation(second_key, chosen).astype(jnp.int32)


def draw_counts(key, part):
    pair_count = N_REPLICA // 2
    load_key, full_key, order_key = jax.random.split(jax.random.fold_in(key, 53), 3)
    heavy_load = jax.random.randint(load_key, (pair_count,), BAL, CAP + 1)
    full_pair = jax.random.randint(full_key, (), 0, pair_count)
    heavy_load = jnp.where(jnp.arange(pair_count) == full_pair, CAP, heavy_load)
    heavy_first = jax.random.randint(order_key, (pair_count,), 0, 2)
    even_load = jnp.where(heavy_first == 1, heavy_load, CAP - heavy_load)
    return jnp.stack([even_load, CAP - even_load], axis=1).reshape(N_REPLICA).astype(jnp.int32)


def place_ends(values, rng, smallest, high):
    extent = values.shape
    index_at = [jax.random.randint(jax.random.fold_in(rng, axis), (), 0, extent[axis]) for axis in range(len(extent))]
    values = values.at[tuple(index_at)].set(smallest)
    longest = extent.index(max(extent))
    index_at[longest] = (index_at[longest] + 1) % extent[longest]
    return values.at[tuple(index_at)].set(high)


def block_levels(key, shape, cuts, least, high):
    loudness, own = 1.0, jax.random.fold_in(key, 6)
    for position, blocks in cuts:
        steps = jnp.exp(jax.random.uniform(jax.random.fold_in(own, position), (blocks,), jnp.float32, least / len(cuts), high / len(cuts)))
        loudness = loudness * jnp.repeat(steps, shape[position] // blocks).reshape([-1 if axis == position else 1 for axis in range(len(shape))])
    return loudness


def scatter_about(own_key, extent, spread, most, cuts=(), held_as=jnp.bfloat16):
    level = block_levels(own_key, extent, cuts, -0.22, 0.18) if cuts else 1.0
    drawn = jax.random.normal(own_key, extent, jnp.float32) * spread * level
    return jnp.minimum(jnp.maximum(drawn, -most), most).astype(held_as)


def setup_inputs(seed: int = 0, part: int = 0) -> dict:
    arg_keys = jax.random.split(jax.random.key(seed), 8)
    part_keys = jax.random.split(jax.random.fold_in(arg_keys[7], part), 8)
    queries = draw_queries(jax.random.fold_in(jax.random.fold_in(arg_keys[7], part), 71), part)
    prefix_pool = draw_prefix_pool(jax.random.fold_in(jax.random.fold_in(arg_keys[7], part), 71), part)
    page_table = draw_page_table(jax.random.fold_in(jax.random.fold_in(arg_keys[7], part), 71), part)
    suffix_kv = scatter_about(part_keys[3], (REQ, SUF, 2, KVH, HD), 1.5, 9.0, ((0, 4), (3, 4)))
    new_kv = scatter_about(part_keys[4], (REQ, 2, KVH, HD), 1.7, 10.0, ((0, 4), (2, 4)))
    suffix_len = place_ends(jax.random.randint(part_keys[5], (REQ,), 0, SUF + 1), jax.random.fold_in(part_keys[5], 1), 0, SUF).astype(jnp.int32)
    counts = draw_counts(jax.random.fold_in(jax.random.fold_in(arg_keys[7], part), 71), part)
    return {"queries": queries, "prefix_pool": prefix_pool, "page_table": page_table, "suffix_kv": suffix_kv, "new_kv": new_kv, "suffix_len": suffix_len, "counts": counts}


masked_score = -1.0e30


def rounded_copy(values):
    return lax.optimization_barrier(values.astype(jnp.bfloat16)).astype(jnp.float32)


def reference(queries, prefix_pool, page_table, suffix_kv, new_kv, suffix_len, counts):
    group = QH // KVH
    factor_q = HD ** -0.5
    live_pool = prefix_pool[page_table.astype(jnp.int32)].reshape(PAGES * PAGE, 2, KVH, HD).astype(jnp.float32)
    prefix_keys = live_pool[:, 0]
    prefix_values = live_pool[:, 1]

    def one_block(block_item):
        block_q, block_suffix, block_new, block_len, block_count = block_item
        grouped = block_q.astype(jnp.float32).reshape(CAP, KVH, group, HD)
        suffix_all = block_suffix.astype(jnp.float32)
        new_all = block_new.astype(jnp.float32)
        prefix_scores = jnp.einsum("rgqd,kgd->rgqk", grouped, prefix_keys) * factor_q
        suffix_scores = jnp.einsum("rgqd,rkgd->rgqk", grouped, suffix_all[:, :, 0]) * factor_q
        kept_keys = jnp.arange(SUF, dtype=jnp.int32)[None, :] < block_len[:, None]
        suffix_scores = jnp.where(kept_keys[:, None, None, :], suffix_scores, masked_score)
        new_score = jnp.einsum("rgqd,rgd->rgq", grouped, new_all[:, 0]) * factor_q
        row_max = jnp.maximum(jnp.maximum(jnp.max(prefix_scores, axis=-1), jnp.max(suffix_scores, axis=-1)), new_score)
        prefix_weights = jnp.exp(prefix_scores - row_max[..., None])
        suffix_weights = jnp.exp(suffix_scores - row_max[..., None])
        new_weight = jnp.exp(new_score - row_max)
        row_total = jnp.sum(prefix_weights, axis=-1) + jnp.sum(suffix_weights, axis=-1) + new_weight
        accumulated = jnp.einsum("rgqk,kgd->rgqd", rounded_copy(prefix_weights), prefix_values)
        accumulated = accumulated + jnp.einsum("rgqk,rkgd->rgqd", rounded_copy(suffix_weights), suffix_all[:, :, 1])
        accumulated = accumulated + rounded_copy(new_weight)[..., None] * new_all[:, 1][:, :, None, :]
        result = accumulated / row_total[..., None]
        live_rows = jnp.arange(CAP, dtype=jnp.int32) < block_count
        result = jnp.where(live_rows[:, None, None, None], result, 0.0)
        return result.reshape(CAP, QH, HD).astype(jnp.bfloat16)

    blocks = (
        queries.reshape(N_REPLICA, CAP, QH, HD),
        suffix_kv.reshape(N_REPLICA, CAP, SUF, 2, KVH, HD),
        new_kv.reshape(N_REPLICA, CAP, 2, KVH, HD),
        suffix_len.reshape(N_REPLICA, CAP),
        counts,
    )
    return lax.map(one_block, blocks).reshape(REQ, QH, HD)
```

```python
import functools
import math

import jax
import jax.numpy as jnp
from jax import lax
from jax.experimental import pallas as pl
from jax.experimental.pallas import tpu as pltpu
from jax.sharding import PartitionSpec as P

masked_score = -1e30
lanes = 128


def one_hot(shape, condition):
    row = lax.broadcasted_iota(jnp.int32, shape, 0)
    column = lax.broadcasted_iota(jnp.int32, shape, 1)
    return jnp.where(condition(row, column), 1.0, 0.0).astype(jnp.bfloat16)


def head_concat(grouped, heads, group):
    row = lax.broadcasted_iota(jnp.int32, grouped.shape, 0)
    head = lax.rem(row, heads * group) // group
    values = grouped.astype(jnp.float32)
    parts = [jnp.where(head == g, values, 0.0).astype(jnp.bfloat16) for g in range(heads)]
    return jnp.concatenate(parts, axis=1)


def head_select(wide, heads, group):
    width = wide.shape[1] // heads
    shape = (wide.shape[0], width)
    head = lax.rem(lax.broadcasted_iota(jnp.int32, shape, 0), heads * group) // group
    result = wide[:, :width]
    for g in range(1, heads):
        result = jnp.where(head == g, wide[:, g * width : (g + 1) * width], result)
    return result


def split_page(raw, order, heads):
    sorted_rows = jnp.dot(order, raw, preferred_element_type=jnp.float32).astype(jnp.bfloat16)
    tokens = raw.shape[0] // (2 * heads)
    kinds = [sorted_rows[i * tokens : (i + 1) * tokens] for i in range(2 * heads)]
    return jnp.concatenate(kinds[:heads], axis=1), jnp.concatenate(kinds[heads:], axis=1)


def page_order(page_rows, kinds):
    tokens = page_rows // kinds
    return one_hot(
        (page_rows, page_rows),
        lambda row, column: column == lax.rem(row, tokens) * kinds + row // tokens,
    )


def slot_live(table_ref, slot):
    found = jnp.int32(0)
    for index in range(table_ref.shape[0]):
        found = jnp.maximum(found, (table_ref[index] == slot).astype(jnp.int32))
    return found


def live_lanes(table_ref, slots, page):
    column = lax.broadcasted_iota(jnp.int32, (1, len(slots) * page), 1)
    live = jnp.zeros_like(column)
    for place, slot in enumerate(slots):
        live = jnp.where(column // page == place, slot_live(table_ref, slot), live)
    return live


def fill_tables(raws, order, keys_ref, values_ref, heads, page):
    place = 0
    page_rows = page * 2 * heads
    for raw_ref in raws:
        for at in range(0, raw_ref.shape[0], page_rows):
            keys, values = split_page(raw_ref[at : at + page_rows], order, heads)
            keys_ref[place : place + page] = keys
            values_ref[place : place + page] = values
            place += page


def contract_last(a, b):
    return lax.dot_general(a, b, (((1,), (1,)), ((), ())), preferred_element_type=jnp.float32)


def local_body(
    sizes, table_ref, lens_ref, q_ref, own_ref, suffix_ref, new_ref, acc_ref, stat_ref, keys_ref, values_ref
):
    heads, group, page, suffix, scale, batch = sizes
    kinds = 2 * heads
    row_heads = heads * group
    me = lax.axis_index("replica")
    slots = own_ref.shape[0] // (page * kinds)
    fill_tables([own_ref], page_order(page * kinds, kinds), keys_ref, values_ref, heads, page)
    live = live_lanes(table_ref, [me * slots + s for s in range(slots)], page)
    cached = suffix * kinds
    fresh = batch * kinds
    width = cached + fresh
    column = lax.broadcasted_iota(jnp.int32, (row_heads, width), 1)
    head = lax.broadcasted_iota(jnp.int32, (row_heads, width), 0) // group
    never = jnp.int32(1 << 20)
    token = jnp.where(
        (column < cached) & (lax.rem(column, kinds) == head), column // kinds, never
    )
    block_rows = batch * row_heads
    keys = keys_ref[...]
    values = values_ref[...]

    def one_block(step, carry):
        rows = pl.ds(pl.multiple_of(step * block_rows, block_rows), block_rows)
        q = q_ref[rows]
        prefix = contract_last(head_concat(q, heads, group), keys) * scale
        prefix = jnp.where(live > 0, prefix, masked_score)
        new_rows = new_ref[pl.ds(pl.multiple_of(step * fresh, fresh), fresh)]
        own_kv = []
        scores = []
        for i in range(batch):
            at = pl.multiple_of((step * batch + i) * cached, cached)
            kv = jnp.concatenate([suffix_ref[pl.ds(at, cached)], new_rows], axis=0)
            own_kv.append(kv)
            place = jnp.where(column == cached + i * kinds + head, -1, token)
            score = contract_last(q[i * row_heads : (i + 1) * row_heads], kv) * scale
            scores.append(jnp.where(place < lens_ref[step * batch + i], score, masked_score))
        score = jnp.concatenate(scores, axis=0)
        row_max = jnp.maximum(
            jnp.max(prefix, axis=1, keepdims=True), jnp.max(score, axis=1, keepdims=True)
        )
        weights = jnp.exp2(score - row_max)
        prefix_weights = jnp.exp2(prefix - row_max)
        total = jnp.sum(weights, axis=1, keepdims=True) + jnp.sum(
            prefix_weights, axis=1, keepdims=True
        )
        rounded = pltpu.roll(weights, heads, 1).astype(jnp.bfloat16)
        attended = [
            jnp.dot(
                rounded[i * row_heads : (i + 1) * row_heads],
                own_kv[i],
                preferred_element_type=jnp.float32,
            )
            for i in range(batch)
        ]
        wide = jnp.dot(
            prefix_weights.astype(jnp.bfloat16), values, preferred_element_type=jnp.float32
        )
        acc_ref[rows] = jnp.concatenate(attended, axis=0) + head_select(wide, heads, group)
        lane = lax.broadcasted_iota(jnp.int32, (block_rows, lanes), 1)
        stat_ref[rows] = jnp.where(lane < lanes // 2, row_max, total)
        return carry

    lax.fori_loop(0, q_ref.shape[0] // block_rows, one_block, 0)


def finish_body(sizes, shifts, *refs):
    heads, group, page, scale, block_rows, replicas = sizes
    table_ref, count_ref, q_ref, acc_ref, stat_ref = refs[:5]
    raws = refs[5 : 5 + len(shifts)]
    out_ref, keys_ref, values_ref = refs[5 + len(shifts) :]
    kinds = 2 * heads
    row_heads = heads * group
    me = lax.axis_index("replica")
    slots = raws[0].shape[0] // (page * kinds)
    fill_tables(raws, page_order(page * kinds, kinds), keys_ref, values_ref, heads, page)
    owners = [lax.rem(me + replicas - shift, replicas) for shift in shifts]
    live = live_lanes(
        table_ref, [owner * slots + s for owner in owners for s in range(slots)], page
    )
    live_rows = count_ref[0] * row_heads
    keys = keys_ref[...]
    values = values_ref[...]
    for start in range(0, q_ref.shape[0], block_rows):
        rows = pl.ds(start, block_rows)
        score = contract_last(head_concat(q_ref[rows], heads, group), keys) * scale
        score = jnp.where(live > 0, score, masked_score)
        stat = stat_ref[rows]
        earlier_max = stat[:, :1]
        row_max = jnp.maximum(earlier_max, jnp.max(score, axis=1, keepdims=True))
        weights = jnp.exp2(score - row_max)
        factor = jnp.exp2(earlier_max - row_max)
        total = stat[:, lanes // 2 : lanes // 2 + 1] * factor + jnp.sum(
            weights, axis=1, keepdims=True
        )
        wide = jnp.dot(weights.astype(jnp.bfloat16), values, preferred_element_type=jnp.float32)
        attended = acc_ref[rows] * factor + head_select(wide, heads, group)
        result = attended / total
        row = start + lax.broadcasted_iota(jnp.int32, result.shape, 0)
        out_ref[rows] = jnp.where(row < live_rows, result, 0.0).astype(jnp.bfloat16)


def vmem():
    return pl.BlockSpec(memory_space=pltpu.VMEM)


def smem():
    return pl.BlockSpec(memory_space=pltpu.SMEM)


def shards(replicas, queries, prefix_pool, page_table, suffix_kv, new_kv, suffix_len, counts):
    requests, head_count, width = queries.shape
    slots, page, unused, heads, width = prefix_pool.shape
    suffix = suffix_kv.shape[1]
    group = head_count // heads
    kinds = 2 * heads
    scale = width**-0.5 * math.log2(math.e)
    q = queries.reshape(requests * head_count, width)
    raw = prefix_pool.reshape(slots * page * kinds, width)
    batch = (-suffix * kinds) % lanes // kinds
    rows = requests * head_count
    others = [
        lax.ppermute(raw, "replica", [(i, (i + shift) % replicas) for i in range(replicas)])
        for shift in range(1, replicas)
    ]
    sizes = (heads, group, page, suffix, scale, batch)
    acc, stat = pl.pallas_call(
        functools.partial(local_body, sizes),
        out_shape=[jax.ShapeDtypeStruct((rows, width), jnp.float32)] * 2,
        in_specs=[smem(), smem(), vmem(), vmem(), vmem(), vmem()],
        out_specs=[vmem(), vmem()],
        scratch_shapes=[pltpu.VMEM((slots * page, heads * width), jnp.bfloat16)] * 2,
        compiler_params=pltpu.CompilerParams(vmem_limit_bytes=24 << 20),
        cost_estimate=pl.CostEstimate(
            flops=4 * rows * (slots * page + suffix) * width,
            bytes_accessed=6 << 20,
            transcendentals=rows * 256,
        ),
        name="local_part",
    )(
        page_table,
        suffix_len,
        q,
        raw,
        suffix_kv.reshape(requests * suffix * kinds, width),
        new_kv.reshape(requests * kinds, width),
    )
    tokens = (replicas - 1) * slots * page
    sizes = (heads, group, page, scale, 256, replicas)
    out = pl.pallas_call(
        functools.partial(finish_body, sizes, tuple(range(1, replicas))),
        out_shape=jax.ShapeDtypeStruct((rows, width), jnp.bfloat16),
        in_specs=[smem(), smem()] + [vmem()] * (3 + len(others)),
        out_specs=vmem(),
        scratch_shapes=[pltpu.VMEM((tokens, heads * width), jnp.bfloat16)] * 2,
        compiler_params=pltpu.CompilerParams(vmem_limit_bytes=24 << 20),
        cost_estimate=pl.CostEstimate(
            flops=4 * rows * tokens * width, bytes_accessed=3 << 20, transcendentals=rows * tokens
        ),
        name="finish_part",
    )(page_table, counts, q, acc, stat, *others)
    return out.reshape(requests, head_count, width)


def solution(mesh):
    placed = (
        P(("groups", "replica"), "tensor", None),
        P(("groups", "replica"), None, None, "tensor", None),
        P("groups"),
        P(("groups", "replica"), None, None, "tensor", None),
        P(("groups", "replica"), None, "tensor", None),
        P(("groups", "replica")),
        P(("groups", "replica")),
    )
    return jax.shard_map(
        functools.partial(shards, mesh.shape["replica"]),
        mesh=mesh,
        in_specs=placed,
        out_specs=P(("groups", "replica"), "tensor", None),
        check_vma=False,
    )
```

```python
import functools
import math

import jax
import jax.numpy as jnp
from jax import lax
from jax.experimental import pallas as pl
from jax.experimental.pallas import tpu as pltpu
from jax.sharding import PartitionSpec as P

masked_score = -1e30
lanes = 128


def one_hot(shape, condition):
    row = lax.broadcasted_iota(jnp.int32, shape, 0)
    column = lax.broadcasted_iota(jnp.int32, shape, 1)
    return jnp.where(condition(row, column), 1.0, 0.0).astype(jnp.bfloat16)


def head_concat(grouped, heads, group):
    row = lax.broadcasted_iota(jnp.int32, grouped.shape, 0)
    head = lax.rem(row, heads * group) // group
    values = grouped.astype(jnp.float32)
    parts = [jnp.where(head == g, values, 0.0).astype(jnp.bfloat16) for g in range(heads)]
    return jnp.concatenate(parts, axis=1)


def head_select(wide, heads, group):
    width = wide.shape[1] // heads
    shape = (wide.shape[0], width)
    head = lax.rem(lax.broadcasted_iota(jnp.int32, shape, 0), heads * group) // group
    result = wide[:, :width]
    for g in range(1, heads):
        result = jnp.where(head == g, wide[:, g * width : (g + 1) * width], result)
    return result


def split_page(raw, order, heads):
    sorted_rows = jnp.dot(order, raw, preferred_element_type=jnp.float32).astype(jnp.bfloat16)
    tokens = raw.shape[0] // (2 * heads)
    kinds = [sorted_rows[i * tokens : (i + 1) * tokens] for i in range(2 * heads)]
    return jnp.concatenate(kinds[:heads], axis=1), jnp.concatenate(kinds[heads:], axis=1)


def page_order(page_rows, kinds):
    tokens = page_rows // kinds
    return one_hot(
        (page_rows, page_rows),
        lambda row, column: column == lax.rem(row, tokens) * kinds + row // tokens,
    )


def slot_bias(table_ref, slot):
    found = table_ref[0] == slot
    for index in range(1, table_ref.shape[0]):
        found = found | (table_ref[index] == slot)
    return jnp.where(found, 0.0, masked_score)


def live_bias(table_ref, slots, page, rows):
    column = lax.broadcasted_iota(jnp.int32, (rows, len(slots) * page), 1)
    bias = jnp.zeros(column.shape, jnp.float32)
    for place, slot in enumerate(slots):
        bias = jnp.where(column // page == place, slot_bias(table_ref, slot), bias)
    return bias


def fill_tables(raws, order, keys_ref, values_ref, heads, page):
    place = 0
    page_rows = page * 2 * heads
    for raw_ref in raws:
        for at in range(0, raw_ref.shape[0], page_rows):
            keys, values = split_page(raw_ref[at : at + page_rows], order, heads)
            keys_ref[place : place + page] = keys
            values_ref[place : place + page] = values
            place += page


def contract_last(a, b):
    return lax.dot_general(a, b, (((1,), (1,)), ((), ())), preferred_element_type=jnp.float32)


def local_body(sizes, shifts, *refs):
    heads, group, page, suffix, scale, batch, replicas, unroll = sizes
    table_hbm, lens_hbm, q_hbm, own_hbm, suffix_hbm, new_hbm = refs[:6]
    acc_ref, stat_ref, wide_ref, bias_ref = refs[6:10]
    table_ref, lens_ref, q_ref, own_ref, suffix_ref, new_ref = refs[10:16]
    keys_ref, values_ref, sems = refs[16:]
    pairs = [
        (own_hbm, own_ref),
        (table_hbm, table_ref),
        (q_hbm, q_ref),
        (new_hbm, new_ref),
        (lens_hbm, lens_ref),
        (suffix_hbm, suffix_ref),
    ]
    copies = [
        pltpu.make_async_copy(source, target, sems.at[i])
        for i, (source, target) in enumerate(pairs)
    ]
    for copy in copies:
        copy.start()
    kinds = 2 * heads
    row_heads = heads * group
    me = lax.axis_index("replica")
    slots = own_ref.shape[0] // (page * kinds)
    order = page_order(page * kinds, kinds)
    for copy in copies[:2]:
        copy.wait()
    fill_tables([own_ref], order, keys_ref, values_ref, heads, page)
    live = live_bias(table_ref, [me * slots + s for s in range(slots)], page, 1)
    owners = [lax.rem(me + replicas - shift, replicas) for shift in shifts]
    bias_ref[...] = live_bias(
        table_ref, [owner * slots + s for owner in owners for s in range(slots)], page, 8
    )
    cached = suffix * kinds
    fresh = batch * kinds
    width = cached + fresh
    column = lax.broadcasted_iota(jnp.int32, (row_heads, width), 1)
    head = lax.broadcasted_iota(jnp.int32, (row_heads, width), 0) // group
    never = jnp.int32(1 << 20)
    token = jnp.where(
        (column < cached) & (lax.rem(column, kinds) == head), column // kinds, never
    )
    block_rows = batch * row_heads
    for copy in copies[2:]:
        copy.wait()
    keys = keys_ref[...]
    values = values_ref[...]

    def one_block(step, carry):
        rows = pl.ds(pl.multiple_of(step * block_rows, block_rows), block_rows)
        q = q_ref[rows]
        q_wide = head_concat(q, heads, group)
        wide_ref[rows] = q_wide
        prefix = contract_last(q_wide, keys) * scale + live
        new_rows = new_ref[pl.ds(pl.multiple_of(step * fresh, fresh), fresh)]
        own_kv = []
        scores = []
        for i in range(batch):
            at = pl.multiple_of((step * batch + i) * cached, cached)
            kv = jnp.concatenate([suffix_ref[pl.ds(at, cached)], new_rows], axis=0)
            own_kv.append(kv)
            place = jnp.where(column == cached + i * kinds + head, -1, token)
            score = contract_last(q[i * row_heads : (i + 1) * row_heads], kv) * scale
            scores.append(jnp.where(place < lens_ref[step * batch + i], score, masked_score))
        score = jnp.concatenate(scores, axis=0)
        row_max = jnp.maximum(
            jnp.max(prefix, axis=1, keepdims=True), jnp.max(score, axis=1, keepdims=True)
        )
        weights = jnp.exp2(score - row_max)
        prefix_weights = jnp.exp2(prefix - row_max)
        total = jnp.sum(weights, axis=1, keepdims=True) + jnp.sum(
            prefix_weights, axis=1, keepdims=True
        )
        rounded = pltpu.roll(weights, heads, 1).astype(jnp.bfloat16)
        attended = [
            jnp.dot(
                rounded[i * row_heads : (i + 1) * row_heads],
                own_kv[i],
                preferred_element_type=jnp.float32,
            )
            for i in range(batch)
        ]
        wide = jnp.dot(
            prefix_weights.astype(jnp.bfloat16), values, preferred_element_type=jnp.float32
        )
        acc_ref[rows] = jnp.concatenate(attended, axis=0) + head_select(wide, heads, group)
        lane = lax.broadcasted_iota(jnp.int32, (block_rows, lanes), 1)
        stat_ref[rows] = jnp.where(lane < lanes // 2, row_max, total)
        return carry

    lax.fori_loop(0, q_ref.shape[0] // block_rows, one_block, 0, unroll=unroll)


def finish_body(sizes, *refs):
    heads, group, page, scale, block_rows = sizes
    count_ref, wide_ref, acc_ref, stat_ref, bias_ref = refs[:5]
    raws = refs[5:-5]
    out_hbm, out_ref, keys_ref, values_ref, sems = refs[-5:]
    kinds = 2 * heads
    fill_tables(raws, page_order(page * kinds, kinds), keys_ref, values_ref, heads, page)
    keys = keys_ref[...]
    values = values_ref[...]
    live = bias_ref[:1]
    live_rows = count_ref[...] * (heads * group)
    copies = []
    for block, start in enumerate(range(0, wide_ref.shape[0], block_rows)):
        rows = pl.ds(start, block_rows)
        score = contract_last(wide_ref[rows], keys) * scale + live
        stat = stat_ref[rows]
        earlier_max = stat[:, :1]
        row_max = jnp.maximum(earlier_max, jnp.max(score, axis=1, keepdims=True))
        weights = jnp.exp2(score - row_max)
        factor = jnp.exp2(earlier_max - row_max)
        total = stat[:, lanes // 2 : lanes // 2 + 1] * factor + jnp.sum(weights, axis=1, keepdims=True)
        wide = jnp.dot(weights.astype(jnp.bfloat16), values, preferred_element_type=jnp.float32)
        attended = acc_ref[rows] * factor + head_select(wide, heads, group)
        row = start + lax.broadcasted_iota(jnp.int32, total.shape, 0)
        share = jnp.where(row < live_rows, 1.0 / total, 0.0)
        out_ref[rows] = (attended * share).astype(jnp.bfloat16)
        copies.append(pltpu.make_async_copy(out_ref.at[rows], out_hbm.at[rows], sems.at[block]))
        copies[-1].start()
    for copy in copies:
        copy.wait()


def vmem():
    return pl.BlockSpec(memory_space=pltpu.VMEM)


def hbm():
    return pl.BlockSpec(memory_space=pltpu.HBM)


def shards(replicas, queries, prefix_pool, page_table, suffix_kv, new_kv, suffix_len, counts):
    requests, head_count, width = queries.shape
    slots, page, unused, heads, width = prefix_pool.shape
    suffix = suffix_kv.shape[1]
    group = head_count // heads
    kinds = 2 * heads
    scale = width**-0.5 * math.log2(math.e)
    q = queries.reshape(requests * head_count, width)
    raw = prefix_pool.reshape(slots * page * kinds, width)
    batch = (-suffix * kinds) % lanes // kinds
    rows = requests * head_count
    others = [
        lax.ppermute(raw, "replica", [(i, (i + shift) % replicas) for i in range(replicas)])
        for shift in range(1, replicas)
    ]
    shifts = tuple(range(1, replicas))
    tokens = len(shifts) * slots * page
    suffix_rows = requests * suffix * kinds
    sizes = (heads, group, page, suffix, scale, batch, replicas, 2)
    acc, stat, q_wide, bias = pl.pallas_call(
        functools.partial(local_body, sizes, shifts),
        out_shape=[
            jax.ShapeDtypeStruct((rows, width), jnp.float32),
            jax.ShapeDtypeStruct((rows, lanes), jnp.float32),
            jax.ShapeDtypeStruct((rows, heads * width), jnp.bfloat16),
            jax.ShapeDtypeStruct((8, tokens), jnp.float32),
        ],
        in_specs=[hbm()] * 6,
        out_specs=[vmem()] * 4,
        scratch_shapes=[
            pltpu.SMEM(page_table.shape, jnp.int32),
            pltpu.SMEM(suffix_len.shape, jnp.int32),
            pltpu.VMEM(q.shape, jnp.bfloat16),
            pltpu.VMEM(raw.shape, jnp.bfloat16),
            pltpu.VMEM((suffix_rows, width), jnp.bfloat16),
            pltpu.VMEM((requests * kinds, width), jnp.bfloat16),
            pltpu.VMEM((slots * page, heads * width), jnp.bfloat16),
            pltpu.VMEM((slots * page, heads * width), jnp.bfloat16),
            pltpu.SemaphoreType.DMA((6,)),
        ],
        compiler_params=pltpu.CompilerParams(vmem_limit_bytes=24 << 20),
        cost_estimate=pl.CostEstimate(
            flops=4 * rows * (slots * page + suffix) * width,
            bytes_accessed=6 << 20,
            transcendentals=rows * 256,
        ),
        name="local_part",
    )(*[
        pltpu.with_memory_space_constraint(value, pltpu.HBM)
        for value in (
            page_table,
            suffix_len,
            q,
            raw,
            suffix_kv.reshape(suffix_rows, width),
            new_kv.reshape(requests * kinds, width),
        )
    ])
    sizes = (heads, group, page, scale, 256)
    out = pl.pallas_call(
        functools.partial(finish_body, sizes),
        out_shape=jax.ShapeDtypeStruct((rows, width), jnp.bfloat16),
        in_specs=[vmem()] * (5 + len(others)),
        out_specs=hbm(),
        scratch_shapes=[
            pltpu.VMEM((rows, width), jnp.bfloat16),
            pltpu.VMEM((tokens, heads * width), jnp.bfloat16),
            pltpu.VMEM((tokens, heads * width), jnp.bfloat16),
            pltpu.SemaphoreType.DMA((rows // 256,)),
        ],
        compiler_params=pltpu.CompilerParams(vmem_limit_bytes=24 << 20),
        cost_estimate=pl.CostEstimate(
            flops=4 * rows * tokens * width, bytes_accessed=3 << 20, transcendentals=rows * tokens
        ),
        name="finish_part",
    )(counts.reshape(1, 1), q_wide, acc, stat, bias, *others)
    return out.reshape(requests, head_count, width)


def solution(mesh):
    placed = (
        P(("groups", "replica"), "tensor", None),
        P(("groups", "replica"), None, None, "tensor", None),
        P("groups"),
        P(("groups", "replica"), None, None, "tensor", None),
        P(("groups", "replica"), None, "tensor", None),
        P(("groups", "replica")),
        P(("groups", "replica")),
    )
    return jax.shard_map(
        functools.partial(shards, mesh.shape["replica"]),
        mesh=mesh,
        in_specs=placed,
        out_specs=P(("groups", "replica"), "tensor", None),
        check_vma=False,
    )
```

```python
import functools
import math

import jax
import jax.numpy as jnp
from jax import lax
from jax.experimental import pallas as pl
from jax.experimental.pallas import tpu as pltpu
from jax.sharding import PartitionSpec as P

masked_score = -1e30
lanes = 128


def one_hot(shape, condition):
    row = lax.broadcasted_iota(jnp.int32, shape, 0)
    column = lax.broadcasted_iota(jnp.int32, shape, 1)
    return jnp.where(condition(row, column), 1.0, 0.0).astype(jnp.bfloat16)


def head_concat(grouped, heads, group):
    row = lax.broadcasted_iota(jnp.int32, grouped.shape, 0)
    head = lax.rem(row, heads * group) // group
    values = grouped.astype(jnp.float32)
    parts = [jnp.where(head == g, values, 0.0).astype(jnp.bfloat16) for g in range(heads)]
    return jnp.concatenate(parts, axis=1)


def head_select(wide, heads, group):
    width = wide.shape[1] // heads
    shape = (wide.shape[0], width)
    head = lax.rem(lax.broadcasted_iota(jnp.int32, shape, 0), heads * group) // group
    result = wide[:, :width]
    for g in range(1, heads):
        result = jnp.where(head == g, wide[:, g * width : (g + 1) * width], result)
    return result


def split_page(raw, order, heads):
    sorted_rows = jnp.dot(order, raw, preferred_element_type=jnp.float32).astype(jnp.bfloat16)
    tokens = raw.shape[0] // (2 * heads)
    kinds = [sorted_rows[i * tokens : (i + 1) * tokens] for i in range(2 * heads)]
    return jnp.concatenate(kinds[:heads], axis=1), jnp.concatenate(kinds[heads:], axis=1)


def page_order(page_rows, kinds):
    tokens = page_rows // kinds
    return one_hot(
        (page_rows, page_rows),
        lambda row, column: column == lax.rem(row, tokens) * kinds + row // tokens,
    )


def slot_bias(table_ref, slot):
    found = table_ref[0] == slot
    for index in range(1, table_ref.shape[0]):
        found = found | (table_ref[index] == slot)
    return jnp.where(found, 0.0, masked_score)


def live_bias(table_ref, slots, page, rows):
    column = lax.broadcasted_iota(jnp.int32, (rows, len(slots) * page), 1)
    bias = jnp.zeros(column.shape, jnp.float32)
    for place, slot in enumerate(slots):
        bias = jnp.where(column // page == place, slot_bias(table_ref, slot), bias)
    return bias


def fill_tables(raws, order, keys_ref, values_ref, heads, page):
    place = 0
    page_rows = page * 2 * heads
    for raw_ref in raws:
        for at in range(0, raw_ref.shape[0], page_rows):
            keys, values = split_page(raw_ref[at : at + page_rows], order, heads)
            keys_ref[place : place + page] = keys
            values_ref[place : place + page] = values
            place += page


def contract_last(a, b):
    return lax.dot_general(a, b, (((1,), (1,)), ((), ())), preferred_element_type=jnp.float32)


def local_body(sizes, early_owners, late_owners, *refs):
    heads, group, page, suffix, scale, batch, replicas, unroll = sizes
    table_hbm, lens_hbm, q_hbm, own_hbm, suffix_hbm, new_hbm = refs[:6]
    early = refs[6 : 6 + len(early_owners)]
    refs = refs[6 + len(early_owners) :]
    acc_ref, stat_ref, wide_ref, bias_ref = refs[:4]
    table_ref, lens_ref, q_ref, own_ref, suffix_ref, new_ref = refs[4:10]
    keys_ref, values_ref, sems = refs[10:]
    pairs = [
        (own_hbm, own_ref),
        (table_hbm, table_ref),
        (q_hbm, q_ref),
        (new_hbm, new_ref),
        (lens_hbm, lens_ref),
        (suffix_hbm, suffix_ref),
    ]
    copies = [
        pltpu.make_async_copy(source, target, sems.at[i])
        for i, (source, target) in enumerate(pairs)
    ]
    for copy in copies:
        copy.start()
    kinds = 2 * heads
    row_heads = heads * group
    me = lax.axis_index("replica")
    slots = own_ref.shape[0] // (page * kinds)
    order = page_order(page * kinds, kinds)
    for copy in copies[:2]:
        copy.wait()
    fill_tables([own_ref, *early], order, keys_ref, values_ref, heads, page)
    owners = [me] + [owner(me, replicas) for owner in early_owners]
    live = live_bias(
        table_ref, [owner * slots + s for owner in owners for s in range(slots)], page, 1
    )
    owners = [owner(me, replicas) for owner in late_owners]
    bias_ref[...] = live_bias(
        table_ref, [owner * slots + s for owner in owners for s in range(slots)], page, 8
    )
    cached = suffix * kinds
    fresh = batch * kinds
    width = cached + fresh
    column = lax.broadcasted_iota(jnp.int32, (row_heads, width), 1)
    head = lax.broadcasted_iota(jnp.int32, (row_heads, width), 0) // group
    never = jnp.int32(1 << 20)
    token = jnp.where(
        (column < cached) & (lax.rem(column, kinds) == head), column // kinds, never
    )
    block_rows = batch * row_heads
    for copy in copies[2:]:
        copy.wait()
    keys = keys_ref[...]
    values = values_ref[...]

    def one_block(step, carry):
        rows = pl.ds(pl.multiple_of(step * block_rows, block_rows), block_rows)
        q = q_ref[rows]
        q_wide = head_concat(q, heads, group)
        wide_ref[rows] = q_wide
        prefix = contract_last(q_wide, keys) * scale + live
        new_rows = new_ref[pl.ds(pl.multiple_of(step * fresh, fresh), fresh)]
        own_kv = []
        scores = []
        for i in range(batch):
            at = pl.multiple_of((step * batch + i) * cached, cached)
            kv = jnp.concatenate([suffix_ref[pl.ds(at, cached)], new_rows], axis=0)
            own_kv.append(kv)
            place = jnp.where(column == cached + i * kinds + head, -1, token)
            score = contract_last(q[i * row_heads : (i + 1) * row_heads], kv) * scale
            scores.append(jnp.where(place < lens_ref[step * batch + i], score, masked_score))
        score = jnp.concatenate(scores, axis=0)
        row_max = jnp.maximum(
            jnp.max(prefix, axis=1, keepdims=True), jnp.max(score, axis=1, keepdims=True)
        )
        weights = jnp.exp2(score - row_max)
        prefix_weights = jnp.exp2(prefix - row_max)
        total = jnp.sum(weights, axis=1, keepdims=True) + jnp.sum(
            prefix_weights, axis=1, keepdims=True
        )
        rounded = pltpu.roll(weights, heads, 1).astype(jnp.bfloat16)
        attended = [
            jnp.dot(
                rounded[i * row_heads : (i + 1) * row_heads],
                own_kv[i],
                preferred_element_type=jnp.float32,
            )
            for i in range(batch)
        ]
        wide = jnp.dot(
            prefix_weights.astype(jnp.bfloat16), values, preferred_element_type=jnp.float32
        )
        acc_ref[rows] = jnp.concatenate(attended, axis=0) + head_select(wide, heads, group)
        lane = lax.broadcasted_iota(jnp.int32, (block_rows, lanes), 1)
        stat_ref[rows] = jnp.where(lane < lanes // 2, row_max, total)
        return carry

    lax.fori_loop(0, q_ref.shape[0] // block_rows, one_block, 0, unroll=unroll)


def finish_body(sizes, choices, *refs):
    heads, group, page, scale, block_rows, replicas = sizes
    count_ref, wide_ref, acc_ref, stat_ref, bias_ref = refs[:5]
    raws = refs[5:-5]
    out_hbm, out_ref, keys_ref, values_ref, sems = refs[-5:]
    kinds = 2 * heads
    order = page_order(page * kinds, kinds)
    me = lax.axis_index("replica")
    for applies, chosen in choices:

        @pl.when(applies(me, replicas))
        def fill(chosen=chosen):
            fill_tables(
                [raws[i] for i in chosen], order, keys_ref, values_ref, heads, page
            )

    keys = keys_ref[...]
    values = values_ref[...]
    live = bias_ref[:1]
    live_rows = count_ref[...] * (heads * group)
    copies = []
    for block, start in enumerate(range(0, wide_ref.shape[0], block_rows)):
        rows = pl.ds(start, block_rows)
        score = contract_last(wide_ref[rows], keys) * scale + live
        stat = stat_ref[rows]
        earlier_max = stat[:, :1]
        row_max = jnp.maximum(earlier_max, jnp.max(score, axis=1, keepdims=True))
        weights = jnp.exp2(score - row_max)
        factor = jnp.exp2(earlier_max - row_max)
        total = stat[:, lanes // 2 : lanes // 2 + 1] * factor + jnp.sum(weights, axis=1, keepdims=True)
        wide = jnp.dot(weights.astype(jnp.bfloat16), values, preferred_element_type=jnp.float32)
        attended = acc_ref[rows] * factor + head_select(wide, heads, group)
        row = start + lax.broadcasted_iota(jnp.int32, total.shape, 0)
        share = jnp.where(row < live_rows, 1.0 / total, 0.0)
        out_ref[rows] = (attended * share).astype(jnp.bfloat16)
        copies.append(pltpu.make_async_copy(out_ref.at[rows], out_hbm.at[rows], sems.at[block]))
        copies[-1].start()
    for copy in copies:
        copy.wait()


def vmem():
    return pl.BlockSpec(memory_space=pltpu.VMEM)


def hbm():
    return pl.BlockSpec(memory_space=pltpu.HBM)


def line_plan(raw):
    def swap(values, pairs):
        return lax.ppermute(values, "replica", pairs)

    near = swap(raw, [(0, 1), (1, 0), (2, 3), (3, 2)])
    middle = swap(raw, [(1, 2), (2, 1)])
    ends = swap(raw, [(0, 3), (3, 0)])
    passed = swap(near, [(1, 2), (2, 1)])
    outward = swap(middle, [(1, 0), (2, 3)])
    return (
        [near],
        [lambda me, n: jnp.bitwise_xor(me, 1)],
        [middle, ends, passed, outward],
        [lambda me, n: jnp.bitwise_xor(me, 3), lambda me, n: jnp.bitwise_xor(me, 2)],
        [
            (lambda me, n: (me == 1) | (me == 2), (0, 2)),
            (lambda me, n: (me == 0) | (me == 3), (1, 3)),
        ],
    )


def direct_plan(raw, replicas):
    shifts = range(1, replicas)
    late = [
        lax.ppermute(raw, "replica", [(i, (i + shift) % replicas) for i in range(replicas)])
        for shift in shifts
    ]
    owners = [lambda me, n, shift=shift: lax.rem(me + n - shift, n) for shift in shifts]
    return [], [], late, owners, [(lambda me, n: me >= 0, tuple(range(len(late))))]


def gather_plan(raw, replicas):
    return line_plan(raw) if replicas == 4 else direct_plan(raw, replicas)


def shards(replicas, queries, prefix_pool, page_table, suffix_kv, new_kv, suffix_len, counts):
    requests, head_count, width = queries.shape
    slots, page, unused, heads, width = prefix_pool.shape
    suffix = suffix_kv.shape[1]
    group = head_count // heads
    kinds = 2 * heads
    scale = width**-0.5 * math.log2(math.e)
    q = queries.reshape(requests * head_count, width)
    raw = prefix_pool.reshape(slots * page * kinds, width)
    batch = (-suffix * kinds) % lanes // kinds
    rows = requests * head_count
    early, early_owners, late, late_owners, choices = gather_plan(raw, replicas)
    tokens = len(late_owners) * slots * page
    suffix_rows = requests * suffix * kinds
    sizes = (heads, group, page, suffix, scale, batch, replicas, 2)
    acc, stat, q_wide, bias = pl.pallas_call(
        functools.partial(local_body, sizes, early_owners, late_owners),
        out_shape=[
            jax.ShapeDtypeStruct((rows, width), jnp.float32),
            jax.ShapeDtypeStruct((rows, lanes), jnp.float32),
            jax.ShapeDtypeStruct((rows, heads * width), jnp.bfloat16),
            jax.ShapeDtypeStruct((8, tokens), jnp.float32),
        ],
        in_specs=[hbm()] * 6 + [vmem()] * len(early),
        out_specs=[vmem()] * 4,
        scratch_shapes=[
            pltpu.SMEM(page_table.shape, jnp.int32),
            pltpu.SMEM(suffix_len.shape, jnp.int32),
            pltpu.VMEM(q.shape, jnp.bfloat16),
            pltpu.VMEM(raw.shape, jnp.bfloat16),
            pltpu.VMEM((suffix_rows, width), jnp.bfloat16),
            pltpu.VMEM((requests * kinds, width), jnp.bfloat16),
            pltpu.VMEM(((1 + len(early)) * slots * page, heads * width), jnp.bfloat16),
            pltpu.VMEM(((1 + len(early)) * slots * page, heads * width), jnp.bfloat16),
            pltpu.SemaphoreType.DMA((6,)),
        ],
        compiler_params=pltpu.CompilerParams(vmem_limit_bytes=24 << 20),
        cost_estimate=pl.CostEstimate(
            flops=4 * rows * (slots * page + suffix) * width,
            bytes_accessed=6 << 20,
            transcendentals=rows * 256,
        ),
        name="local_part",
    )(
        *[
            pltpu.with_memory_space_constraint(value, pltpu.HBM)
            for value in (
                page_table,
                suffix_len,
                q,
                raw,
                suffix_kv.reshape(suffix_rows, width),
                new_kv.reshape(requests * kinds, width),
            )
        ],
        *early,
    )
    sizes = (heads, group, page, scale, 256, replicas)
    out = pl.pallas_call(
        functools.partial(finish_body, sizes, choices),
        out_shape=jax.ShapeDtypeStruct((rows, width), jnp.bfloat16),
        in_specs=[vmem()] * (5 + len(late)),
        out_specs=hbm(),
        scratch_shapes=[
            pltpu.VMEM((rows, width), jnp.bfloat16),
            pltpu.VMEM((tokens, heads * width), jnp.bfloat16),
            pltpu.VMEM((tokens, heads * width), jnp.bfloat16),
            pltpu.SemaphoreType.DMA((rows // 256,)),
        ],
        compiler_params=pltpu.CompilerParams(vmem_limit_bytes=24 << 20),
        cost_estimate=pl.CostEstimate(
            flops=4 * rows * tokens * width, bytes_accessed=3 << 20, transcendentals=rows * tokens
        ),
        name="finish_part",
    )(counts.reshape(1, 1), q_wide, acc, stat, bias, *late)
    return out.reshape(requests, head_count, width)


def solution(mesh):
    placed = (
        P(("groups", "replica"), "tensor", None),
        P(("groups", "replica"), None, None, "tensor", None),
        P("groups"),
        P(("groups", "replica"), None, None, "tensor", None),
        P(("groups", "replica"), None, "tensor", None),
        P(("groups", "replica")),
        P(("groups", "replica")),
    )
    return jax.shard_map(
        functools.partial(shards, mesh.shape["replica"]),
        mesh=mesh,
        in_specs=placed,
        out_specs=P(("groups", "replica"), "tensor", None),
        check_vma=False,
    )
```

```python
import functools
import math

import jax
import jax.numpy as jnp
from jax import lax
from jax.experimental import pallas as pl
from jax.experimental.pallas import tpu as pltpu
from jax.sharding import PartitionSpec as P

masked_score = -1e30
lanes = 128


def one_hot(shape, condition):
    row = lax.broadcasted_iota(jnp.int32, shape, 0)
    column = lax.broadcasted_iota(jnp.int32, shape, 1)
    return jnp.where(condition(row, column), 1.0, 0.0).astype(jnp.bfloat16)


def head_concat(grouped, heads, group):
    row = lax.broadcasted_iota(jnp.int32, grouped.shape, 0)
    head = lax.rem(row, heads * group) // group
    values = grouped.astype(jnp.float32)
    parts = [jnp.where(head == g, values, 0.0).astype(jnp.bfloat16) for g in range(heads)]
    return jnp.concatenate(parts, axis=1)


def head_select(wide, heads, group):
    width = wide.shape[1] // heads
    shape = (wide.shape[0], width)
    head = lax.rem(lax.broadcasted_iota(jnp.int32, shape, 0), heads * group) // group
    result = wide[:, :width]
    for g in range(1, heads):
        result = jnp.where(head == g, wide[:, g * width : (g + 1) * width], result)
    return result


def split_page(raw, order, heads):
    sorted_rows = jnp.dot(order, raw, preferred_element_type=jnp.float32).astype(jnp.bfloat16)
    tokens = raw.shape[0] // (2 * heads)
    kinds = [sorted_rows[i * tokens : (i + 1) * tokens] for i in range(2 * heads)]
    return jnp.concatenate(kinds[:heads], axis=1), jnp.concatenate(kinds[heads:], axis=1)


def page_order(page_rows, kinds):
    tokens = page_rows // kinds
    return one_hot(
        (page_rows, page_rows),
        lambda row, column: column == lax.rem(row, tokens) * kinds + row // tokens,
    )


def slot_bias(table_ref, slot):
    size = table_ref.shape[0]

    def look(index, found):
        return jnp.maximum(found, (table_ref[index] == slot).astype(jnp.int32))

    found = lax.fori_loop(0, size, look, jnp.int32(0), unroll=size <= 16)
    return jnp.where(found > 0, 0.0, masked_score)


def live_bias(table_ref, slots, page, rows):
    column = lax.broadcasted_iota(jnp.int32, (rows, len(slots) * page), 1)
    bias = jnp.zeros(column.shape, jnp.float32)
    for place, slot in enumerate(slots):
        bias = jnp.where(column // page == place, slot_bias(table_ref, slot), bias)
    return bias


def fill_tables(raws, order, keys_ref, values_ref, heads, page):
    place = 0
    page_rows = page * 2 * heads
    for raw_ref in raws:
        for at in range(0, raw_ref.shape[0], page_rows):
            keys, values = split_page(raw_ref[at : at + page_rows], order, heads)
            keys_ref[place : place + page] = keys
            values_ref[place : place + page] = values
            place += page


def contract_last(a, b):
    return lax.dot_general(a, b, (((1,), (1,)), ((), ())), preferred_element_type=jnp.float32)


def local_body(sizes, owners, *refs):
    heads, group, page, suffix, scale, batch, replicas, wave = sizes
    table_hbm, lens_hbm, q_hbm, own_hbm, suffix_hbm, new_hbm = refs[:6]
    acc_ref, max_ref, part_ref, wide_ref, bias_ref = refs[6:11]
    table_ref, lens_ref, q_ref, own_ref, suffix_ref, new_ref = refs[11:17]
    keys_ref, values_ref, sems = refs[17:]
    kinds = 2 * heads
    row_heads = heads * group
    cached = suffix * kinds
    fresh = batch * kinds
    width = cached + fresh
    batches = q_ref.shape[0] // (batch * row_heads)
    waves = batches // wave
    wave_rows = wave * batch * cached
    pairs = [
        (own_hbm, own_ref),
        (q_hbm, q_ref),
        (new_hbm, new_ref),
        (table_hbm, table_ref),
        (lens_hbm, lens_ref),
    ] + [
        (suffix_hbm.at[pl.ds(i * wave_rows, wave_rows)], suffix_ref.at[pl.ds(i * wave_rows, wave_rows)])
        for i in range(waves)
    ]
    copies = [
        pltpu.make_async_copy(source, target, sems.at[i])
        for i, (source, target) in enumerate(pairs)
    ]
    for copy in copies:
        copy.start()
    me = lax.axis_index("replica")
    slots = own_ref.shape[0] // (page * kinds)
    order = page_order(page * kinds, kinds)
    column = lax.broadcasted_iota(jnp.int32, (row_heads, width), 1)
    head = lax.broadcasted_iota(jnp.int32, (row_heads, width), 0) // group
    never = jnp.int32(1 << 20)
    token = jnp.where(
        (column < cached) & (lax.rem(column, kinds) == head), column // kinds, never
    )
    places = [
        jnp.where(column == cached + i * kinds + head, -1, token) for i in range(batch)
    ]
    for copy in copies[:5]:
        copy.wait()
    fill_tables([own_ref], order, keys_ref, values_ref, heads, page)
    live = live_bias(table_ref, [me * slots + s for s in range(slots)], page, 1)
    bias_ref[...] = live_bias(
        table_ref,
        [owner(me, replicas) * slots + s for owner in owners for s in range(slots)],
        page,
        8,
    )
    keys = keys_ref[...]
    values = values_ref[...]
    block_rows = wave * batch * row_heads
    for turn in range(waves):
        copies[5 + turn].wait()
        rows = pl.ds(turn * block_rows, block_rows)
        q = q_ref[rows]
        q_wide = head_concat(q, heads, group)
        wide_ref[rows] = q_wide
        prefix = contract_last(q_wide, keys) * scale + live
        pieces = []
        scores = []
        for i in range(wave * batch):
            request = turn * wave * batch + i
            kv = jnp.concatenate(
                [
                    suffix_ref[request * cached : (request + 1) * cached],
                    new_ref[request // batch * fresh : (request // batch + 1) * fresh],
                ],
                axis=0,
            )
            pieces.append(kv)
            score = contract_last(q[i * row_heads : (i + 1) * row_heads], kv) * scale
            scores.append(
                jnp.where(places[i % batch] < lens_ref[request], score, masked_score)
            )
        score = jnp.concatenate(scores, axis=0)
        row_max = jnp.max(jnp.maximum(prefix, score), axis=1, keepdims=True)
        weights = jnp.exp2(score - row_max)
        prefix_weights = jnp.exp2(prefix - row_max)
        part_ref[rows] = weights + prefix_weights
        max_ref[rows] = jnp.broadcast_to(row_max, weights.shape)
        rounded = pltpu.roll(weights, heads, 1).astype(jnp.bfloat16)
        wide = jnp.dot(
            prefix_weights.astype(jnp.bfloat16), values, preferred_element_type=jnp.float32
        )
        attended = [
            jnp.dot(
                rounded[i * row_heads : (i + 1) * row_heads],
                pieces[i],
                preferred_element_type=jnp.float32,
            )
            for i in range(wave * batch)
        ]
        acc_ref[rows] = jnp.concatenate(attended, axis=0) + head_select(wide, heads, group)


def absorb(sizes, rows, wide_ref, acc_ref, max_ref, part_ref, keys, values, live):
    heads, group, scale = sizes
    score = contract_last(wide_ref[rows], keys) * scale + live
    chunks = [score[:, i : i + lanes] for i in range(0, score.shape[1], lanes)]
    top = functools.reduce(jnp.maximum, chunks)
    earlier = max_ref[rows]
    row_max = jnp.maximum(earlier, jnp.max(top, axis=1, keepdims=True))
    weights = [jnp.exp2(chunk - row_max) for chunk in chunks]
    factor = jnp.exp2(earlier - row_max)
    part = part_ref[rows] * factor + functools.reduce(jnp.add, weights)
    rounded = jnp.concatenate([w.astype(jnp.bfloat16) for w in weights], axis=1)
    wide = jnp.dot(rounded, values, preferred_element_type=jnp.float32)
    return acc_ref[rows] * factor + head_select(wide, heads, group), row_max, part


def fold_body(sizes, place, *refs):
    heads, group, page, scale, block_rows, replicas = sizes
    wide_ref, acc_in, max_in, part_in, bias_ref = refs[:5]
    raws = refs[5:-5]
    acc_ref, max_ref, part_ref, keys_ref, values_ref = refs[-5:]
    kinds = 2 * heads
    fill_tables(raws, page_order(page * kinds, kinds), keys_ref, values_ref, heads, page)
    keys = keys_ref[...]
    values = values_ref[...]
    live = bias_ref[:1, place : place + keys.shape[0]]
    for start in range(0, wide_ref.shape[0], block_rows):
        rows = pl.ds(start, block_rows)
        acc_ref[rows], max_ref[rows], part_ref[rows] = absorb(
            (heads, group, scale), rows, wide_ref, acc_in, max_in, part_in, keys, values, live
        )


def finish_body(sizes, place, *refs):
    heads, group, page, scale, block_rows, replicas = sizes
    count_ref, wide_ref, acc_in, max_in, part_in, bias_ref = refs[:6]
    raws = refs[6:-5]
    out_hbm, out_ref, keys_ref, values_ref, sems = refs[-5:]
    kinds = 2 * heads
    fill_tables(raws, page_order(page * kinds, kinds), keys_ref, values_ref, heads, page)
    keys = keys_ref[...]
    values = values_ref[...]
    live = bias_ref[:1, place : place + keys.shape[0]]
    live_rows = count_ref[...] * (heads * group)
    copies = []
    for block, start in enumerate(range(0, wide_ref.shape[0], block_rows)):
        rows = pl.ds(start, block_rows)
        acc, row_max, part = absorb(
            (heads, group, scale), rows, wide_ref, acc_in, max_in, part_in, keys, values, live
        )
        total = jnp.sum(part, axis=1, keepdims=True)
        row = start + lax.broadcasted_iota(jnp.int32, total.shape, 0)
        share = jnp.where(row < live_rows, 1.0 / total, 0.0)
        out_ref[rows] = (acc * share).astype(jnp.bfloat16)
        copies.append(pltpu.make_async_copy(out_ref.at[rows], out_hbm.at[rows], sems.at[block]))
        copies[-1].start()
    for copy in copies:
        copy.wait()


def vmem():
    return pl.BlockSpec(memory_space=pltpu.VMEM)


def hbm():
    return pl.BlockSpec(memory_space=pltpu.HBM)


def xor_exchange(values, step):
    return lax.ppermute(values, "replica", [(i, i ^ step) for i in range(4)])


def doubling_start(raw):
    owners = [lambda me, n, step=step: jnp.bitwise_xor(me, step) for step in (1, 2, 3)]
    return [xor_exchange(raw, 2), xor_exchange(raw, 1)], owners


def doubling_finish(blocks, anchor):
    across, near = blocks
    across, anchor = lax.optimization_barrier((across, anchor))
    return [[near, across], [xor_exchange(across, 1)]], anchor


def gathered_stages(raw, replicas):
    everything = lax.all_gather(raw, "replica", axis=0, tiled=True)
    owners = [lambda me, n, at=at: jnp.where(me == at, -1, at) for at in range(replicas)]
    together = math.gcd(replicas, 4) * raw.shape[0]
    return [
        [everything[i : i + together]] for i in range(0, everything.shape[0], together)
    ], owners


def shards(replicas, queries, prefix_pool, page_table, suffix_kv, new_kv, suffix_len, counts):
    requests, head_count, width = queries.shape
    slots, page, unused, heads, width = prefix_pool.shape
    suffix = suffix_kv.shape[1]
    group = head_count // heads
    kinds = 2 * heads
    scale = width**-0.5 * math.log2(math.e)
    raw = prefix_pool.reshape(slots * page * kinds, width)
    batch = (-suffix * kinds) % lanes // kinds
    wave = 4
    block_rows = 256
    rows = requests * head_count
    block_tokens = slots * page
    doubling = replicas == 4
    if doubling:
        blocks, owners = doubling_start(raw)
    else:
        stages, owners = gathered_stages(raw, replicas)
    suffix_rows = requests * suffix * kinds
    full = jax.ShapeDtypeStruct((rows, lanes), jnp.float32)
    params = pltpu.CompilerParams(vmem_limit_bytes=24 << 20)

    def cost(tokens):
        return pl.CostEstimate(
            flops=4 * rows * tokens * width, bytes_accessed=3 << 20, transcendentals=rows * tokens
        )

    def tables(tokens):
        return [pltpu.VMEM((tokens, heads * width), jnp.bfloat16)] * 2

    acc, row_max, part, q_wide, bias = pl.pallas_call(
        functools.partial(
            local_body, (heads, group, page, suffix, scale, batch, replicas, wave), owners
        ),
        out_shape=[
            full,
            full,
            full,
            jax.ShapeDtypeStruct((rows, heads * width), jnp.bfloat16),
            jax.ShapeDtypeStruct((8, len(owners) * block_tokens), jnp.float32),
        ],
        in_specs=[hbm()] * 6,
        out_specs=[vmem()] * 5,
        scratch_shapes=[
            pltpu.SMEM(page_table.shape, jnp.int32),
            pltpu.SMEM(suffix_len.shape, jnp.int32),
            pltpu.VMEM((rows, width), jnp.bfloat16),
            pltpu.VMEM(raw.shape, jnp.bfloat16),
            pltpu.VMEM((suffix_rows, width), jnp.bfloat16),
            pltpu.VMEM((requests * kinds, width), jnp.bfloat16),
            *tables(block_tokens),
            pltpu.SemaphoreType.DMA((5 + requests // batch // wave,)),
        ],
        compiler_params=params,
        cost_estimate=cost(2 * block_tokens),
        name="local_part",
    )(
        *[
            pltpu.with_memory_space_constraint(value, pltpu.HBM)
            for value in (
                page_table,
                suffix_len,
                queries.reshape(rows, width),
                raw,
                suffix_kv.reshape(suffix_rows, width),
                new_kv.reshape(requests * kinds, width),
            )
        ]
    )
    if doubling:
        stages, acc = doubling_finish(blocks, acc)
    sizes = (heads, group, page, scale, block_rows, replicas)
    place = 0
    for blocks in stages[:-1]:
        tokens = sum(block.shape[0] for block in blocks) // kinds
        acc, row_max, part = pl.pallas_call(
            functools.partial(fold_body, sizes, place),
            out_shape=[full] * 3,
            in_specs=[vmem()] * (5 + len(blocks)),
            out_specs=[vmem()] * 3,
            scratch_shapes=tables(tokens),
            compiler_params=params,
            cost_estimate=cost(tokens),
            name="fold_part",
        )(q_wide, acc, row_max, part, bias, *blocks)
        place += tokens
    tokens = sum(block.shape[0] for block in stages[-1]) // kinds
    out = pl.pallas_call(
        functools.partial(finish_body, sizes, place),
        out_shape=jax.ShapeDtypeStruct((rows, width), jnp.bfloat16),
        in_specs=[vmem()] * (6 + len(stages[-1])),
        out_specs=hbm(),
        scratch_shapes=[
            pltpu.VMEM((rows, width), jnp.bfloat16),
            *tables(tokens),
            pltpu.SemaphoreType.DMA((rows // block_rows,)),
        ],
        compiler_params=params,
        cost_estimate=cost(tokens),
        name="finish_part",
    )(counts.reshape(1, 1), q_wide, acc, row_max, part, bias, *stages[-1])
    return out.reshape(requests, head_count, width)


def solution(mesh):
    placed = (
        P(("groups", "replica"), "tensor", None),
        P(("groups", "replica"), None, None, "tensor", None),
        P("groups"),
        P(("groups", "replica"), None, None, "tensor", None),
        P(("groups", "replica"), None, "tensor", None),
        P(("groups", "replica")),
        P(("groups", "replica")),
    )
    return jax.shard_map(
        functools.partial(shards, mesh.shape["replica"]),
        mesh=mesh,
        in_specs=placed,
        out_specs=P(("groups", "replica"), "tensor", None),
        check_vma=False,
    )
```

```python
import functools
import math

import jax
import jax.numpy as jnp
from jax import lax
from jax.experimental import pallas as pl
from jax.experimental.pallas import tpu as pltpu
from jax.sharding import PartitionSpec as P

masked_score = -1e30
lanes = 128


def one_hot(shape, condition):
    row = lax.broadcasted_iota(jnp.int32, shape, 0)
    column = lax.broadcasted_iota(jnp.int32, shape, 1)
    return jnp.where(condition(row, column), 1.0, 0.0).astype(jnp.bfloat16)


def head_concat(grouped, heads, group):
    row = lax.broadcasted_iota(jnp.int32, grouped.shape, 0)
    head = lax.rem(row, heads * group) // group
    values = grouped.astype(jnp.float32)
    parts = [jnp.where(head == g, values, 0.0).astype(jnp.bfloat16) for g in range(heads)]
    return jnp.concatenate(parts, axis=1)


def head_select(wide, heads, group):
    width = wide.shape[1] // heads
    shape = (wide.shape[0], width)
    head = lax.rem(lax.broadcasted_iota(jnp.int32, shape, 0), heads * group) // group
    result = wide[:, :width]
    for g in range(1, heads):
        result = jnp.where(head == g, wide[:, g * width : (g + 1) * width], result)
    return result


def split_page(raw, order, heads):
    sorted_rows = jnp.dot(order, raw, preferred_element_type=jnp.float32).astype(jnp.bfloat16)
    tokens = raw.shape[0] // (2 * heads)
    kinds = [sorted_rows[i * tokens : (i + 1) * tokens] for i in range(2 * heads)]
    return jnp.concatenate(kinds[:heads], axis=1), jnp.concatenate(kinds[heads:], axis=1)


def page_order(page_rows, kinds):
    tokens = page_rows // kinds
    return one_hot(
        (page_rows, page_rows),
        lambda row, column: column == lax.rem(row, tokens) * kinds + row // tokens,
    )


def slot_bias(table_ref, slot):
    size = table_ref.shape[0]

    def look(index, found):
        return jnp.maximum(found, (table_ref[index] == slot).astype(jnp.int32))

    found = lax.fori_loop(0, size, look, jnp.int32(0), unroll=size <= 16)
    return jnp.where(found > 0, 0.0, masked_score)


def live_bias(table_ref, slots, page, rows):
    column = lax.broadcasted_iota(jnp.int32, (rows, len(slots) * page), 1)
    bias = jnp.zeros(column.shape, jnp.float32)
    for place, slot in enumerate(slots):
        bias = jnp.where(column // page == place, slot_bias(table_ref, slot), bias)
    return bias


def fill_tables(raws, order, keys_ref, values_ref, heads, page):
    place = 0
    page_rows = page * 2 * heads
    for raw_ref in raws:
        for at in range(0, raw_ref.shape[0], page_rows):
            keys, values = split_page(raw_ref[at : at + page_rows], order, heads)
            keys_ref[place : place + page] = keys
            values_ref[place : place + page] = values
            place += page


def contract_last(a, b):
    return lax.dot_general(a, b, (((1,), (1,)), ((), ())), preferred_element_type=jnp.float32)


def local_body(sizes, owners, *refs):
    heads, group, page, suffix, scale, batch, replicas, wave = sizes
    table_hbm, lens_hbm, q_hbm, own_hbm, suffix_hbm, new_hbm = refs[:6]
    acc_ref, max_ref, part_ref, wide_ref, bias_ref = refs[6:11]
    table_ref, lens_ref, q_ref, own_ref, suffix_ref, new_ref = refs[11:17]
    keys_ref, values_ref, sems = refs[17:]
    kinds = 2 * heads
    row_heads = heads * group
    cached = suffix * kinds
    fresh = batch * kinds
    width = cached + fresh
    batches = q_ref.shape[0] // (batch * row_heads)
    waves = batches // wave
    wave_rows = wave * batch * cached
    pairs = [
        (own_hbm, own_ref),
        (q_hbm, q_ref),
        (new_hbm, new_ref),
        (table_hbm, table_ref),
        (lens_hbm, lens_ref),
    ] + [
        (suffix_hbm.at[pl.ds(i * wave_rows, wave_rows)], suffix_ref.at[pl.ds(i * wave_rows, wave_rows)])
        for i in range(waves)
    ]
    copies = [
        pltpu.make_async_copy(source, target, sems.at[i])
        for i, (source, target) in enumerate(pairs)
    ]
    for copy in copies:
        copy.start()
    me = lax.axis_index("replica")
    slots = own_ref.shape[0] // (page * kinds)
    order = page_order(page * kinds, kinds)
    column = lax.broadcasted_iota(jnp.int32, (row_heads, width), 1)
    head = lax.broadcasted_iota(jnp.int32, (row_heads, width), 0) // group
    never = jnp.int32(1 << 20)
    token = jnp.where(
        (column < cached) & (lax.rem(column, kinds) == head), column // kinds, never
    )
    places = [
        jnp.where(column == cached + i * kinds + head, -1, token) for i in range(batch)
    ]
    for copy in copies[:5]:
        copy.wait()
    fill_tables([own_ref], order, keys_ref, values_ref, heads, page)
    live = live_bias(table_ref, [me * slots + s for s in range(slots)], page, 1)
    bias_ref[...] = live_bias(
        table_ref,
        [owner(me, replicas) * slots + s for owner in owners for s in range(slots)],
        page,
        8,
    )
    keys = keys_ref[...]
    values = values_ref[...]
    block_rows = wave * batch * row_heads
    for turn in range(waves):
        copies[5 + turn].wait()
        rows = pl.ds(turn * block_rows, block_rows)
        q = q_ref[rows]
        q_wide = head_concat(q, heads, group)
        wide_ref[rows] = q_wide
        prefix = contract_last(q_wide, keys) * scale + live
        pieces = []
        scores = []
        for i in range(wave * batch):
            request = turn * wave * batch + i
            kv = jnp.concatenate(
                [
                    suffix_ref[request * cached : (request + 1) * cached],
                    new_ref[request // batch * fresh : (request // batch + 1) * fresh],
                ],
                axis=0,
            )
            pieces.append(kv)
            score = contract_last(q[i * row_heads : (i + 1) * row_heads], kv) * scale
            scores.append(
                jnp.where(places[i % batch] < lens_ref[request], score, masked_score)
            )
        score = jnp.concatenate(scores, axis=0)
        row_max = jnp.max(jnp.maximum(prefix, score), axis=1, keepdims=True)
        weights = jnp.exp2(score - row_max)
        prefix_weights = jnp.exp2(prefix - row_max)
        part_ref[rows] = weights + prefix_weights
        max_ref[rows] = jnp.broadcast_to(row_max, weights.shape)
        rounded = pltpu.roll(weights, heads, 1).astype(jnp.bfloat16)
        wide = jnp.dot(
            prefix_weights.astype(jnp.bfloat16), values, preferred_element_type=jnp.float32
        )
        attended = [
            jnp.dot(
                rounded[i * row_heads : (i + 1) * row_heads],
                pieces[i],
                preferred_element_type=jnp.float32,
            )
            for i in range(wave * batch)
        ]
        acc_ref[rows] = jnp.concatenate(attended, axis=0) + head_select(wide, heads, group)


def absorb(sizes, rows, wide_ref, acc_ref, max_ref, part_ref, keys, values, live):
    heads, group, scale = sizes
    score = contract_last(wide_ref[rows], keys) * scale + live
    chunks = [score[:, i : i + lanes] for i in range(0, score.shape[1], lanes)]
    top = functools.reduce(jnp.maximum, chunks)
    earlier = max_ref[rows]
    row_max = jnp.maximum(earlier, jnp.max(top, axis=1, keepdims=True))
    weights = [jnp.exp2(chunk - row_max) for chunk in chunks]
    factor = jnp.exp2(earlier - row_max)
    part = part_ref[rows] * factor + functools.reduce(jnp.add, weights)
    rounded = jnp.concatenate([w.astype(jnp.bfloat16) for w in weights], axis=1)
    wide = jnp.dot(rounded, values, preferred_element_type=jnp.float32)
    return acc_ref[rows] * factor + head_select(wide, heads, group), row_max, part


def fold_body(sizes, place, *refs):
    heads, group, page, scale, block_rows, replicas = sizes
    count_in, wide_ref, acc_in, max_in, part_in, bias_ref = refs[:6]
    raws = refs[6:-6]
    count_ref, acc_ref, max_ref, part_ref, keys_ref, values_ref = refs[-6:]
    count_ref[...] = jnp.broadcast_to(count_in[:1, :1], count_ref.shape)
    kinds = 2 * heads
    fill_tables(raws, page_order(page * kinds, kinds), keys_ref, values_ref, heads, page)
    keys = keys_ref[...]
    values = values_ref[...]
    live = bias_ref[:1, place : place + keys.shape[0]]
    for start in range(0, wide_ref.shape[0], block_rows):
        rows = pl.ds(start, block_rows)
        acc_ref[rows], max_ref[rows], part_ref[rows] = absorb(
            (heads, group, scale), rows, wide_ref, acc_in, max_in, part_in, keys, values, live
        )


def finish_body(sizes, place, *refs):
    heads, group, page, scale, block_rows, replicas = sizes
    count_ref, wide_ref, acc_in, max_in, part_in, bias_ref = refs[:6]
    raws = refs[6:-5]
    out_hbm, out_ref, keys_ref, values_ref, sems = refs[-5:]
    kinds = 2 * heads
    fill_tables(raws, page_order(page * kinds, kinds), keys_ref, values_ref, heads, page)
    keys = keys_ref[...]
    values = values_ref[...]
    live = bias_ref[:1, place : place + keys.shape[0]]
    live_rows = count_ref[:1, :1] * (heads * group)
    copies = []
    for block, start in enumerate(range(0, wide_ref.shape[0], block_rows)):
        rows = pl.ds(start, block_rows)
        acc, row_max, part = absorb(
            (heads, group, scale), rows, wide_ref, acc_in, max_in, part_in, keys, values, live
        )
        total = jnp.sum(part, axis=1, keepdims=True)
        row = start + lax.broadcasted_iota(jnp.int32, total.shape, 0)
        share = jnp.where(row < live_rows, 1.0 / total, 0.0)
        out_ref[rows] = (acc * share).astype(jnp.bfloat16)
        copies.append(pltpu.make_async_copy(out_ref.at[rows], out_hbm.at[rows], sems.at[block]))
        copies[-1].start()
    for copy in copies:
        copy.wait()


def vmem():
    return pl.BlockSpec(memory_space=pltpu.VMEM)


def hbm():
    return pl.BlockSpec(memory_space=pltpu.HBM)


def xor_exchange(values, step):
    return lax.ppermute(values, "replica", [(i, i ^ step) for i in range(4)])


def doubling_start(raw):
    owners = [lambda me, n, step=step: jnp.bitwise_xor(me, step) for step in (1, 3, 2)]
    return [xor_exchange(raw, 3), xor_exchange(raw, 1)], owners


def doubling_finish(blocks, anchor):
    across, near = blocks
    across, near, anchor = lax.optimization_barrier((across, near, anchor))
    return [[near, across], [xor_exchange(across, 1)]], anchor


def gathered_stages(raw, replicas):
    everything = lax.all_gather(raw, "replica", axis=0, tiled=True)
    owners = [lambda me, n, at=at: jnp.where(me == at, -1, at) for at in range(replicas)]
    together = math.gcd(replicas, 4) * raw.shape[0]
    return [
        [everything[i : i + together]] for i in range(0, everything.shape[0], together)
    ], owners


def shards(replicas, queries, prefix_pool, page_table, suffix_kv, new_kv, suffix_len, counts):
    requests, head_count, width = queries.shape
    slots, page, unused, heads, width = prefix_pool.shape
    suffix = suffix_kv.shape[1]
    group = head_count // heads
    kinds = 2 * heads
    scale = width**-0.5 * math.log2(math.e)
    raw = prefix_pool.reshape(slots * page * kinds, width)
    batch = (-suffix * kinds) % lanes // kinds
    wave = 4
    block_rows = 256
    rows = requests * head_count
    block_tokens = slots * page
    doubling = replicas == 4
    if doubling:
        blocks, owners = doubling_start(raw)
    else:
        stages, owners = gathered_stages(raw, replicas)
    suffix_rows = requests * suffix * kinds
    full = jax.ShapeDtypeStruct((rows, lanes), jnp.float32)
    params = pltpu.CompilerParams(vmem_limit_bytes=24 << 20)

    def cost(tokens):
        return pl.CostEstimate(
            flops=4 * rows * tokens * width, bytes_accessed=3 << 20, transcendentals=rows * tokens
        )

    def tables(tokens):
        return [pltpu.VMEM((tokens, heads * width), jnp.bfloat16)] * 2

    acc, row_max, part, q_wide, bias = pl.pallas_call(
        functools.partial(
            local_body, (heads, group, page, suffix, scale, batch, replicas, wave), owners
        ),
        out_shape=[
            full,
            full,
            full,
            jax.ShapeDtypeStruct((rows, heads * width), jnp.bfloat16),
            jax.ShapeDtypeStruct((8, len(owners) * block_tokens), jnp.float32),
        ],
        in_specs=[hbm()] * 6,
        out_specs=[vmem()] * 5,
        scratch_shapes=[
            pltpu.SMEM(page_table.shape, jnp.int32),
            pltpu.SMEM(suffix_len.shape, jnp.int32),
            pltpu.VMEM((rows, width), jnp.bfloat16),
            pltpu.VMEM(raw.shape, jnp.bfloat16),
            pltpu.VMEM((suffix_rows, width), jnp.bfloat16),
            pltpu.VMEM((requests * kinds, width), jnp.bfloat16),
            *tables(block_tokens),
            pltpu.SemaphoreType.DMA((5 + requests // batch // wave,)),
        ],
        compiler_params=params,
        cost_estimate=cost(2 * block_tokens),
        name="local_part",
    )(
        *[
            pltpu.with_memory_space_constraint(value, pltpu.HBM)
            for value in (
                page_table,
                suffix_len,
                queries.reshape(rows, width),
                raw,
                suffix_kv.reshape(suffix_rows, width),
                new_kv.reshape(requests * kinds, width),
            )
        ]
    )
    if doubling:
        stages, acc = doubling_finish(blocks, acc)
    sizes = (heads, group, page, scale, block_rows, replicas)
    place = 0
    count = counts.reshape(1, 1)
    for blocks in stages[:-1]:
        tokens = sum(block.shape[0] for block in blocks) // kinds
        count, acc, row_max, part = pl.pallas_call(
            functools.partial(fold_body, sizes, place),
            out_shape=[jax.ShapeDtypeStruct((8, lanes), jnp.int32)] + [full] * 3,
            in_specs=[vmem()] * (6 + len(blocks)),
            out_specs=[vmem()] * 4,
            scratch_shapes=tables(tokens),
            compiler_params=params,
            cost_estimate=cost(tokens),
            name="fold_part",
        )(count, q_wide, acc, row_max, part, bias, *blocks)
        place += tokens
    tokens = sum(block.shape[0] for block in stages[-1]) // kinds
    out = pl.pallas_call(
        functools.partial(finish_body, sizes, place),
        out_shape=jax.ShapeDtypeStruct((rows, width), jnp.bfloat16),
        in_specs=[vmem()] * (6 + len(stages[-1])),
        out_specs=hbm(),
        scratch_shapes=[
            pltpu.VMEM((rows, width), jnp.bfloat16),
            *tables(tokens),
            pltpu.SemaphoreType.DMA((rows // block_rows,)),
        ],
        compiler_params=params,
        cost_estimate=cost(tokens),
        name="finish_part",
    )(count, q_wide, acc, row_max, part, bias, *stages[-1])
    return out.reshape(requests, head_count, width)


def solution(mesh):
    placed = (
        P(("groups", "replica"), "tensor", None),
        P(("groups", "replica"), None, None, "tensor", None),
        P("groups"),
        P(("groups", "replica"), None, None, "tensor", None),
        P(("groups", "replica"), None, "tensor", None),
        P(("groups", "replica")),
        P(("groups", "replica")),
    )
    return jax.shard_map(
        functools.partial(shards, mesh.shape["replica"]),
        mesh=mesh,
        in_specs=placed,
        out_specs=P(("groups", "replica"), "tensor", None),
        check_vma=False,
    )
```

```python
import functools
import math

import jax
import jax.numpy as jnp
from jax import lax
from jax.experimental import pallas as pl
from jax.experimental.pallas import tpu as pltpu
from jax.sharding import PartitionSpec as P

masked_score = -1e30
lanes = 128


def one_hot(shape, condition):
    row = lax.broadcasted_iota(jnp.int32, shape, 0)
    column = lax.broadcasted_iota(jnp.int32, shape, 1)
    return jnp.where(condition(row, column), 1.0, 0.0).astype(jnp.bfloat16)


def head_concat(grouped, heads, group):
    row = lax.broadcasted_iota(jnp.int32, grouped.shape, 0)
    head = lax.rem(row, heads * group) // group
    values = grouped.astype(jnp.float32)
    parts = [jnp.where(head == g, values, 0.0).astype(jnp.bfloat16) for g in range(heads)]
    return jnp.concatenate(parts, axis=1)


def head_select(wide, heads, group):
    width = wide.shape[1] // heads
    shape = (wide.shape[0], width)
    head = lax.rem(lax.broadcasted_iota(jnp.int32, shape, 0), heads * group) // group
    result = wide[:, :width]
    for g in range(1, heads):
        result = jnp.where(head == g, wide[:, g * width : (g + 1) * width], result)
    return result


def split_page(raw, order, heads):
    sorted_rows = jnp.dot(order, raw, preferred_element_type=jnp.float32).astype(jnp.bfloat16)
    tokens = raw.shape[0] // (2 * heads)
    kinds = [sorted_rows[i * tokens : (i + 1) * tokens] for i in range(2 * heads)]
    return jnp.concatenate(kinds[:heads], axis=1), jnp.concatenate(kinds[heads:], axis=1)


def page_order(page_rows, kinds):
    tokens = page_rows // kinds
    return one_hot(
        (page_rows, page_rows),
        lambda row, column: column == lax.rem(row, tokens) * kinds + row // tokens,
    )


def slot_bias(table_ref, slot):
    size = table_ref.shape[0]

    def look(index, found):
        return jnp.maximum(found, (table_ref[index] == slot).astype(jnp.int32))

    found = lax.fori_loop(0, size, look, jnp.int32(0), unroll=size <= 16)
    return jnp.where(found > 0, 0.0, masked_score)


def live_bias(table_ref, slots, page, rows):
    column = lax.broadcasted_iota(jnp.int32, (rows, len(slots) * page), 1)
    bias = jnp.zeros(column.shape, jnp.float32)
    for place, slot in enumerate(slots):
        bias = jnp.where(column // page == place, slot_bias(table_ref, slot), bias)
    return bias


def fill_tables(raws, order, keys_ref, values_ref, heads, page):
    place = 0
    page_rows = page * 2 * heads
    for raw_ref in raws:
        for at in range(0, raw_ref.shape[0], page_rows):
            keys, values = split_page(raw_ref[at : at + page_rows], order, heads)
            keys_ref[place : place + page] = keys
            values_ref[place : place + page] = values
            place += page


def contract_last(a, b):
    return lax.dot_general(a, b, (((1,), (1,)), ((), ())), preferred_element_type=jnp.float32)


def local_body(sizes, owners, *refs):
    heads, group, page, suffix, scale, batch, replicas, wave = sizes
    table_hbm, lens_hbm, q_hbm, own_hbm, suffix_hbm, new_hbm = refs[:6]
    acc_ref, max_ref, part_ref, wide_ref, bias_ref = refs[6:11]
    table_ref, lens_ref, q_ref, own_ref, suffix_ref, new_ref = refs[11:17]
    keys_ref, values_ref, sems = refs[17:]
    kinds = 2 * heads
    row_heads = heads * group
    cached = suffix * kinds
    fresh = batch * kinds
    width = cached + fresh
    batches = q_ref.shape[0] // (batch * row_heads)
    waves = batches // wave
    wave_rows = wave * batch * cached
    pairs = [
        (own_hbm, own_ref),
        (q_hbm, q_ref),
        (new_hbm, new_ref),
        (table_hbm, table_ref),
        (lens_hbm, lens_ref),
    ] + [
        (suffix_hbm.at[pl.ds(i * wave_rows, wave_rows)], suffix_ref.at[pl.ds(i * wave_rows, wave_rows)])
        for i in range(waves)
    ]
    copies = [
        pltpu.make_async_copy(source, target, sems.at[i])
        for i, (source, target) in enumerate(pairs)
    ]
    for copy in copies:
        copy.start()
    me = lax.axis_index("replica")
    slots = own_ref.shape[0] // (page * kinds)
    order = page_order(page * kinds, kinds)
    column = lax.broadcasted_iota(jnp.int32, (row_heads, width), 1)
    head = lax.broadcasted_iota(jnp.int32, (row_heads, width), 0) // group
    never = jnp.int32(1 << 20)
    token = jnp.where(
        (column < cached) & (lax.rem(column, kinds) == head), column // kinds, never
    )
    places = [
        jnp.where(column == cached + i * kinds + head, -1, token) for i in range(batch)
    ]
    for copy in copies[:5]:
        copy.wait()
    fill_tables([own_ref], order, keys_ref, values_ref, heads, page)
    live = live_bias(table_ref, [me * slots + s for s in range(slots)], page, 1)
    bias_ref[...] = live_bias(
        table_ref,
        [owner(me, replicas) * slots + s for owner in owners for s in range(slots)],
        page,
        8,
    )
    keys = keys_ref[...]
    values = values_ref[...]
    block_rows = wave * batch * row_heads
    for turn in range(waves):
        copies[5 + turn].wait()
        rows = pl.ds(turn * block_rows, block_rows)
        q = q_ref[rows]
        q_wide = head_concat(q, heads, group)
        wide_ref[rows] = q_wide
        prefix = contract_last(q_wide, keys) * scale + live
        pieces = []
        scores = []
        for i in range(wave * batch):
            request = turn * wave * batch + i
            kv = jnp.concatenate(
                [
                    suffix_ref[request * cached : (request + 1) * cached],
                    new_ref[request // batch * fresh : (request // batch + 1) * fresh],
                ],
                axis=0,
            )
            pieces.append(kv)
            score = contract_last(q[i * row_heads : (i + 1) * row_heads], kv) * scale
            scores.append(
                jnp.where(places[i % batch] < lens_ref[request], score, masked_score)
            )
        score = jnp.concatenate(scores, axis=0)
        row_max = jnp.max(jnp.maximum(prefix, score), axis=1, keepdims=True)
        weights = jnp.exp2(score - row_max)
        prefix_weights = jnp.exp2(prefix - row_max)
        part_ref[rows] = weights + prefix_weights
        max_ref[rows] = jnp.broadcast_to(row_max, weights.shape)
        rounded = pltpu.roll(weights, heads, 1).astype(jnp.bfloat16)
        wide = jnp.dot(
            prefix_weights.astype(jnp.bfloat16), values, preferred_element_type=jnp.float32
        )
        attended = [
            jnp.dot(
                rounded[i * row_heads : (i + 1) * row_heads],
                pieces[i],
                preferred_element_type=jnp.float32,
            )
            for i in range(wave * batch)
        ]
        acc_ref[rows] = jnp.concatenate(attended, axis=0) + head_select(wide, heads, group)


def absorb(sizes, rows, wide_ref, acc_ref, max_ref, part_ref, keys, values, live):
    heads, group, scale = sizes
    score = contract_last(wide_ref[rows], keys) * scale + live
    chunks = [score[:, i : i + lanes] for i in range(0, score.shape[1], lanes)]
    top = functools.reduce(jnp.maximum, chunks)
    earlier = max_ref[rows]
    row_max = jnp.maximum(earlier, jnp.max(top, axis=1, keepdims=True))
    weights = [jnp.exp2(chunk - row_max) for chunk in chunks]
    factor = jnp.exp2(earlier - row_max)
    part = part_ref[rows] * factor + functools.reduce(jnp.add, weights)
    rounded = jnp.concatenate([w.astype(jnp.bfloat16) for w in weights], axis=1)
    wide = jnp.dot(rounded, values, preferred_element_type=jnp.float32)
    return acc_ref[rows] * factor + head_select(wide, heads, group), row_max, part


def fold_body(sizes, place, *refs):
    heads, group, page, scale, block_rows, replicas = sizes
    count_in, wide_ref, acc_in, max_in, part_in, bias_ref = refs[:6]
    raws = refs[6:-6]
    count_ref, acc_ref, max_ref, part_ref, keys_ref, values_ref = refs[-6:]
    count_ref[...] = jnp.broadcast_to(count_in[:1, :1], count_ref.shape)
    kinds = 2 * heads
    fill_tables(raws, page_order(page * kinds, kinds), keys_ref, values_ref, heads, page)
    keys = keys_ref[...]
    values = values_ref[...]
    live = bias_ref[:1, place : place + keys.shape[0]]
    for start in range(0, wide_ref.shape[0], block_rows):
        rows = pl.ds(start, block_rows)
        acc_ref[rows], max_ref[rows], part_ref[rows] = absorb(
            (heads, group, scale), rows, wide_ref, acc_in, max_in, part_in, keys, values, live
        )


def finish_body(sizes, place, *refs):
    heads, group, page, scale, block_rows, replicas = sizes
    count_ref, wide_ref, acc_in, max_in, part_in, bias_ref = refs[:6]
    raws = refs[6:-5]
    out_hbm, out_ref, keys_ref, values_ref, sem = refs[-5:]
    kinds = 2 * heads
    fill_tables(raws, page_order(page * kinds, kinds), keys_ref, values_ref, heads, page)
    keys = keys_ref[...]
    values = values_ref[...]
    live = bias_ref[:1, place : place + keys.shape[0]]
    live_rows = count_ref[:1, :1] * (heads * group)
    for start in range(0, wide_ref.shape[0], block_rows):
        rows = pl.ds(start, block_rows)
        acc, row_max, part = absorb(
            (heads, group, scale), rows, wide_ref, acc_in, max_in, part_in, keys, values, live
        )
        total = jnp.sum(part, axis=1, keepdims=True)
        row = start + lax.broadcasted_iota(jnp.int32, total.shape, 0)
        share = jnp.where(row < live_rows, 1.0 / total, 0.0)
        out_ref[rows] = (acc * share).astype(jnp.bfloat16)
    copy = pltpu.make_async_copy(out_ref, out_hbm, sem)
    copy.start()
    copy.wait()


def vmem():
    return pl.BlockSpec(memory_space=pltpu.VMEM)


def hbm():
    return pl.BlockSpec(memory_space=pltpu.HBM)


def xor_exchange(values, step):
    return lax.ppermute(values, "replica", [(i, i ^ step) for i in range(4)])


def doubling_finish(raw, across, anchor):
    raw, anchor = lax.optimization_barrier((raw, anchor))
    near = xor_exchange(raw, 1)
    across, anchor = lax.optimization_barrier((across, anchor))
    return [[across, near], [xor_exchange(across, 1)]], anchor


def gathered_stages(raw, replicas):
    everything = lax.all_gather(raw, "replica", axis=0, tiled=True)
    owners = [lambda me, n, at=at: jnp.where(me == at, -1, at) for at in range(replicas)]
    together = math.gcd(replicas, 4) * raw.shape[0]
    return [
        [everything[i : i + together]] for i in range(0, everything.shape[0], together)
    ], owners


def shards(replicas, queries, prefix_pool, page_table, suffix_kv, new_kv, suffix_len, counts):
    requests, head_count, width = queries.shape
    slots, page, unused, heads, width = prefix_pool.shape
    suffix = suffix_kv.shape[1]
    group = head_count // heads
    kinds = 2 * heads
    scale = width**-0.5 * math.log2(math.e)
    raw = prefix_pool.reshape(slots * page * kinds, width)
    batch = (-suffix * kinds) % lanes // kinds
    wave = requests // batch
    block_rows = 256
    rows = requests * head_count
    block_tokens = slots * page
    doubling = replicas == 4
    if doubling:
        across = xor_exchange(raw, 3)
        owners = [lambda me, n, step=step: jnp.bitwise_xor(me, step) for step in (3, 1, 2)]
    else:
        stages, owners = gathered_stages(raw, replicas)
    suffix_rows = requests * suffix * kinds
    full = jax.ShapeDtypeStruct((rows, lanes), jnp.float32)
    params = pltpu.CompilerParams(vmem_limit_bytes=24 << 20)

    def cost(tokens):
        return pl.CostEstimate(
            flops=4 * rows * tokens * width, bytes_accessed=3 << 20, transcendentals=rows * tokens
        )

    def tables(tokens):
        return [pltpu.VMEM((tokens, heads * width), jnp.bfloat16)] * 2

    acc, row_max, part, q_wide, bias = pl.pallas_call(
        functools.partial(
            local_body, (heads, group, page, suffix, scale, batch, replicas, wave), owners
        ),
        out_shape=[
            full,
            full,
            full,
            jax.ShapeDtypeStruct((rows, heads * width), jnp.bfloat16),
            jax.ShapeDtypeStruct((8, len(owners) * block_tokens), jnp.float32),
        ],
        in_specs=[hbm()] * 6,
        out_specs=[vmem()] * 5,
        scratch_shapes=[
            pltpu.SMEM(page_table.shape, jnp.int32),
            pltpu.SMEM(suffix_len.shape, jnp.int32),
            pltpu.VMEM((rows, width), jnp.bfloat16),
            pltpu.VMEM(raw.shape, jnp.bfloat16),
            pltpu.VMEM((suffix_rows, width), jnp.bfloat16),
            pltpu.VMEM((requests * kinds, width), jnp.bfloat16),
            *tables(block_tokens),
            pltpu.SemaphoreType.DMA((5 + requests // batch // wave,)),
        ],
        compiler_params=params,
        cost_estimate=cost(2 * block_tokens),
        name="local_part",
    )(
        *[
            pltpu.with_memory_space_constraint(value, pltpu.HBM)
            for value in (
                page_table,
                suffix_len,
                queries.reshape(rows, width),
                raw,
                suffix_kv.reshape(suffix_rows, width),
                new_kv.reshape(requests * kinds, width),
            )
        ]
    )
    if doubling:
        stages, acc = doubling_finish(raw, across, acc)
    sizes = (heads, group, page, scale, block_rows, replicas)
    place = 0
    count = counts.reshape(1, 1)
    for blocks in stages[:-1]:
        tokens = sum(block.shape[0] for block in blocks) // kinds
        count, acc, row_max, part = pl.pallas_call(
            functools.partial(fold_body, sizes, place),
            out_shape=[jax.ShapeDtypeStruct((8, lanes), jnp.int32)] + [full] * 3,
            in_specs=[vmem()] * (6 + len(blocks)),
            out_specs=[vmem()] * 4,
            scratch_shapes=tables(tokens),
            compiler_params=params,
            cost_estimate=cost(tokens),
            name="fold_part",
        )(count, q_wide, acc, row_max, part, bias, *blocks)
        place += tokens
    tokens = sum(block.shape[0] for block in stages[-1]) // kinds
    out = pl.pallas_call(
        functools.partial(finish_body, sizes, place),
        out_shape=jax.ShapeDtypeStruct((rows, width), jnp.bfloat16),
        in_specs=[vmem()] * (6 + len(stages[-1])),
        out_specs=hbm(),
        scratch_shapes=[
            pltpu.VMEM((rows, width), jnp.bfloat16),
            *tables(tokens),
            pltpu.SemaphoreType.DMA,
        ],
        compiler_params=params,
        cost_estimate=cost(tokens),
        name="finish_part",
    )(count, q_wide, acc, row_max, part, bias, *stages[-1])
    return out.reshape(requests, head_count, width)


def solution(mesh):
    placed = (
        P(("groups", "replica"), "tensor", None),
        P(("groups", "replica"), None, None, "tensor", None),
        P("groups"),
        P(("groups", "replica"), None, None, "tensor", None),
        P(("groups", "replica"), None, "tensor", None),
        P(("groups", "replica")),
        P(("groups", "replica")),
    )
    return jax.shard_map(
        functools.partial(shards, mesh.shape["replica"]),
        mesh=mesh,
        in_specs=placed,
        out_specs=P(("groups", "replica"), "tensor", None),
        check_vma=False,
    )
```

```python
import functools
import math

import jax
import jax.numpy as jnp
from jax import lax
from jax.experimental import pallas as pl
from jax.experimental.pallas import tpu as pltpu
from jax.sharding import PartitionSpec as P

masked_score = -1e30
lanes = 128


def one_hot(shape, condition):
    row = lax.broadcasted_iota(jnp.int32, shape, 0)
    column = lax.broadcasted_iota(jnp.int32, shape, 1)
    return jnp.where(condition(row, column), 1.0, 0.0).astype(jnp.bfloat16)


def head_concat(grouped, heads, group):
    row = lax.broadcasted_iota(jnp.int32, grouped.shape, 0)
    head = lax.rem(row, heads * group) // group
    values = grouped.astype(jnp.float32)
    parts = [jnp.where(head == g, values, 0.0).astype(jnp.bfloat16) for g in range(heads)]
    return jnp.concatenate(parts, axis=1)


def head_select(wide, heads, group):
    width = wide.shape[1] // heads
    shape = (wide.shape[0], width)
    head = lax.rem(lax.broadcasted_iota(jnp.int32, shape, 0), heads * group) // group
    result = wide[:, :width]
    for g in range(1, heads):
        result = jnp.where(head == g, wide[:, g * width : (g + 1) * width], result)
    return result


def split_page(raw, order, heads):
    sorted_rows = jnp.dot(order, raw, preferred_element_type=jnp.float32).astype(jnp.bfloat16)
    tokens = raw.shape[0] // (2 * heads)
    kinds = [sorted_rows[i * tokens : (i + 1) * tokens] for i in range(2 * heads)]
    return jnp.concatenate(kinds[:heads], axis=1), jnp.concatenate(kinds[heads:], axis=1)


def page_order(page_rows, kinds):
    tokens = page_rows // kinds
    return one_hot(
        (page_rows, page_rows),
        lambda row, column: column == lax.rem(row, tokens) * kinds + row // tokens,
    )


def slot_bias(table_ref, slot):
    size = table_ref.shape[0]

    def look(index, found):
        return jnp.maximum(found, (table_ref[index] == slot).astype(jnp.int32))

    found = lax.fori_loop(0, size, look, jnp.int32(0), unroll=size <= 16)
    return jnp.where(found > 0, 0.0, masked_score)


def live_bias(table_ref, slots, page, rows):
    column = lax.broadcasted_iota(jnp.int32, (rows, len(slots) * page), 1)
    bias = jnp.zeros(column.shape, jnp.float32)
    for place, slot in enumerate(slots):
        bias = jnp.where(column // page == place, slot_bias(table_ref, slot), bias)
    return bias


def fill_tables(raws, order, keys_ref, values_ref, heads, page):
    place = 0
    page_rows = page * 2 * heads
    for raw_ref in raws:
        for at in range(0, raw_ref.shape[0], page_rows):
            keys, values = split_page(raw_ref[at : at + page_rows], order, heads)
            keys_ref[place : place + page] = keys
            values_ref[place : place + page] = values
            place += page


def contract_last(a, b):
    return lax.dot_general(a, b, (((1,), (1,)), ((), ())), preferred_element_type=jnp.float32)


def local_body(sizes, owners, *refs):
    heads, group, page, suffix, scale, batch, replicas, wave = sizes
    table_hbm, lens_hbm, q_hbm, own_hbm, suffix_hbm, new_hbm = refs[:6]
    acc_ref, max_ref, part_ref, wide_ref, bias_ref = refs[6:11]
    table_ref, lens_ref, q_ref, own_ref, suffix_ref, new_ref = refs[11:17]
    keys_ref, values_ref, sems = refs[17:]
    kinds = 2 * heads
    row_heads = heads * group
    cached = suffix * kinds
    fresh = batch * kinds
    width = cached + fresh
    batches = q_ref.shape[0] // (batch * row_heads)
    waves = batches // wave
    wave_rows = wave * batch * cached
    pairs = [
        (own_hbm, own_ref),
        (q_hbm, q_ref),
        (new_hbm, new_ref),
        (table_hbm, table_ref),
        (lens_hbm, lens_ref),
    ] + [
        (suffix_hbm.at[pl.ds(i * wave_rows, wave_rows)], suffix_ref.at[pl.ds(i * wave_rows, wave_rows)])
        for i in range(waves)
    ]
    copies = [
        pltpu.make_async_copy(source, target, sems.at[i])
        for i, (source, target) in enumerate(pairs)
    ]
    for copy in copies:
        copy.start()
    me = lax.axis_index("replica")
    slots = own_ref.shape[0] // (page * kinds)
    order = page_order(page * kinds, kinds)
    column = lax.broadcasted_iota(jnp.int32, (row_heads, width), 1)
    head = lax.broadcasted_iota(jnp.int32, (row_heads, width), 0) // group
    never = jnp.int32(1 << 20)
    token = jnp.where(
        (column < cached) & (lax.rem(column, kinds) == head), column // kinds, never
    )
    places = [
        jnp.where(column == cached + i * kinds + head, -1, token) for i in range(batch)
    ]
    for copy in copies[:5]:
        copy.wait()
    fill_tables([own_ref], order, keys_ref, values_ref, heads, page)
    live = live_bias(table_ref, [me * slots + s for s in range(slots)], page, 1)
    bias_ref[...] = live_bias(
        table_ref,
        [owner(me, replicas) * slots + s for owner in owners for s in range(slots)],
        page,
        8,
    )
    keys = keys_ref[...]
    values = values_ref[...]
    block_rows = wave * batch * row_heads
    for turn in range(waves):
        copies[5 + turn].wait()
        rows = pl.ds(turn * block_rows, block_rows)
        q = q_ref[rows]
        q_wide = head_concat(q, heads, group)
        wide_ref[rows] = q_wide
        prefix = contract_last(q_wide, keys) * scale + live
        pieces = []
        scores = []
        for i in range(wave * batch):
            request = turn * wave * batch + i
            kv = jnp.concatenate(
                [
                    suffix_ref[request * cached : (request + 1) * cached],
                    new_ref[request // batch * fresh : (request // batch + 1) * fresh],
                ],
                axis=0,
            )
            pieces.append(kv)
            score = contract_last(q[i * row_heads : (i + 1) * row_heads], kv) * scale
            scores.append(
                jnp.where(places[i % batch] < lens_ref[request], score, masked_score)
            )
        score = jnp.concatenate(scores, axis=0)
        row_max = jnp.max(jnp.maximum(prefix, score), axis=1, keepdims=True)
        weights = jnp.exp2(score - row_max)
        prefix_weights = jnp.exp2(prefix - row_max)
        part_ref[rows] = weights + prefix_weights
        max_ref[rows] = jnp.broadcast_to(row_max, weights.shape)
        rounded = pltpu.roll(weights, heads, 1).astype(jnp.bfloat16)
        wide = jnp.dot(
            prefix_weights.astype(jnp.bfloat16), values, preferred_element_type=jnp.float32
        )
        attended = [
            jnp.dot(
                rounded[i * row_heads : (i + 1) * row_heads],
                pieces[i],
                preferred_element_type=jnp.float32,
            )
            for i in range(wave * batch)
        ]
        acc_ref[rows] = jnp.concatenate(attended, axis=0) + head_select(wide, heads, group)


def absorb(sizes, rows, wide_ref, acc_ref, max_ref, part_ref, keys, values, live):
    heads, group, scale = sizes
    score = contract_last(wide_ref[rows], keys) * scale + live
    chunks = [score[:, i : i + lanes] for i in range(0, score.shape[1], lanes)]
    top = functools.reduce(jnp.maximum, chunks)
    earlier = max_ref[rows]
    row_max = jnp.maximum(earlier, jnp.max(top, axis=1, keepdims=True))
    weights = [jnp.exp2(chunk - row_max) for chunk in chunks]
    factor = jnp.exp2(earlier - row_max)
    part = part_ref[rows] * factor + functools.reduce(jnp.add, weights)
    rounded = jnp.concatenate([w.astype(jnp.bfloat16) for w in weights], axis=1)
    wide = jnp.dot(rounded, values, preferred_element_type=jnp.float32)
    return acc_ref[rows] * factor + head_select(wide, heads, group), row_max, part


def fold_body(sizes, place, *refs):
    heads, group, page, scale, block_rows, replicas = sizes
    count_in, wide_ref, acc_in, max_in, part_in, bias_ref = refs[:6]
    raws = refs[6:-6]
    count_ref, acc_ref, max_ref, part_ref, keys_ref, values_ref = refs[-6:]
    count_ref[...] = jnp.broadcast_to(count_in[:1, :1], count_ref.shape)
    kinds = 2 * heads
    fill_tables(raws, page_order(page * kinds, kinds), keys_ref, values_ref, heads, page)
    keys = keys_ref[...]
    values = values_ref[...]
    live = bias_ref[:1, place : place + keys.shape[0]]
    for start in range(0, wide_ref.shape[0], block_rows):
        rows = pl.ds(start, block_rows)
        acc_ref[rows], max_ref[rows], part_ref[rows] = absorb(
            (heads, group, scale), rows, wide_ref, acc_in, max_in, part_in, keys, values, live
        )


def finish_body(sizes, place, *refs):
    heads, group, page, scale, block_rows, replicas = sizes
    count_ref, wide_ref, acc_in, max_in, part_in, bias_ref = refs[:6]
    raws = refs[6:-5]
    out_hbm, out_ref, keys_ref, values_ref, sem = refs[-5:]
    kinds = 2 * heads
    fill_tables(raws, page_order(page * kinds, kinds), keys_ref, values_ref, heads, page)
    keys = keys_ref[...]
    values = values_ref[...]
    live = bias_ref[:1, place : place + keys.shape[0]]
    live_rows = count_ref[:1, :] * (heads * group)
    for start in range(0, wide_ref.shape[0], block_rows):
        rows = pl.ds(start, block_rows)
        acc, row_max, part = absorb(
            (heads, group, scale), rows, wide_ref, acc_in, max_in, part_in, keys, values, live
        )
        total = jnp.broadcast_to(jnp.sum(part, axis=1, keepdims=True), part.shape)
        row = start + lax.broadcasted_iota(jnp.int32, part.shape, 0)
        share = jnp.where(row < live_rows, 1.0 / total, 0.0)
        out_ref[rows] = (acc * share).astype(jnp.bfloat16)
    copy = pltpu.make_async_copy(out_ref, out_hbm, sem)
    copy.start()
    copy.wait()


def vmem():
    return pl.BlockSpec(memory_space=pltpu.VMEM)


def hbm():
    return pl.BlockSpec(memory_space=pltpu.HBM)


def xor_exchange(values, step):
    return lax.ppermute(values, "replica", [(i, i ^ step) for i in range(4)])


def doubling_start(raw):
    owners = [lambda me, n, step=step: jnp.bitwise_xor(me, step) for step in (3, 1, 2)]
    return xor_exchange(raw, 3), xor_exchange(raw, 1), owners


def doubling_finish(across, near, anchor):
    across, anchor = lax.optimization_barrier((across, anchor))
    return [[across, near], [xor_exchange(across, 1)]], anchor


def gathered_stages(raw, replicas):
    everything = lax.all_gather(raw, "replica", axis=0, tiled=True)
    owners = [lambda me, n, at=at: jnp.where(me == at, -1, at) for at in range(replicas)]
    together = math.gcd(replicas, 4) * raw.shape[0]
    return [
        [everything[i : i + together]] for i in range(0, everything.shape[0], together)
    ], owners


def shards(replicas, queries, prefix_pool, page_table, suffix_kv, new_kv, suffix_len, counts):
    requests, head_count, width = queries.shape
    slots, page, unused, heads, width = prefix_pool.shape
    suffix = suffix_kv.shape[1]
    group = head_count // heads
    kinds = 2 * heads
    scale = width**-0.5 * math.log2(math.e)
    raw = prefix_pool.reshape(slots * page * kinds, width)
    batch = (-suffix * kinds) % lanes // kinds
    wave = requests // batch
    block_rows = 256
    rows = requests * head_count
    block_tokens = slots * page
    doubling = replicas == 4
    if doubling:
        across, near, owners = doubling_start(raw)
    else:
        stages, owners = gathered_stages(raw, replicas)
    suffix_rows = requests * suffix * kinds
    full = jax.ShapeDtypeStruct((rows, lanes), jnp.float32)
    params = pltpu.CompilerParams(vmem_limit_bytes=24 << 20)

    def cost(tokens):
        return pl.CostEstimate(
            flops=4 * rows * tokens * width, bytes_accessed=3 << 20, transcendentals=rows * tokens
        )

    def tables(tokens):
        return [pltpu.VMEM((tokens, heads * width), jnp.bfloat16)] * 2

    acc, row_max, part, q_wide, bias = pl.pallas_call(
        functools.partial(
            local_body, (heads, group, page, suffix, scale, batch, replicas, wave), owners
        ),
        out_shape=[
            full,
            full,
            full,
            jax.ShapeDtypeStruct((rows, heads * width), jnp.bfloat16),
            jax.ShapeDtypeStruct((8, len(owners) * block_tokens), jnp.float32),
        ],
        in_specs=[hbm()] * 6,
        out_specs=[vmem()] * 5,
        scratch_shapes=[
            pltpu.SMEM(page_table.shape, jnp.int32),
            pltpu.SMEM(suffix_len.shape, jnp.int32),
            pltpu.VMEM((rows, width), jnp.bfloat16),
            pltpu.VMEM(raw.shape, jnp.bfloat16),
            pltpu.VMEM((suffix_rows, width), jnp.bfloat16),
            pltpu.VMEM((requests * kinds, width), jnp.bfloat16),
            *tables(block_tokens),
            pltpu.SemaphoreType.DMA((5 + requests // batch // wave,)),
        ],
        compiler_params=params,
        cost_estimate=cost(2 * block_tokens),
        name="local_part",
    )(
        *[
            pltpu.with_memory_space_constraint(value, pltpu.HBM)
            for value in (
                page_table,
                suffix_len,
                queries.reshape(rows, width),
                raw,
                suffix_kv.reshape(suffix_rows, width),
                new_kv.reshape(requests * kinds, width),
            )
        ]
    )
    if doubling:
        stages, acc = doubling_finish(across, near, acc)
    sizes = (heads, group, page, scale, block_rows, replicas)
    place = 0
    count = jnp.broadcast_to(counts, (8, lanes)) if len(stages) == 1 else counts.reshape(1, 1)
    for blocks in stages[:-1]:
        tokens = sum(block.shape[0] for block in blocks) // kinds
        count, acc, row_max, part = pl.pallas_call(
            functools.partial(fold_body, sizes, place),
            out_shape=[jax.ShapeDtypeStruct((8, lanes), jnp.int32)] + [full] * 3,
            in_specs=[vmem()] * (6 + len(blocks)),
            out_specs=[vmem()] * 4,
            scratch_shapes=tables(tokens),
            compiler_params=params,
            cost_estimate=cost(tokens),
            name="fold_part",
        )(count, q_wide, acc, row_max, part, bias, *blocks)
        place += tokens
    tokens = sum(block.shape[0] for block in stages[-1]) // kinds
    out = pl.pallas_call(
        functools.partial(finish_body, sizes, place),
        out_shape=jax.ShapeDtypeStruct((rows, width), jnp.bfloat16),
        in_specs=[vmem()] * (6 + len(stages[-1])),
        out_specs=hbm(),
        scratch_shapes=[
            pltpu.VMEM((rows, width), jnp.bfloat16),
            *tables(tokens),
            pltpu.SemaphoreType.DMA,
        ],
        compiler_params=params,
        cost_estimate=cost(tokens),
        name="finish_part",
    )(count, q_wide, acc, row_max, part, bias, *stages[-1])
    return out.reshape(requests, head_count, width)


def solution(mesh):
    placed = (
        P(("groups", "replica"), "tensor", None),
        P(("groups", "replica"), None, None, "tensor", None),
        P("groups"),
        P(("groups", "replica"), None, None, "tensor", None),
        P(("groups", "replica"), None, "tensor", None),
        P(("groups", "replica")),
        P(("groups", "replica")),
    )
    return jax.shard_map(
        functools.partial(shards, mesh.shape["replica"]),
        mesh=mesh,
        in_specs=placed,
        out_specs=P(("groups", "replica"), "tensor", None),
        check_vma=False,
    )
```

```python
import functools
import math

import jax
import jax.numpy as jnp
from jax import lax
from jax.experimental import pallas as pl
from jax.experimental.pallas import tpu as pltpu
from jax.sharding import PartitionSpec as P

masked_score = -1e30
lanes = 128


def one_hot(shape, condition):
    row = lax.broadcasted_iota(jnp.int32, shape, 0)
    column = lax.broadcasted_iota(jnp.int32, shape, 1)
    return jnp.where(condition(row, column), 1.0, 0.0).astype(jnp.bfloat16)


def head_concat(grouped, heads, group):
    row = lax.broadcasted_iota(jnp.int32, grouped.shape, 0)
    head = lax.rem(row, heads * group) // group
    values = grouped.astype(jnp.float32)
    parts = [jnp.where(head == g, values, 0.0).astype(jnp.bfloat16) for g in range(heads)]
    return jnp.concatenate(parts, axis=1)


def head_select(wide, heads, group):
    width = wide.shape[1] // heads
    shape = (wide.shape[0], width)
    head = lax.rem(lax.broadcasted_iota(jnp.int32, shape, 0), heads * group) // group
    result = wide[:, :width]
    for g in range(1, heads):
        result = jnp.where(head == g, wide[:, g * width : (g + 1) * width], result)
    return result


def split_page(raw, order, heads):
    sorted_rows = jnp.dot(order, raw, preferred_element_type=jnp.float32).astype(jnp.bfloat16)
    tokens = raw.shape[0] // (2 * heads)
    kinds = [sorted_rows[i * tokens : (i + 1) * tokens] for i in range(2 * heads)]
    return jnp.concatenate(kinds[:heads], axis=1), jnp.concatenate(kinds[heads:], axis=1)


def page_order(page_rows, kinds):
    tokens = page_rows // kinds
    return one_hot(
        (page_rows, page_rows),
        lambda row, column: column == lax.rem(row, tokens) * kinds + row // tokens,
    )


def slot_bias(table_ref, slot):
    size = table_ref.shape[0]

    def look(index, found):
        return jnp.maximum(found, (table_ref[index] == slot).astype(jnp.int32))

    found = lax.fori_loop(0, size, look, jnp.int32(0), unroll=size <= 16)
    return jnp.where(found > 0, 0.0, masked_score)


def live_bias(table_ref, slots, page, rows):
    column = lax.broadcasted_iota(jnp.int32, (rows, len(slots) * page), 1)
    bias = jnp.zeros(column.shape, jnp.float32)
    for place, slot in enumerate(slots):
        bias = jnp.where(column // page == place, slot_bias(table_ref, slot), bias)
    return bias


def fill_tables(raws, order, keys_ref, values_ref, heads, page):
    place = 0
    page_rows = page * 2 * heads
    for raw_ref in raws:
        for at in range(0, raw_ref.shape[0], page_rows):
            keys, values = split_page(raw_ref[at : at + page_rows], order, heads)
            keys_ref[place : place + page] = keys
            values_ref[place : place + page] = values
            place += page


def contract_last(a, b):
    return lax.dot_general(a, b, (((1,), (1,)), ((), ())), preferred_element_type=jnp.float32)


def local_body(sizes, owners, *refs):
    heads, group, page, suffix, scale, batch, replicas, wave = sizes
    table_hbm, lens_hbm, q_hbm, own_hbm, suffix_hbm, new_hbm = refs[:6]
    acc_ref, max_ref, part_ref, wide_ref, bias_ref = refs[6:11]
    table_ref, lens_ref, q_ref, own_ref, suffix_ref, new_ref = refs[11:17]
    keys_ref, values_ref, sems = refs[17:]
    kinds = 2 * heads
    row_heads = heads * group
    cached = suffix * kinds
    fresh = batch * kinds
    width = cached + fresh
    batches = q_ref.shape[0] // (batch * row_heads)
    waves = batches // wave
    wave_rows = wave * batch * cached
    pairs = [
        (own_hbm, own_ref),
        (q_hbm, q_ref),
        (new_hbm, new_ref),
        (table_hbm, table_ref),
        (lens_hbm, lens_ref),
    ] + [
        (suffix_hbm.at[pl.ds(i * wave_rows, wave_rows)], suffix_ref.at[pl.ds(i * wave_rows, wave_rows)])
        for i in range(waves)
    ]
    copies = [
        pltpu.make_async_copy(source, target, sems.at[i])
        for i, (source, target) in enumerate(pairs)
    ]
    for copy in copies:
        copy.start()
    me = lax.axis_index("replica")
    slots = own_ref.shape[0] // (page * kinds)
    order = page_order(page * kinds, kinds)
    column = lax.broadcasted_iota(jnp.int32, (row_heads, width), 1)
    head = lax.broadcasted_iota(jnp.int32, (row_heads, width), 0) // group
    never = jnp.int32(1 << 20)
    token = jnp.where(
        (column < cached) & (lax.rem(column, kinds) == head), column // kinds, never
    )
    places = [
        jnp.where(column == cached + i * kinds + head, -1, token) for i in range(batch)
    ]
    for copy in copies[:5]:
        copy.wait()
    fill_tables([own_ref], order, keys_ref, values_ref, heads, page)
    live = live_bias(table_ref, [me * slots + s for s in range(slots)], page, 1)
    bias_ref[...] = live_bias(
        table_ref,
        [owner(me, replicas) * slots + s for owner in owners for s in range(slots)],
        page,
        8,
    )
    keys = keys_ref[...]
    values = values_ref[...]
    block_rows = wave * batch * row_heads
    for turn in range(waves):
        copies[5 + turn].wait()
        rows = pl.ds(turn * block_rows, block_rows)
        q = q_ref[rows]
        q_wide = head_concat(q, heads, group)
        wide_ref[rows] = q_wide
        prefix = contract_last(q_wide, keys) * scale + live
        pieces = []
        scores = []
        for i in range(wave * batch):
            request = turn * wave * batch + i
            kv = jnp.concatenate(
                [
                    suffix_ref[request * cached : (request + 1) * cached],
                    new_ref[request // batch * fresh : (request // batch + 1) * fresh],
                ],
                axis=0,
            )
            pieces.append(kv)
            score = contract_last(q[i * row_heads : (i + 1) * row_heads], kv) * scale
            scores.append(
                jnp.where(places[i % batch] < lens_ref[request], score, masked_score)
            )
        score = jnp.concatenate(scores, axis=0)
        row_max = jnp.max(jnp.maximum(prefix, score), axis=1, keepdims=True)
        weights = jnp.exp2(score - row_max)
        prefix_weights = jnp.exp2(prefix - row_max)
        part_ref[rows] = weights + prefix_weights
        max_ref[rows] = jnp.broadcast_to(row_max, weights.shape)
        rounded = pltpu.roll(weights, heads, 1).astype(jnp.bfloat16)
        wide = jnp.dot(
            prefix_weights.astype(jnp.bfloat16), values, preferred_element_type=jnp.float32
        )
        attended = [
            jnp.dot(
                rounded[i * row_heads : (i + 1) * row_heads],
                pieces[i],
                preferred_element_type=jnp.float32,
            )
            for i in range(wave * batch)
        ]
        acc_ref[rows] = jnp.concatenate(attended, axis=0) + head_select(wide, heads, group)


def absorb(sizes, rows, wide_ref, acc_ref, max_ref, part_ref, keys, values, live):
    heads, group, scale = sizes
    score = contract_last(wide_ref[rows], keys) * scale + live
    chunks = [score[:, i : i + lanes] for i in range(0, score.shape[1], lanes)]
    top = functools.reduce(jnp.maximum, chunks)
    earlier = max_ref[rows]
    row_max = jnp.maximum(earlier, jnp.max(top, axis=1, keepdims=True))
    weights = [jnp.exp2(chunk - row_max) for chunk in chunks]
    factor = jnp.exp2(earlier - row_max)
    part = part_ref[rows] * factor + functools.reduce(jnp.add, weights)
    rounded = jnp.concatenate([w.astype(jnp.bfloat16) for w in weights], axis=1)
    wide = jnp.dot(rounded, values, preferred_element_type=jnp.float32)
    return acc_ref[rows] * factor + head_select(wide, heads, group), row_max, part


def fold_body(sizes, place, *refs):
    heads, group, page, scale, block_rows, replicas = sizes
    count_in, wide_ref, acc_in, max_in, part_in, bias_ref = refs[:6]
    raws = refs[6:-6]
    count_ref, acc_ref, max_ref, part_ref, keys_ref, values_ref = refs[-6:]
    count_ref[...] = jnp.broadcast_to(count_in[:1, :1], count_ref.shape)
    kinds = 2 * heads
    fill_tables(raws, page_order(page * kinds, kinds), keys_ref, values_ref, heads, page)
    keys = keys_ref[...]
    values = values_ref[...]
    live = bias_ref[:1, place : place + keys.shape[0]]
    for start in range(0, wide_ref.shape[0], block_rows):
        rows = pl.ds(start, block_rows)
        acc_ref[rows], max_ref[rows], part_ref[rows] = absorb(
            (heads, group, scale), rows, wide_ref, acc_in, max_in, part_in, keys, values, live
        )


def finish_body(sizes, place, *refs):
    heads, group, page, scale, block_rows, replicas = sizes
    count_ref, wide_ref, acc_in, max_in, part_in, bias_ref = refs[:6]
    raws = refs[6:-5]
    out_hbm, out_ref, keys_ref, values_ref, sem = refs[-5:]
    kinds = 2 * heads
    fill_tables(raws, page_order(page * kinds, kinds), keys_ref, values_ref, heads, page)
    keys = keys_ref[...]
    values = values_ref[...]
    live = bias_ref[:1, place : place + keys.shape[0]]
    live_rows = count_ref[:1, :] * (heads * group)
    for start in range(0, wide_ref.shape[0], block_rows):
        rows = pl.ds(start, block_rows)
        acc, row_max, part = absorb(
            (heads, group, scale), rows, wide_ref, acc_in, max_in, part_in, keys, values, live
        )
        total = jnp.broadcast_to(jnp.sum(part, axis=1, keepdims=True), part.shape)
        row = start + lax.broadcasted_iota(jnp.int32, part.shape, 0)
        share = jnp.where(row < live_rows, 1.0 / total, 0.0)
        out_ref[rows] = (acc * share).astype(jnp.bfloat16)
    copy = pltpu.make_async_copy(out_ref, out_hbm, sem)
    copy.start()
    copy.wait()


def vmem():
    return pl.BlockSpec(memory_space=pltpu.VMEM)


def hbm():
    return pl.BlockSpec(memory_space=pltpu.HBM)


def xor_exchange(values, step):
    return lax.ppermute(values, "replica", [(i, i ^ step) for i in range(4)])


def doubling_start(raw):
    owners = [lambda me, n, step=step: jnp.bitwise_xor(me, step) for step in (3, 1, 2)]
    return xor_exchange(raw, 3), xor_exchange(raw, 1), owners


def doubling_finish(across, near, anchor):
    across, anchor = lax.optimization_barrier((across, anchor))
    half = across.shape[0] // 2
    passed = [xor_exchange(across[:half], 1), xor_exchange(across[half:], 1)]
    return [[across, near], passed], anchor


def gathered_stages(raw, replicas):
    everything = lax.all_gather(raw, "replica", axis=0, tiled=True)
    owners = [lambda me, n, at=at: jnp.where(me == at, -1, at) for at in range(replicas)]
    together = math.gcd(replicas, 4) * raw.shape[0]
    return [
        [everything[i : i + together]] for i in range(0, everything.shape[0], together)
    ], owners


def shards(replicas, queries, prefix_pool, page_table, suffix_kv, new_kv, suffix_len, counts):
    requests, head_count, width = queries.shape
    slots, page, unused, heads, width = prefix_pool.shape
    suffix = suffix_kv.shape[1]
    group = head_count // heads
    kinds = 2 * heads
    scale = width**-0.5 * math.log2(math.e)
    raw = prefix_pool.reshape(slots * page * kinds, width)
    batch = (-suffix * kinds) % lanes // kinds
    wave = requests // batch
    block_rows = 256
    rows = requests * head_count
    block_tokens = slots * page
    doubling = replicas == 4
    if doubling:
        across, near, owners = doubling_start(raw)
    else:
        stages, owners = gathered_stages(raw, replicas)
    suffix_rows = requests * suffix * kinds
    full = jax.ShapeDtypeStruct((rows, lanes), jnp.float32)
    params = pltpu.CompilerParams(vmem_limit_bytes=24 << 20)

    def cost(tokens):
        return pl.CostEstimate(
            flops=4 * rows * tokens * width, bytes_accessed=3 << 20, transcendentals=rows * tokens
        )

    def tables(tokens):
        return [pltpu.VMEM((tokens, heads * width), jnp.bfloat16)] * 2

    acc, row_max, part, q_wide, bias = pl.pallas_call(
        functools.partial(
            local_body, (heads, group, page, suffix, scale, batch, replicas, wave), owners
        ),
        out_shape=[
            full,
            full,
            full,
            jax.ShapeDtypeStruct((rows, heads * width), jnp.bfloat16),
            jax.ShapeDtypeStruct((8, len(owners) * block_tokens), jnp.float32),
        ],
        in_specs=[hbm()] * 6,
        out_specs=[vmem()] * 5,
        scratch_shapes=[
            pltpu.SMEM(page_table.shape, jnp.int32),
            pltpu.SMEM(suffix_len.shape, jnp.int32),
            pltpu.VMEM((rows, width), jnp.bfloat16),
            pltpu.VMEM(raw.shape, jnp.bfloat16),
            pltpu.VMEM((suffix_rows, width), jnp.bfloat16),
            pltpu.VMEM((requests * kinds, width), jnp.bfloat16),
            *tables(block_tokens),
            pltpu.SemaphoreType.DMA((5 + requests // batch // wave,)),
        ],
        compiler_params=params,
        cost_estimate=cost(2 * block_tokens),
        name="local_part",
    )(
        *[
            pltpu.with_memory_space_constraint(value, pltpu.HBM)
            for value in (
                page_table,
                suffix_len,
                queries.reshape(rows, width),
                raw,
                suffix_kv.reshape(suffix_rows, width),
                new_kv.reshape(requests * kinds, width),
            )
        ]
    )
    if doubling:
        stages, acc = doubling_finish(across, near, acc)
    sizes = (heads, group, page, scale, block_rows, replicas)
    place = 0
    count = jnp.broadcast_to(counts, (8, lanes)) if len(stages) == 1 else counts.reshape(1, 1)
    for blocks in stages[:-1]:
        tokens = sum(block.shape[0] for block in blocks) // kinds
        count, acc, row_max, part = pl.pallas_call(
            functools.partial(fold_body, sizes, place),
            out_shape=[jax.ShapeDtypeStruct((8, lanes), jnp.int32)] + [full] * 3,
            in_specs=[vmem()] * (6 + len(blocks)),
            out_specs=[vmem()] * 4,
            scratch_shapes=tables(tokens),
            compiler_params=params,
            cost_estimate=cost(tokens),
            name="fold_part",
        )(count, q_wide, acc, row_max, part, bias, *blocks)
        place += tokens
    tokens = sum(block.shape[0] for block in stages[-1]) // kinds
    out = pl.pallas_call(
        functools.partial(finish_body, sizes, place),
        out_shape=jax.ShapeDtypeStruct((rows, width), jnp.bfloat16),
        in_specs=[vmem()] * (6 + len(stages[-1])),
        out_specs=hbm(),
        scratch_shapes=[
            pltpu.VMEM((rows, width), jnp.bfloat16),
            *tables(tokens),
            pltpu.SemaphoreType.DMA,
        ],
        compiler_params=params,
        cost_estimate=cost(tokens),
        name="finish_part",
    )(count, q_wide, acc, row_max, part, bias, *stages[-1])
    return out.reshape(requests, head_count, width)


def solution(mesh):
    placed = (
        P(("groups", "replica"), "tensor", None),
        P(("groups", "replica"), None, None, "tensor", None),
        P("groups"),
        P(("groups", "replica"), None, None, "tensor", None),
        P(("groups", "replica"), None, "tensor", None),
        P(("groups", "replica")),
        P(("groups", "replica")),
    )
    return jax.shard_map(
        functools.partial(shards, mesh.shape["replica"]),
        mesh=mesh,
        in_specs=placed,
        out_specs=P(("groups", "replica"), "tensor", None),
        check_vma=False,
    )
```

```python
import functools
import math

import jax
import jax.numpy as jnp
from jax import lax
from jax.experimental import pallas as pl
from jax.experimental.pallas import tpu as pltpu
from jax.sharding import PartitionSpec as P

masked_score = -1e30
lanes = 128


def one_hot(shape, condition):
    row = lax.broadcasted_iota(jnp.int32, shape, 0)
    column = lax.broadcasted_iota(jnp.int32, shape, 1)
    return jnp.where(condition(row, column), 1.0, 0.0).astype(jnp.bfloat16)


def head_concat(grouped, heads, group):
    row = lax.broadcasted_iota(jnp.int32, grouped.shape, 0)
    head = lax.rem(row, heads * group) // group
    values = grouped.astype(jnp.float32)
    parts = [jnp.where(head == g, values, 0.0).astype(jnp.bfloat16) for g in range(heads)]
    return jnp.concatenate(parts, axis=1)


def head_select(wide, heads, group):
    width = wide.shape[1] // heads
    shape = (wide.shape[0], width)
    head = lax.rem(lax.broadcasted_iota(jnp.int32, shape, 0), heads * group) // group
    result = wide[:, :width]
    for g in range(1, heads):
        result = jnp.where(head == g, wide[:, g * width : (g + 1) * width], result)
    return result


def split_page(raw, order, heads):
    sorted_rows = jnp.dot(order, raw, preferred_element_type=jnp.float32).astype(jnp.bfloat16)
    tokens = raw.shape[0] // (2 * heads)
    kinds = [sorted_rows[i * tokens : (i + 1) * tokens] for i in range(2 * heads)]
    return jnp.concatenate(kinds[:heads], axis=1), jnp.concatenate(kinds[heads:], axis=1)


def page_order(page_rows, kinds):
    tokens = page_rows // kinds
    return one_hot(
        (page_rows, page_rows),
        lambda row, column: column == lax.rem(row, tokens) * kinds + row // tokens,
    )


def slot_bias(table_ref, slot):
    size = table_ref.shape[0]

    def look(index, found):
        return jnp.maximum(found, (table_ref[index] == slot).astype(jnp.int32))

    found = lax.fori_loop(0, size, look, jnp.int32(0), unroll=size <= 16)
    return jnp.where(found > 0, 0.0, masked_score)


def live_bias(table_ref, slots, page, rows):
    column = lax.broadcasted_iota(jnp.int32, (rows, len(slots) * page), 1)
    bias = jnp.zeros(column.shape, jnp.float32)
    for place, slot in enumerate(slots):
        bias = jnp.where(column // page == place, slot_bias(table_ref, slot), bias)
    return bias


def fill_tables(raws, order, keys_ref, values_ref, heads, page):
    place = 0
    page_rows = page * 2 * heads
    for raw_ref in raws:
        for at in range(0, raw_ref.shape[0], page_rows):
            keys, values = split_page(raw_ref[at : at + page_rows], order, heads)
            keys_ref[place : place + page] = keys
            values_ref[place : place + page] = values
            place += page


def contract_last(a, b):
    return lax.dot_general(a, b, (((1,), (1,)), ((), ())), preferred_element_type=jnp.float32)


def local_body(sizes, early_owners, owners, *refs):
    heads, group, page, suffix, scale, batch, replicas, wave = sizes
    table_hbm, lens_hbm, q_hbm, own_hbm, suffix_hbm, new_hbm = refs[:6]
    early = refs[6 : 6 + len(early_owners)]
    refs = refs[6 + len(early_owners) :]
    acc_ref, max_ref, part_ref, wide_ref, bias_ref = refs[:5]
    table_ref, lens_ref, q_ref, own_ref, suffix_ref, new_ref = refs[5:11]
    keys_ref, values_ref, sems = refs[11:]
    kinds = 2 * heads
    row_heads = heads * group
    cached = suffix * kinds
    fresh = batch * kinds
    width = cached + fresh
    batches = q_ref.shape[0] // (batch * row_heads)
    waves = batches // wave
    wave_rows = wave * batch * cached
    pairs = [
        (own_hbm, own_ref),
        (q_hbm, q_ref),
        (new_hbm, new_ref),
        (table_hbm, table_ref),
        (lens_hbm, lens_ref),
    ] + [
        (suffix_hbm.at[pl.ds(i * wave_rows, wave_rows)], suffix_ref.at[pl.ds(i * wave_rows, wave_rows)])
        for i in range(waves)
    ]
    copies = [
        pltpu.make_async_copy(source, target, sems.at[i])
        for i, (source, target) in enumerate(pairs)
    ]
    for copy in copies:
        copy.start()
    me = lax.axis_index("replica")
    slots = own_ref.shape[0] // (page * kinds)
    order = page_order(page * kinds, kinds)
    column = lax.broadcasted_iota(jnp.int32, (row_heads, width), 1)
    head = lax.broadcasted_iota(jnp.int32, (row_heads, width), 0) // group
    never = jnp.int32(1 << 20)
    token = jnp.where(
        (column < cached) & (lax.rem(column, kinds) == head), column // kinds, never
    )
    places = [
        jnp.where(column == cached + i * kinds + head, -1, token) for i in range(batch)
    ]
    for copy in copies[:5]:
        copy.wait()
    fill_tables([own_ref, *early], order, keys_ref, values_ref, heads, page)
    near = [me] + [owner(me, replicas) for owner in early_owners]
    live = live_bias(
        table_ref, [owner * slots + s for owner in near for s in range(slots)], page, 1
    )
    bias_ref[...] = live_bias(
        table_ref,
        [owner(me, replicas) * slots + s for owner in owners for s in range(slots)],
        page,
        8,
    )
    keys = keys_ref[...]
    values = values_ref[...]
    block_rows = wave * batch * row_heads
    for turn in range(waves):
        copies[5 + turn].wait()
        rows = pl.ds(turn * block_rows, block_rows)
        q = q_ref[rows]
        q_wide = head_concat(q, heads, group)
        wide_ref[rows] = q_wide
        prefix = contract_last(q_wide, keys) * scale + live
        pieces = []
        scores = []
        for i in range(wave * batch):
            request = turn * wave * batch + i
            kv = jnp.concatenate(
                [
                    suffix_ref[request * cached : (request + 1) * cached],
                    new_ref[request // batch * fresh : (request // batch + 1) * fresh],
                ],
                axis=0,
            )
            pieces.append(kv)
            score = contract_last(q[i * row_heads : (i + 1) * row_heads], kv) * scale
            scores.append(
                jnp.where(places[i % batch] < lens_ref[request], score, masked_score)
            )
        score = jnp.concatenate(scores, axis=0)
        chunks = [prefix[:, i : i + lanes] for i in range(0, prefix.shape[1], lanes)]
        top = functools.reduce(jnp.maximum, chunks, score)
        row_max = jnp.max(top, axis=1, keepdims=True)
        weights = jnp.exp2(score - row_max)
        prefix_weights = [jnp.exp2(chunk - row_max) for chunk in chunks]
        part_ref[rows] = functools.reduce(jnp.add, prefix_weights, weights)
        max_ref[rows] = jnp.broadcast_to(row_max, weights.shape)
        rounded = pltpu.roll(weights, heads, 1).astype(jnp.bfloat16)
        wide = jnp.dot(
            jnp.concatenate([w.astype(jnp.bfloat16) for w in prefix_weights], axis=1),
            values,
            preferred_element_type=jnp.float32,
        )
        attended = [
            jnp.dot(
                rounded[i * row_heads : (i + 1) * row_heads],
                pieces[i],
                preferred_element_type=jnp.float32,
            )
            for i in range(wave * batch)
        ]
        acc_ref[rows] = jnp.concatenate(attended, axis=0) + head_select(wide, heads, group)


def absorb(sizes, rows, wide_ref, acc_ref, max_ref, part_ref, keys, values, live):
    heads, group, scale = sizes
    score = contract_last(wide_ref[rows], keys) * scale + live
    chunks = [score[:, i : i + lanes] for i in range(0, score.shape[1], lanes)]
    top = functools.reduce(jnp.maximum, chunks)
    earlier = max_ref[rows]
    row_max = jnp.maximum(earlier, jnp.max(top, axis=1, keepdims=True))
    weights = [jnp.exp2(chunk - row_max) for chunk in chunks]
    factor = jnp.exp2(earlier - row_max)
    part = part_ref[rows] * factor + functools.reduce(jnp.add, weights)
    rounded = jnp.concatenate([w.astype(jnp.bfloat16) for w in weights], axis=1)
    wide = jnp.dot(rounded, values, preferred_element_type=jnp.float32)
    return acc_ref[rows] * factor + head_select(wide, heads, group), row_max, part


def fold_body(sizes, place, *refs):
    heads, group, page, scale, block_rows, replicas = sizes
    count_in, wide_ref, acc_in, max_in, part_in, bias_ref = refs[:6]
    raws = refs[6:-6]
    count_ref, acc_ref, max_ref, part_ref, keys_ref, values_ref = refs[-6:]
    count_ref[...] = jnp.broadcast_to(count_in[:1, :1], count_ref.shape)
    kinds = 2 * heads
    fill_tables(raws, page_order(page * kinds, kinds), keys_ref, values_ref, heads, page)
    keys = keys_ref[...]
    values = values_ref[...]
    live = bias_ref[:1, place : place + keys.shape[0]]
    for start in range(0, wide_ref.shape[0], block_rows):
        rows = pl.ds(start, block_rows)
        acc_ref[rows], max_ref[rows], part_ref[rows] = absorb(
            (heads, group, scale), rows, wide_ref, acc_in, max_in, part_in, keys, values, live
        )


def finish_body(sizes, place, choices, *refs):
    heads, group, page, scale, block_rows, replicas = sizes
    count_ref, wide_ref, acc_in, max_in, part_in, bias_ref = refs[:6]
    raws = refs[6:-5]
    out_hbm, out_ref, keys_ref, values_ref, sem = refs[-5:]
    kinds = 2 * heads
    me = lax.axis_index("replica")
    raws = [choice(me, raws) for choice in choices]
    fill_tables(raws, page_order(page * kinds, kinds), keys_ref, values_ref, heads, page)
    keys = keys_ref[...]
    values = values_ref[...]
    live = bias_ref[:1, place : place + keys.shape[0]]
    live_rows = count_ref[:1, :] * (heads * group)
    for start in range(0, wide_ref.shape[0], block_rows):
        rows = pl.ds(start, block_rows)
        acc, row_max, part = absorb(
            (heads, group, scale), rows, wide_ref, acc_in, max_in, part_in, keys, values, live
        )
        total = jnp.broadcast_to(jnp.sum(part, axis=1, keepdims=True), part.shape)
        row = start + lax.broadcasted_iota(jnp.int32, part.shape, 0)
        share = jnp.where(row < live_rows, 1.0 / total, 0.0)
        out_ref[rows] = (acc * share).astype(jnp.bfloat16)
    copy = pltpu.make_async_copy(out_ref, out_hbm, sem)
    copy.start()
    copy.wait()


def vmem():
    return pl.BlockSpec(memory_space=pltpu.VMEM)


def hbm():
    return pl.BlockSpec(memory_space=pltpu.HBM)


def xor_exchange(values, step):
    return lax.ppermute(values, "replica", [(i, i ^ step) for i in range(4)])


def line_plan(raw):
    def exchange(values, partners):
        return lax.ppermute(values, "replica", list(enumerate(partners)))

    middle = exchange(raw, (0, 2, 1, 3))
    near = exchange(raw, (1, 0, 3, 2))
    ends = exchange(raw, (3, 1, 2, 0))
    outward = exchange(middle, (1, 0, 3, 2))
    across = exchange(near, (0, 2, 1, 3))
    late = [middle, ends, across, outward]

    def pick(first):
        def choice(me, blocks):
            inner = (me == 1) | (me == 2)
            return lax.select(inner, blocks[first][...], blocks[first + 1][...])

        return choice

    owners = [lambda me, n, step=step: jnp.bitwise_xor(me, step) for step in (1, 3, 2)]
    return [near], owners[:1], late, owners[1:], [pick(0), pick(2)]


def gathered_stages(raw, replicas):
    everything = lax.all_gather(raw, "replica", axis=0, tiled=True)
    owners = [lambda me, n, at=at: jnp.where(me == at, -1, at) for at in range(replicas)]
    together = math.gcd(replicas, 4) * raw.shape[0]
    return [
        [everything[i : i + together]] for i in range(0, everything.shape[0], together)
    ], owners


def shards(replicas, queries, prefix_pool, page_table, suffix_kv, new_kv, suffix_len, counts):
    requests, head_count, width = queries.shape
    slots, page, unused, heads, width = prefix_pool.shape
    suffix = suffix_kv.shape[1]
    group = head_count // heads
    kinds = 2 * heads
    scale = width**-0.5 * math.log2(math.e)
    raw = prefix_pool.reshape(slots * page * kinds, width)
    batch = (-suffix * kinds) % lanes // kinds
    wave = requests // batch
    block_rows = 256
    rows = requests * head_count
    block_tokens = slots * page
    early, early_owners, choices = [], [], None
    if replicas == 4:
        early, early_owners, late, owners, choices = line_plan(raw)
        stages = [late]
    else:
        stages, owners = gathered_stages(raw, replicas)
    suffix_rows = requests * suffix * kinds
    full = jax.ShapeDtypeStruct((rows, lanes), jnp.float32)
    params = pltpu.CompilerParams(vmem_limit_bytes=24 << 20)

    def cost(tokens):
        return pl.CostEstimate(
            flops=4 * rows * tokens * width, bytes_accessed=3 << 20, transcendentals=rows * tokens
        )

    def tables(tokens):
        return [pltpu.VMEM((tokens, heads * width), jnp.bfloat16)] * 2

    acc, row_max, part, q_wide, bias = pl.pallas_call(
        functools.partial(
            local_body,
            (heads, group, page, suffix, scale, batch, replicas, wave),
            early_owners,
            owners,
        ),
        out_shape=[
            full,
            full,
            full,
            jax.ShapeDtypeStruct((rows, heads * width), jnp.bfloat16),
            jax.ShapeDtypeStruct((8, len(owners) * block_tokens), jnp.float32),
        ],
        in_specs=[hbm()] * 6 + [vmem()] * len(early),
        out_specs=[vmem()] * 5,
        scratch_shapes=[
            pltpu.SMEM(page_table.shape, jnp.int32),
            pltpu.SMEM(suffix_len.shape, jnp.int32),
            pltpu.VMEM((rows, width), jnp.bfloat16),
            pltpu.VMEM(raw.shape, jnp.bfloat16),
            pltpu.VMEM((suffix_rows, width), jnp.bfloat16),
            pltpu.VMEM((requests * kinds, width), jnp.bfloat16),
            *tables((1 + len(early)) * block_tokens),
            pltpu.SemaphoreType.DMA((5 + requests // batch // wave,)),
        ],
        compiler_params=params,
        cost_estimate=cost(2 * block_tokens),
        name="local_part",
    )(
        *[
            pltpu.with_memory_space_constraint(value, pltpu.HBM)
            for value in (
                page_table,
                suffix_len,
                queries.reshape(rows, width),
                raw,
                suffix_kv.reshape(suffix_rows, width),
                new_kv.reshape(requests * kinds, width),
            )
        ],
        *early,
    )
    sizes = (heads, group, page, scale, block_rows, replicas)
    place = 0
    count = jnp.broadcast_to(counts, (8, lanes)) if len(stages) == 1 else counts.reshape(1, 1)
    for blocks in stages[:-1]:
        tokens = sum(block.shape[0] for block in blocks) // kinds
        count, acc, row_max, part = pl.pallas_call(
            functools.partial(fold_body, sizes, place),
            out_shape=[jax.ShapeDtypeStruct((8, lanes), jnp.int32)] + [full] * 3,
            in_specs=[vmem()] * (6 + len(blocks)),
            out_specs=[vmem()] * 4,
            scratch_shapes=tables(tokens),
            compiler_params=params,
            cost_estimate=cost(tokens),
            name="fold_part",
        )(count, q_wide, acc, row_max, part, bias, *blocks)
        place += tokens
    if choices is None:
        choices = [lambda me, blocks, i=i: blocks[i] for i in range(len(stages[-1]))]
    tokens = len(choices) * stages[-1][0].shape[0] // kinds
    out = pl.pallas_call(
        functools.partial(finish_body, sizes, place, choices),
        out_shape=jax.ShapeDtypeStruct((rows, width), jnp.bfloat16),
        in_specs=[vmem()] * (6 + len(stages[-1])),
        out_specs=hbm(),
        scratch_shapes=[
            pltpu.VMEM((rows, width), jnp.bfloat16),
            *tables(tokens),
            pltpu.SemaphoreType.DMA,
        ],
        compiler_params=params,
        cost_estimate=cost(tokens),
        name="finish_part",
    )(count, q_wide, acc, row_max, part, bias, *stages[-1])
    return out.reshape(requests, head_count, width)


def solution(mesh):
    placed = (
        P(("groups", "replica"), "tensor", None),
        P(("groups", "replica"), None, None, "tensor", None),
        P("groups"),
        P(("groups", "replica"), None, None, "tensor", None),
        P(("groups", "replica"), None, "tensor", None),
        P(("groups", "replica")),
        P(("groups", "replica")),
    )
    return jax.shard_map(
        functools.partial(shards, mesh.shape["replica"]),
        mesh=mesh,
        in_specs=placed,
        out_specs=P(("groups", "replica"), "tensor", None),
        check_vma=False,
    )
```

```python
import functools
import math

import jax
import jax.numpy as jnp
from jax import lax
from jax.experimental import pallas as pl
from jax.experimental.pallas import tpu as pltpu
from jax.sharding import PartitionSpec as P

masked_score = -1e30
lanes = 128


def one_hot(shape, condition):
    row = lax.broadcasted_iota(jnp.int32, shape, 0)
    column = lax.broadcasted_iota(jnp.int32, shape, 1)
    return jnp.where(condition(row, column), 1.0, 0.0).astype(jnp.bfloat16)


def head_concat(grouped, heads, group):
    row = lax.broadcasted_iota(jnp.int32, grouped.shape, 0)
    head = lax.rem(row, heads * group) // group
    values = grouped.astype(jnp.float32)
    parts = [jnp.where(head == g, values, 0.0).astype(jnp.bfloat16) for g in range(heads)]
    return jnp.concatenate(parts, axis=1)


def head_select(wide, heads, group):
    width = wide.shape[1] // heads
    shape = (wide.shape[0], width)
    head = lax.rem(lax.broadcasted_iota(jnp.int32, shape, 0), heads * group) // group
    result = wide[:, :width]
    for g in range(1, heads):
        result = jnp.where(head == g, wide[:, g * width : (g + 1) * width], result)
    return result


def split_page(raw, order, heads):
    sorted_rows = jnp.dot(order, raw, preferred_element_type=jnp.float32).astype(jnp.bfloat16)
    tokens = raw.shape[0] // (2 * heads)
    kinds = [sorted_rows[i * tokens : (i + 1) * tokens] for i in range(2 * heads)]
    return jnp.concatenate(kinds[:heads], axis=1), jnp.concatenate(kinds[heads:], axis=1)


def page_order(page_rows, kinds):
    tokens = page_rows // kinds
    return one_hot(
        (page_rows, page_rows),
        lambda row, column: column == lax.rem(row, tokens) * kinds + row // tokens,
    )


def slot_bias(table_ref, slot):
    size = table_ref.shape[0]

    def look(index, found):
        return jnp.maximum(found, (table_ref[index] == slot).astype(jnp.int32))

    found = lax.fori_loop(0, size, look, jnp.int32(0), unroll=size <= 16)
    return jnp.where(found > 0, 0.0, masked_score)


def live_bias(table_ref, slots, page, rows):
    column = lax.broadcasted_iota(jnp.int32, (rows, len(slots) * page), 1)
    bias = jnp.zeros(column.shape, jnp.float32)
    for place, slot in enumerate(slots):
        bias = jnp.where(column // page == place, slot_bias(table_ref, slot), bias)
    return bias


def fill_tables(raws, order, keys_ref, values_ref, heads, page):
    place = 0
    page_rows = page * 2 * heads
    for raw_ref in raws:
        for at in range(0, raw_ref.shape[0], page_rows):
            keys, values = split_page(raw_ref[at : at + page_rows], order, heads)
            keys_ref[place : place + page] = keys
            values_ref[place : place + page] = values
            place += page


def contract_last(a, b):
    return lax.dot_general(a, b, (((1,), (1,)), ((), ())), preferred_element_type=jnp.float32)


def local_body(sizes, owners, *refs):
    heads, group, page, suffix, scale, batch, replicas, wave = sizes
    table_hbm, lens_hbm, q_hbm, own_hbm, suffix_hbm, new_hbm = refs[:6]
    acc_ref, max_ref, part_ref, wide_ref, bias_ref = refs[6:11]
    table_ref, lens_ref, q_ref, own_ref, suffix_ref, new_ref = refs[11:17]
    keys_ref, values_ref, sems = refs[17:]
    kinds = 2 * heads
    row_heads = heads * group
    cached = suffix * kinds
    fresh = batch * kinds
    width = cached + fresh
    batches = q_ref.shape[0] // (batch * row_heads)
    waves = batches // wave
    wave_rows = wave * batch * cached
    pairs = [
        (own_hbm, own_ref),
        (q_hbm, q_ref),
        (new_hbm, new_ref),
        (table_hbm, table_ref),
        (lens_hbm, lens_ref),
    ] + [
        (suffix_hbm.at[pl.ds(i * wave_rows, wave_rows)], suffix_ref.at[pl.ds(i * wave_rows, wave_rows)])
        for i in range(waves)
    ]
    copies = [
        pltpu.make_async_copy(source, target, sems.at[i])
        for i, (source, target) in enumerate(pairs)
    ]
    for copy in copies:
        copy.start()
    me = lax.axis_index("replica")
    slots = own_ref.shape[0] // (page * kinds)
    order = page_order(page * kinds, kinds)
    column = lax.broadcasted_iota(jnp.int32, (row_heads, width), 1)
    head = lax.broadcasted_iota(jnp.int32, (row_heads, width), 0) // group
    never = jnp.int32(1 << 20)
    token = jnp.where(
        (column < cached) & (lax.rem(column, kinds) == head), column // kinds, never
    )
    places = [
        jnp.where(column == cached + i * kinds + head, -1, token) for i in range(batch)
    ]
    for copy in copies[:5]:
        copy.wait()
    fill_tables([own_ref], order, keys_ref, values_ref, heads, page)
    live = live_bias(table_ref, [me * slots + s for s in range(slots)], page, 1)
    bias_ref[...] = live_bias(
        table_ref,
        [owner(me, replicas) * slots + s for owner in owners for s in range(slots)],
        page,
        8,
    )
    keys = keys_ref[...]
    values = values_ref[...]
    block_rows = wave * batch * row_heads
    for turn in range(waves):
        copies[5 + turn].wait()
        rows = pl.ds(turn * block_rows, block_rows)
        q = q_ref[rows]
        q_wide = head_concat(q, heads, group)
        wide_ref[rows] = q_wide
        prefix = contract_last(q_wide, keys) * scale + live
        pieces = []
        scores = []
        for i in range(wave * batch):
            request = turn * wave * batch + i
            kv = jnp.concatenate(
                [
                    suffix_ref[request * cached : (request + 1) * cached],
                    new_ref[request // batch * fresh : (request // batch + 1) * fresh],
                ],
                axis=0,
            )
            pieces.append(kv)
            score = contract_last(q[i * row_heads : (i + 1) * row_heads], kv) * scale
            scores.append(
                jnp.where(places[i % batch] < lens_ref[request], score, masked_score)
            )
        score = jnp.concatenate(scores, axis=0)
        row_max = jnp.max(jnp.maximum(prefix, score), axis=1, keepdims=True)
        weights = jnp.exp2(score - row_max)
        prefix_weights = jnp.exp2(prefix - row_max)
        part_ref[rows] = weights + prefix_weights
        max_ref[rows] = jnp.broadcast_to(row_max, weights.shape)
        rounded = pltpu.roll(weights, heads, 1).astype(jnp.bfloat16)
        wide = jnp.dot(
            prefix_weights.astype(jnp.bfloat16), values, preferred_element_type=jnp.float32
        )
        attended = [
            jnp.dot(
                rounded[i * row_heads : (i + 1) * row_heads],
                pieces[i],
                preferred_element_type=jnp.float32,
            )
            for i in range(wave * batch)
        ]
        acc_ref[rows] = jnp.concatenate(attended, axis=0) + head_select(wide, heads, group)


def absorb(sizes, rows, wide_ref, acc_ref, max_ref, part_ref, keys, values, live):
    heads, group, scale = sizes
    score = contract_last(wide_ref[rows], keys) * scale + live
    chunks = [score[:, i : i + lanes] for i in range(0, score.shape[1], lanes)]
    top = functools.reduce(jnp.maximum, chunks)
    earlier = max_ref[rows]
    row_max = jnp.maximum(earlier, jnp.max(top, axis=1, keepdims=True))
    weights = [jnp.exp2(chunk - row_max) for chunk in chunks]
    factor = jnp.exp2(earlier - row_max)
    part = part_ref[rows] * factor + functools.reduce(jnp.add, weights)
    rounded = jnp.concatenate([w.astype(jnp.bfloat16) for w in weights], axis=1)
    wide = jnp.dot(rounded, values, preferred_element_type=jnp.float32)
    return acc_ref[rows] * factor + head_select(wide, heads, group), row_max, part


def fold_body(sizes, place, *refs):
    heads, group, page, scale, block_rows, replicas = sizes
    count_in, wide_ref, acc_in, max_in, part_in, bias_ref = refs[:6]
    raws = refs[6:-6]
    count_ref, acc_ref, max_ref, part_ref, keys_ref, values_ref = refs[-6:]
    count_ref[...] = jnp.broadcast_to(count_in[:1, :1], count_ref.shape)
    kinds = 2 * heads
    fill_tables(raws, page_order(page * kinds, kinds), keys_ref, values_ref, heads, page)
    keys = keys_ref[...]
    values = values_ref[...]
    live = bias_ref[:1, place : place + keys.shape[0]]
    for start in range(0, wide_ref.shape[0], block_rows):
        rows = pl.ds(start, block_rows)
        acc_ref[rows], max_ref[rows], part_ref[rows] = absorb(
            (heads, group, scale), rows, wide_ref, acc_in, max_in, part_in, keys, values, live
        )


def finish_body(sizes, place, *refs):
    heads, group, page, scale, block_rows, replicas = sizes
    count_ref, wide_ref, acc_in, max_in, part_in, bias_ref = refs[:6]
    raws = refs[6:-5]
    out_hbm, out_ref, keys_ref, values_ref, sem = refs[-5:]
    kinds = 2 * heads
    fill_tables(raws, page_order(page * kinds, kinds), keys_ref, values_ref, heads, page)
    keys = keys_ref[...]
    values = values_ref[...]
    live = bias_ref[:1, place : place + keys.shape[0]]
    live_rows = count_ref[:1, :] * (heads * group)
    for start in range(0, wide_ref.shape[0], block_rows):
        rows = pl.ds(start, block_rows)
        acc, row_max, part = absorb(
            (heads, group, scale), rows, wide_ref, acc_in, max_in, part_in, keys, values, live
        )
        total = jnp.broadcast_to(jnp.sum(part, axis=1, keepdims=True), part.shape)
        row = start + lax.broadcasted_iota(jnp.int32, part.shape, 0)
        share = jnp.where(row < live_rows, 1.0 / total, 0.0)
        out_ref[rows] = (acc * share).astype(jnp.bfloat16)
    copy = pltpu.make_async_copy(out_ref, out_hbm, sem)
    copy.start()
    copy.wait()


def vmem():
    return pl.BlockSpec(memory_space=pltpu.VMEM)


def hbm():
    return pl.BlockSpec(memory_space=pltpu.HBM)


def folded_ring(replicas):
    return list(range(0, replicas, 2)) + list(range(1, replicas, 2))[::-1]


def ring_step(values, ring, step):
    return lax.ppermute(
        values, "replica", [(ring[i], ring[(i + step) % len(ring)]) for i in range(len(ring))]
    )


def ring_owner(ring, step):
    def owner(me, n):
        found = jnp.int32(ring[-step])
        for i in range(1, len(ring)):
            found = jnp.where(me == ring[i], ring[(i - step) % len(ring)], found)
        return found

    return owner


def ring_start(raw, replicas):
    ring = folded_ring(replicas)
    owners = [ring_owner(ring, step) for step in (1, -1, 2)]
    return ring_step(raw, ring, 1), ring_step(raw, ring, -1), owners


def ring_finish(ahead, back, replicas, anchor):
    ahead, anchor = lax.optimization_barrier((ahead, anchor))
    return [[ahead, back], [ring_step(ahead, folded_ring(replicas), 1)]], anchor


def gathered_stages(raw, replicas):
    everything = lax.all_gather(raw, "replica", axis=0, tiled=True)
    owners = [lambda me, n, at=at: jnp.where(me == at, -1, at) for at in range(replicas)]
    together = math.gcd(replicas, 4) * raw.shape[0]
    return [
        [everything[i : i + together]] for i in range(0, everything.shape[0], together)
    ], owners


def shards(replicas, queries, prefix_pool, page_table, suffix_kv, new_kv, suffix_len, counts):
    requests, head_count, width = queries.shape
    slots, page, unused, heads, width = prefix_pool.shape
    suffix = suffix_kv.shape[1]
    group = head_count // heads
    kinds = 2 * heads
    scale = width**-0.5 * math.log2(math.e)
    raw = prefix_pool.reshape(slots * page * kinds, width)
    batch = (-suffix * kinds) % lanes // kinds
    wave = requests // batch
    block_rows = 256
    rows = requests * head_count
    block_tokens = slots * page
    two_ways = replicas == 4
    if two_ways:
        ahead, back, owners = ring_start(raw, replicas)
    else:
        stages, owners = gathered_stages(raw, replicas)
    suffix_rows = requests * suffix * kinds
    full = jax.ShapeDtypeStruct((rows, lanes), jnp.float32)
    params = pltpu.CompilerParams(vmem_limit_bytes=24 << 20)

    def cost(tokens):
        return pl.CostEstimate(
            flops=4 * rows * tokens * width, bytes_accessed=3 << 20, transcendentals=rows * tokens
        )

    def tables(tokens):
        return [pltpu.VMEM((tokens, heads * width), jnp.bfloat16)] * 2

    acc, row_max, part, q_wide, bias = pl.pallas_call(
        functools.partial(
            local_body, (heads, group, page, suffix, scale, batch, replicas, wave), owners
        ),
        out_shape=[
            full,
            full,
            full,
            jax.ShapeDtypeStruct((rows, heads * width), jnp.bfloat16),
            jax.ShapeDtypeStruct((8, len(owners) * block_tokens), jnp.float32),
        ],
        in_specs=[hbm()] * 6,
        out_specs=[vmem()] * 5,
        scratch_shapes=[
            pltpu.SMEM(page_table.shape, jnp.int32),
            pltpu.SMEM(suffix_len.shape, jnp.int32),
            pltpu.VMEM((rows, width), jnp.bfloat16),
            pltpu.VMEM(raw.shape, jnp.bfloat16),
            pltpu.VMEM((suffix_rows, width), jnp.bfloat16),
            pltpu.VMEM((requests * kinds, width), jnp.bfloat16),
            *tables(block_tokens),
            pltpu.SemaphoreType.DMA((5 + requests // batch // wave,)),
        ],
        compiler_params=params,
        cost_estimate=cost(2 * block_tokens),
        name="local_part",
    )(
        *[
            pltpu.with_memory_space_constraint(value, pltpu.HBM)
            for value in (
                page_table,
                suffix_len,
                queries.reshape(rows, width),
                raw,
                suffix_kv.reshape(suffix_rows, width),
                new_kv.reshape(requests * kinds, width),
            )
        ]
    )
    if two_ways:
        stages, acc = ring_finish(ahead, back, replicas, acc)
    sizes = (heads, group, page, scale, block_rows, replicas)
    place = 0
    count = jnp.broadcast_to(counts, (8, lanes)) if len(stages) == 1 else counts.reshape(1, 1)
    for blocks in stages[:-1]:
        tokens = sum(block.shape[0] for block in blocks) // kinds
        count, acc, row_max, part = pl.pallas_call(
            functools.partial(fold_body, sizes, place),
            out_shape=[jax.ShapeDtypeStruct((8, lanes), jnp.int32)] + [full] * 3,
            in_specs=[vmem()] * (6 + len(blocks)),
            out_specs=[vmem()] * 4,
            scratch_shapes=tables(tokens),
            compiler_params=params,
            cost_estimate=cost(tokens),
            name="fold_part",
        )(count, q_wide, acc, row_max, part, bias, *blocks)
        place += tokens
    tokens = sum(block.shape[0] for block in stages[-1]) // kinds
    out = pl.pallas_call(
        functools.partial(finish_body, sizes, place),
        out_shape=jax.ShapeDtypeStruct((rows, width), jnp.bfloat16),
        in_specs=[vmem()] * (6 + len(stages[-1])),
        out_specs=hbm(),
        scratch_shapes=[
            pltpu.VMEM((rows, width), jnp.bfloat16),
            *tables(tokens),
            pltpu.SemaphoreType.DMA,
        ],
        compiler_params=params,
        cost_estimate=cost(tokens),
        name="finish_part",
    )(count, q_wide, acc, row_max, part, bias, *stages[-1])
    return out.reshape(requests, head_count, width)


def solution(mesh):
    placed = (
        P(("groups", "replica"), "tensor", None),
        P(("groups", "replica"), None, None, "tensor", None),
        P("groups"),
        P(("groups", "replica"), None, None, "tensor", None),
        P(("groups", "replica"), None, "tensor", None),
        P(("groups", "replica")),
        P(("groups", "replica")),
    )
    return jax.shard_map(
        functools.partial(shards, mesh.shape["replica"]),
        mesh=mesh,
        in_specs=placed,
        out_specs=P(("groups", "replica"), "tensor", None),
        check_vma=False,
    )
```

```python
import functools
import math

import jax
import jax.numpy as jnp
from jax import lax
from jax.experimental import pallas as pl
from jax.experimental.pallas import tpu as pltpu
from jax.sharding import PartitionSpec as P

masked_score = -1e30
lanes = 128


def one_hot(shape, condition):
    row = lax.broadcasted_iota(jnp.int32, shape, 0)
    column = lax.broadcasted_iota(jnp.int32, shape, 1)
    return jnp.where(condition(row, column), 1.0, 0.0).astype(jnp.bfloat16)


def head_concat(grouped, heads, group):
    row = lax.broadcasted_iota(jnp.int32, grouped.shape, 0)
    head = lax.rem(row, heads * group) // group
    values = grouped.astype(jnp.float32)
    parts = [jnp.where(head == g, values, 0.0).astype(jnp.bfloat16) for g in range(heads)]
    return jnp.concatenate(parts, axis=1)


def head_select(wide, heads, group):
    width = wide.shape[1] // heads
    shape = (wide.shape[0], width)
    head = lax.rem(lax.broadcasted_iota(jnp.int32, shape, 0), heads * group) // group
    result = wide[:, :width]
    for g in range(1, heads):
        result = jnp.where(head == g, wide[:, g * width : (g + 1) * width], result)
    return result


def split_page(raw, order, heads):
    sorted_rows = jnp.dot(order, raw, preferred_element_type=jnp.float32).astype(jnp.bfloat16)
    tokens = raw.shape[0] // (2 * heads)
    kinds = [sorted_rows[i * tokens : (i + 1) * tokens] for i in range(2 * heads)]
    return jnp.concatenate(kinds[:heads], axis=1), jnp.concatenate(kinds[heads:], axis=1)


def page_order(page_rows, kinds):
    tokens = page_rows // kinds
    return one_hot(
        (page_rows, page_rows),
        lambda row, column: column == lax.rem(row, tokens) * kinds + row // tokens,
    )


def slot_bias(table_ref, slot):
    size = table_ref.shape[0]

    def look(index, found):
        return jnp.maximum(found, (table_ref[index] == slot).astype(jnp.int32))

    found = lax.fori_loop(0, size, look, jnp.int32(0), unroll=size <= 16)
    return jnp.where(found > 0, 0.0, masked_score)


def live_bias(table_ref, slots, page, rows):
    column = lax.broadcasted_iota(jnp.int32, (rows, len(slots) * page), 1)
    bias = jnp.zeros(column.shape, jnp.float32)
    for place, slot in enumerate(slots):
        bias = jnp.where(column // page == place, slot_bias(table_ref, slot), bias)
    return bias


def fill_tables(raws, order, keys_ref, values_ref, heads, page):
    place = 0
    page_rows = page * 2 * heads
    for raw_ref in raws:
        for at in range(0, raw_ref.shape[0], page_rows):
            keys, values = split_page(raw_ref[at : at + page_rows], order, heads)
            keys_ref[place : place + page] = keys
            values_ref[place : place + page] = values
            place += page


def contract_last(a, b):
    return lax.dot_general(a, b, (((1,), (1,)), ((), ())), preferred_element_type=jnp.float32)


def load_body(sizes, owners, *refs):
    heads, group, page, suffix, batch, replicas = sizes
    table_hbm, lens_hbm, q_hbm, own_hbm, suffix_hbm, new_hbm = refs[:6]
    q_ref, suffix_ref, new_ref, keys_ref, values_ref, wide_ref, mask_ref, bias_ref = refs[6:14]
    table_ref, lens_ref, own_ref, sems = refs[14:]
    kinds = 2 * heads
    row_heads = heads * group
    cached = suffix * kinds
    width = cached + batch * kinds
    pairs = [
        (table_hbm, table_ref),
        (lens_hbm, lens_ref),
        (own_hbm, own_ref),
        (q_hbm, q_ref),
        (new_hbm, new_ref),
        (suffix_hbm, suffix_ref),
    ]
    copies = [
        pltpu.make_async_copy(source, target, sems.at[i])
        for i, (source, target) in enumerate(pairs)
    ]
    for copy in copies:
        copy.start()
    me = lax.axis_index("replica")
    slots = own_ref.shape[0] // (page * kinds)
    order = page_order(page * kinds, kinds)
    column = lax.broadcasted_iota(jnp.int32, (row_heads, width), 1)
    head = lax.broadcasted_iota(jnp.int32, (row_heads, width), 0) // group
    never = jnp.int32(1 << 20)
    token = jnp.where(
        (column < cached) & (lax.rem(column, kinds) == head), column // kinds, never
    )
    places = [
        jnp.where(column == cached + i * kinds + head, -1, token) for i in range(batch)
    ]
    for copy in copies[:2]:
        copy.wait()
    owners = [lambda me, n: me] + owners
    bias_ref[...] = live_bias(
        table_ref,
        [owner(me, replicas) * slots + s for owner in owners for s in range(slots)],
        page,
        8,
    )
    for request in range(lens_ref.shape[0]):
        mask_ref[request * row_heads : (request + 1) * row_heads] = jnp.where(
            places[request % batch] < lens_ref[request], 0.0, masked_score
        )
    for copy in copies[2:4]:
        copy.wait()
    fill_tables([own_ref], order, keys_ref, values_ref, heads, page)
    wide_ref[...] = head_concat(q_ref[...], heads, group)
    for copy in copies[4:]:
        copy.wait()


def local_body(sizes, *refs):
    heads, group, suffix, scale, batch = sizes
    q_ref, suffix_ref, new_ref, keys_ref, values_ref, wide_ref, mask_ref, bias_ref = refs[:8]
    acc_ref, max_ref, part_ref = refs[8:]
    kinds = 2 * heads
    row_heads = heads * group
    cached = suffix * kinds
    fresh = batch * kinds
    live = bias_ref[:1, : keys_ref.shape[0]]
    prefix = contract_last(wide_ref[...], keys_ref[...]) * scale + live
    pieces = []
    scores = []
    for request in range(q_ref.shape[0] // row_heads):
        kv = jnp.concatenate(
            [
                suffix_ref[request * cached : (request + 1) * cached],
                new_ref[request // batch * fresh : (request // batch + 1) * fresh],
            ],
            axis=0,
        )
        pieces.append(kv)
        rows = slice(request * row_heads, (request + 1) * row_heads)
        scores.append(contract_last(q_ref[rows], kv) * scale + mask_ref[rows])
    score = jnp.concatenate(scores, axis=0)
    row_max = jnp.max(jnp.maximum(prefix, score), axis=1, keepdims=True)
    weights = jnp.exp2(score - row_max)
    prefix_weights = jnp.exp2(prefix - row_max)
    part_ref[...] = weights + prefix_weights
    max_ref[...] = jnp.broadcast_to(row_max, weights.shape)
    rounded = pltpu.roll(weights, heads, 1).astype(jnp.bfloat16)
    wide = jnp.dot(
        prefix_weights.astype(jnp.bfloat16), values_ref[...], preferred_element_type=jnp.float32
    )
    attended = [
        jnp.dot(
            rounded[i * row_heads : (i + 1) * row_heads],
            piece,
            preferred_element_type=jnp.float32,
        )
        for i, piece in enumerate(pieces)
    ]
    acc_ref[...] = jnp.concatenate(attended, axis=0) + head_select(wide, heads, group)


def absorb(sizes, rows, wide_ref, acc_ref, max_ref, part_ref, keys, values, live):
    heads, group, scale = sizes
    score = contract_last(wide_ref[rows], keys) * scale + live
    chunks = [score[:, i : i + lanes] for i in range(0, score.shape[1], lanes)]
    top = functools.reduce(jnp.maximum, chunks)
    earlier = max_ref[rows]
    row_max = jnp.maximum(earlier, jnp.max(top, axis=1, keepdims=True))
    weights = [jnp.exp2(chunk - row_max) for chunk in chunks]
    factor = jnp.exp2(earlier - row_max)
    part = part_ref[rows] * factor + functools.reduce(jnp.add, weights)
    rounded = jnp.concatenate([w.astype(jnp.bfloat16) for w in weights], axis=1)
    wide = jnp.dot(rounded, values, preferred_element_type=jnp.float32)
    return acc_ref[rows] * factor + head_select(wide, heads, group), row_max, part


def fold_body(sizes, place, *refs):
    heads, group, page, scale, block_rows, replicas = sizes
    count_in, wide_ref, acc_in, max_in, part_in, bias_ref = refs[:6]
    raws = refs[6:-6]
    count_ref, acc_ref, max_ref, part_ref, keys_ref, values_ref = refs[-6:]
    count_ref[...] = jnp.broadcast_to(count_in[:1, :1], count_ref.shape)
    kinds = 2 * heads
    fill_tables(raws, page_order(page * kinds, kinds), keys_ref, values_ref, heads, page)
    keys = keys_ref[...]
    values = values_ref[...]
    live = bias_ref[:1, place : place + keys.shape[0]]
    for start in range(0, wide_ref.shape[0], block_rows):
        rows = pl.ds(start, block_rows)
        acc_ref[rows], max_ref[rows], part_ref[rows] = absorb(
            (heads, group, scale), rows, wide_ref, acc_in, max_in, part_in, keys, values, live
        )


def finish_body(sizes, place, *refs):
    heads, group, page, scale, block_rows, replicas = sizes
    count_ref, wide_ref, acc_in, max_in, part_in, bias_ref = refs[:6]
    raws = refs[6:-5]
    out_hbm, out_ref, keys_ref, values_ref, sem = refs[-5:]
    kinds = 2 * heads
    fill_tables(raws, page_order(page * kinds, kinds), keys_ref, values_ref, heads, page)
    keys = keys_ref[...]
    values = values_ref[...]
    live = bias_ref[:1, place : place + keys.shape[0]]
    live_rows = count_ref[:1, :] * (heads * group)
    for start in range(0, wide_ref.shape[0], block_rows):
        rows = pl.ds(start, block_rows)
        acc, row_max, part = absorb(
            (heads, group, scale), rows, wide_ref, acc_in, max_in, part_in, keys, values, live
        )
        total = jnp.broadcast_to(jnp.sum(part, axis=1, keepdims=True), part.shape)
        row = start + lax.broadcasted_iota(jnp.int32, part.shape, 0)
        share = jnp.where(row < live_rows, 1.0 / total, 0.0)
        out_ref[rows] = (acc * share).astype(jnp.bfloat16)
    copy = pltpu.make_async_copy(out_ref, out_hbm, sem)
    copy.start()
    copy.wait()


def vmem():
    return pl.BlockSpec(memory_space=pltpu.VMEM)


def hbm():
    return pl.BlockSpec(memory_space=pltpu.HBM)


def folded_ring(replicas):
    return list(range(0, replicas, 2)) + list(range(1, replicas, 2))[::-1]


def ring_step(values, ring, step):
    return lax.ppermute(
        values, "replica", [(ring[i], ring[(i + step) % len(ring)]) for i in range(len(ring))]
    )


def ring_owner(ring, step):
    def owner(me, n):
        found = jnp.int32(ring[-step])
        for i in range(1, len(ring)):
            found = jnp.where(me == ring[i], ring[(i - step) % len(ring)], found)
        return found

    return owner


def gathered_stages(raw, replicas):
    everything = lax.all_gather(raw, "replica", axis=0, tiled=True)
    owners = [lambda me, n, at=at: jnp.where(me == at, -1, at) for at in range(replicas)]
    together = math.gcd(replicas, 4) * raw.shape[0]
    return [
        [everything[i : i + together]] for i in range(0, everything.shape[0], together)
    ], owners


def shards(replicas, queries, prefix_pool, page_table, suffix_kv, new_kv, suffix_len, counts):
    requests, head_count, width = queries.shape
    slots, page, unused, heads, width = prefix_pool.shape
    suffix = suffix_kv.shape[1]
    group = head_count // heads
    kinds = 2 * heads
    scale = width**-0.5 * math.log2(math.e)
    raw = prefix_pool.reshape(slots * page * kinds, width)
    batch = (-suffix * kinds) % lanes // kinds
    block_rows = 256
    rows = requests * head_count
    block_tokens = slots * page
    two_ways = replicas == 4
    if two_ways:
        ring = folded_ring(replicas)
        ahead = ring_step(raw, ring, 1)
        owners = [ring_owner(ring, step) for step in (1, -1, 2)]
    else:
        stages, owners = gathered_stages(raw, replicas)
    suffix_rows = requests * suffix * kinds
    full = jax.ShapeDtypeStruct((rows, lanes), jnp.float32)
    params = pltpu.CompilerParams(vmem_limit_bytes=24 << 20)

    def cost(tokens):
        return pl.CostEstimate(
            flops=4 * rows * tokens * width, bytes_accessed=3 << 20, transcendentals=rows * tokens
        )

    def tables(tokens):
        return [pltpu.VMEM((tokens, heads * width), jnp.bfloat16)] * 2

    def low(*shape):
        return jax.ShapeDtypeStruct(shape, jnp.bfloat16)

    loaded = pl.pallas_call(
        functools.partial(load_body, (heads, group, page, suffix, batch, replicas), owners),
        out_shape=[
            low(rows, width),
            low(suffix_rows, width),
            low(requests * kinds, width),
            low(block_tokens, heads * width),
            low(block_tokens, heads * width),
            low(rows, heads * width),
            full,
            jax.ShapeDtypeStruct((8, (1 + len(owners)) * block_tokens), jnp.float32),
        ],
        in_specs=[hbm()] * 6,
        out_specs=[vmem()] * 8,
        scratch_shapes=[
            pltpu.SMEM(page_table.shape, jnp.int32),
            pltpu.SMEM(suffix_len.shape, jnp.int32),
            pltpu.VMEM(raw.shape, jnp.bfloat16),
            pltpu.SemaphoreType.DMA((6,)),
        ],
        compiler_params=params,
        cost_estimate=cost(block_tokens),
        name="load_part",
    )(
        *[
            pltpu.with_memory_space_constraint(value, pltpu.HBM)
            for value in (
                page_table,
                suffix_len,
                queries.reshape(rows, width),
                raw,
                suffix_kv.reshape(suffix_rows, width),
                new_kv.reshape(requests * kinds, width),
            )
        ]
    )
    q_wide, bias = loaded[5], loaded[7]
    if two_ways:
        own, bias = lax.optimization_barrier((raw, bias))
        back = ring_step(own, ring, -1)
    acc, row_max, part = pl.pallas_call(
        functools.partial(local_body, (heads, group, suffix, scale, batch)),
        out_shape=[full] * 3,
        in_specs=[vmem()] * 8,
        out_specs=[vmem()] * 3,
        compiler_params=params,
        cost_estimate=cost(2 * block_tokens),
        name="local_part",
    )(*loaded[:7], bias)
    if two_ways:
        ahead, acc = lax.optimization_barrier((ahead, acc))
        stages = [[ahead, back], [ring_step(ahead, ring, 1)]]
    sizes = (heads, group, page, scale, block_rows, replicas)
    place = block_tokens
    count = jnp.broadcast_to(counts, (8, lanes)) if len(stages) == 1 else counts.reshape(1, 1)
    for blocks in stages[:-1]:
        tokens = sum(block.shape[0] for block in blocks) // kinds
        count, acc, row_max, part = pl.pallas_call(
            functools.partial(fold_body, sizes, place),
            out_shape=[jax.ShapeDtypeStruct((8, lanes), jnp.int32)] + [full] * 3,
            in_specs=[vmem()] * (6 + len(blocks)),
            out_specs=[vmem()] * 4,
            scratch_shapes=tables(tokens),
            compiler_params=params,
            cost_estimate=cost(tokens),
            name="fold_part",
        )(count, q_wide, acc, row_max, part, bias, *blocks)
        place += tokens
    tokens = sum(block.shape[0] for block in stages[-1]) // kinds
    out = pl.pallas_call(
        functools.partial(finish_body, sizes, place),
        out_shape=jax.ShapeDtypeStruct((rows, width), jnp.bfloat16),
        in_specs=[vmem()] * (6 + len(stages[-1])),
        out_specs=hbm(),
        scratch_shapes=[
            pltpu.VMEM((rows, width), jnp.bfloat16),
            *tables(tokens),
            pltpu.SemaphoreType.DMA,
        ],
        compiler_params=params,
        cost_estimate=cost(tokens),
        name="finish_part",
    )(count, q_wide, acc, row_max, part, bias, *stages[-1])
    return out.reshape(requests, head_count, width)


def solution(mesh):
    placed = (
        P(("groups", "replica"), "tensor", None),
        P(("groups", "replica"), None, None, "tensor", None),
        P("groups"),
        P(("groups", "replica"), None, None, "tensor", None),
        P(("groups", "replica"), None, "tensor", None),
        P(("groups", "replica")),
        P(("groups", "replica")),
    )
    return jax.shard_map(
        functools.partial(shards, mesh.shape["replica"]),
        mesh=mesh,
        in_specs=placed,
        out_specs=P(("groups", "replica"), "tensor", None),
        check_vma=False,
    )
```

```python
import functools
import math

import jax
import jax.numpy as jnp
from jax import lax
from jax.experimental import pallas as pl
from jax.experimental.pallas import tpu as pltpu
from jax.sharding import PartitionSpec as P

masked_score = -1e30
lanes = 128


def one_hot(shape, condition):
    row = lax.broadcasted_iota(jnp.int32, shape, 0)
    column = lax.broadcasted_iota(jnp.int32, shape, 1)
    return jnp.where(condition(row, column), 1.0, 0.0).astype(jnp.bfloat16)


def head_concat(grouped, heads, group):
    row = lax.broadcasted_iota(jnp.int32, grouped.shape, 0)
    head = lax.rem(row, heads * group) // group
    values = grouped.astype(jnp.float32)
    parts = [jnp.where(head == g, values, 0.0).astype(jnp.bfloat16) for g in range(heads)]
    return jnp.concatenate(parts, axis=1)


def head_select(wide, heads, group):
    width = wide.shape[1] // heads
    shape = (wide.shape[0], width)
    head = lax.rem(lax.broadcasted_iota(jnp.int32, shape, 0), heads * group) // group
    result = wide[:, :width]
    for g in range(1, heads):
        result = jnp.where(head == g, wide[:, g * width : (g + 1) * width], result)
    return result


def split_page(raw, order, heads):
    sorted_rows = jnp.dot(order, raw, preferred_element_type=jnp.float32).astype(jnp.bfloat16)
    tokens = raw.shape[0] // (2 * heads)
    kinds = [sorted_rows[i * tokens : (i + 1) * tokens] for i in range(2 * heads)]
    return jnp.concatenate(kinds[:heads], axis=1), jnp.concatenate(kinds[heads:], axis=1)


def page_order(page_rows, kinds):
    tokens = page_rows // kinds
    return one_hot(
        (page_rows, page_rows),
        lambda row, column: column == lax.rem(row, tokens) * kinds + row // tokens,
    )


def slot_bias(table_ref, slot):
    size = table_ref.shape[0]

    def look(index, found):
        return jnp.maximum(found, (table_ref[index] == slot).astype(jnp.int32))

    found = lax.fori_loop(0, size, look, jnp.int32(0), unroll=size <= 16)
    return jnp.where(found > 0, 0.0, masked_score)


def live_bias(table_ref, slots, page, rows):
    column = lax.broadcasted_iota(jnp.int32, (rows, len(slots) * page), 1)
    bias = jnp.zeros(column.shape, jnp.float32)
    for place, slot in enumerate(slots):
        bias = jnp.where(column // page == place, slot_bias(table_ref, slot), bias)
    return bias


def fill_tables(raws, order, keys_ref, values_ref, heads, page):
    place = 0
    page_rows = page * 2 * heads
    for raw_ref in raws:
        for at in range(0, raw_ref.shape[0], page_rows):
            keys, values = split_page(raw_ref[at : at + page_rows], order, heads)
            keys_ref[place : place + page] = keys
            values_ref[place : place + page] = values
            place += page


def contract_last(a, b):
    return lax.dot_general(a, b, (((1,), (1,)), ((), ())), preferred_element_type=jnp.float32)


def load_body(sizes, owners, *refs):
    heads, group, page, suffix, batch, replicas = sizes
    table_hbm, lens_hbm, q_hbm, own_hbm, suffix_hbm, new_hbm = refs[:6]
    q_ref, suffix_ref, new_ref, keys_ref, values_ref, wide_ref, mask_ref, bias_ref = refs[6:14]
    table_ref, lens_ref, own_ref, sems = refs[14:]
    kinds = 2 * heads
    row_heads = heads * group
    cached = suffix * kinds
    width = cached + batch * kinds
    pairs = [
        (table_hbm, table_ref),
        (lens_hbm, lens_ref),
        (own_hbm, own_ref),
        (q_hbm, q_ref),
        (new_hbm, new_ref),
        (suffix_hbm, suffix_ref),
    ]
    copies = [
        pltpu.make_async_copy(source, target, sems.at[i])
        for i, (source, target) in enumerate(pairs)
    ]
    for copy in copies:
        copy.start()
    me = lax.axis_index("replica")
    slots = own_ref.shape[0] // (page * kinds)
    order = page_order(page * kinds, kinds)
    column = lax.broadcasted_iota(jnp.int32, (row_heads, width), 1)
    head = lax.broadcasted_iota(jnp.int32, (row_heads, width), 0) // group
    never = jnp.int32(1 << 20)
    token = jnp.where(
        (column < cached) & (lax.rem(column, kinds) == head), column // kinds, never
    )
    places = [
        jnp.where(column == cached + i * kinds + head, -1, token) for i in range(batch)
    ]
    for copy in copies[:2]:
        copy.wait()
    owners = [lambda me, n: me] + owners
    bias_ref[...] = live_bias(
        table_ref,
        [owner(me, replicas) * slots + s for owner in owners for s in range(slots)],
        page,
        8,
    )
    for request in range(lens_ref.shape[0]):
        mask_ref[request * row_heads : (request + 1) * row_heads] = jnp.where(
            places[request % batch] < lens_ref[request], 0.0, masked_score
        )
    for copy in copies[2:4]:
        copy.wait()
    fill_tables([own_ref], order, keys_ref, values_ref, heads, page)
    wide_ref[...] = head_concat(q_ref[...], heads, group)
    for copy in copies[4:]:
        copy.wait()


def local_body(sizes, *refs):
    heads, group, suffix, scale, batch = sizes
    q_ref, suffix_ref, new_ref, keys_ref, values_ref, wide_ref, mask_ref, bias_ref = refs[:8]
    acc_ref, max_ref, part_ref = refs[8:]
    kinds = 2 * heads
    row_heads = heads * group
    cached = suffix * kinds
    fresh = batch * kinds
    live = bias_ref[:1, : keys_ref.shape[0]]
    prefix = contract_last(wide_ref[...], keys_ref[...]) * scale + live
    pieces = []
    scores = []
    for request in range(q_ref.shape[0] // row_heads):
        kv = jnp.concatenate(
            [
                suffix_ref[request * cached : (request + 1) * cached],
                new_ref[request // batch * fresh : (request // batch + 1) * fresh],
            ],
            axis=0,
        )
        pieces.append(kv)
        rows = slice(request * row_heads, (request + 1) * row_heads)
        scores.append(contract_last(q_ref[rows], kv) * scale + mask_ref[rows])
    score = jnp.concatenate(scores, axis=0)
    row_max = jnp.max(jnp.maximum(prefix, score), axis=1, keepdims=True)
    weights = jnp.exp2(score - row_max)
    prefix_weights = jnp.exp2(prefix - row_max)
    part_ref[...] = weights + prefix_weights
    max_ref[...] = jnp.broadcast_to(row_max, weights.shape)
    rounded = pltpu.roll(weights, heads, 1).astype(jnp.bfloat16)
    wide = jnp.dot(
        prefix_weights.astype(jnp.bfloat16), values_ref[...], preferred_element_type=jnp.float32
    )
    attended = [
        jnp.dot(
            rounded[i * row_heads : (i + 1) * row_heads],
            piece,
            preferred_element_type=jnp.float32,
        )
        for i, piece in enumerate(pieces)
    ]
    acc_ref[...] = jnp.concatenate(attended, axis=0) + head_select(wide, heads, group)


def absorb(sizes, rows, wide_ref, acc_ref, max_ref, part_ref, keys, values, live):
    heads, group, scale = sizes
    score = contract_last(wide_ref[rows], keys) * scale + live
    chunks = [score[:, i : i + lanes] for i in range(0, score.shape[1], lanes)]
    top = functools.reduce(jnp.maximum, chunks)
    earlier = max_ref[rows]
    row_max = jnp.maximum(earlier, jnp.max(top, axis=1, keepdims=True))
    weights = [jnp.exp2(chunk - row_max) for chunk in chunks]
    factor = jnp.exp2(earlier - row_max)
    part = part_ref[rows] * factor + functools.reduce(jnp.add, weights)
    rounded = jnp.concatenate([w.astype(jnp.bfloat16) for w in weights], axis=1)
    wide = jnp.dot(rounded, values, preferred_element_type=jnp.float32)
    return acc_ref[rows] * factor + head_select(wide, heads, group), row_max, part


def fold_body(sizes, place, *refs):
    heads, group, page, scale, block_rows, replicas = sizes
    count_in, wide_ref, acc_in, max_in, part_in, bias_ref = refs[:6]
    raws = refs[6:-6]
    count_ref, acc_ref, max_ref, part_ref, keys_ref, values_ref = refs[-6:]
    count_ref[...] = jnp.broadcast_to(count_in[:1, :1], count_ref.shape)
    kinds = 2 * heads
    fill_tables(raws, page_order(page * kinds, kinds), keys_ref, values_ref, heads, page)
    keys = keys_ref[...]
    values = values_ref[...]
    live = bias_ref[:1, place : place + keys.shape[0]]
    for start in range(0, wide_ref.shape[0], block_rows):
        rows = pl.ds(start, block_rows)
        acc_ref[rows], max_ref[rows], part_ref[rows] = absorb(
            (heads, group, scale), rows, wide_ref, acc_in, max_in, part_in, keys, values, live
        )


def finish_body(sizes, place, *refs):
    heads, group, page, scale, block_rows, replicas = sizes
    count_ref, wide_ref, acc_in, max_in, part_in, bias_ref = refs[:6]
    raws = refs[6:-5]
    out_hbm, out_ref, keys_ref, values_ref, sem = refs[-5:]
    kinds = 2 * heads
    fill_tables(raws, page_order(page * kinds, kinds), keys_ref, values_ref, heads, page)
    keys = keys_ref[...]
    values = values_ref[...]
    live = bias_ref[:1, place : place + keys.shape[0]]
    live_rows = count_ref[:1, :] * (heads * group)
    for start in range(0, wide_ref.shape[0], block_rows):
        rows = pl.ds(start, block_rows)
        acc, row_max, part = absorb(
            (heads, group, scale), rows, wide_ref, acc_in, max_in, part_in, keys, values, live
        )
        total = jnp.broadcast_to(jnp.sum(part, axis=1, keepdims=True), part.shape)
        row = start + lax.broadcasted_iota(jnp.int32, part.shape, 0)
        share = jnp.where(row < live_rows, 1.0 / total, 0.0)
        out_ref[rows] = (acc * share).astype(jnp.bfloat16)
    copy = pltpu.make_async_copy(out_ref, out_hbm, sem)
    copy.start()
    copy.wait()


def vmem():
    return pl.BlockSpec(memory_space=pltpu.VMEM)


def hbm():
    return pl.BlockSpec(memory_space=pltpu.HBM)


def folded_ring(replicas):
    return list(range(0, replicas, 2)) + list(range(1, replicas, 2))[::-1]


def ring_step(values, ring, step):
    return lax.ppermute(
        values, "replica", [(ring[i], ring[(i + step) % len(ring)]) for i in range(len(ring))]
    )


def ring_owner(ring, step):
    def owner(me, n):
        found = jnp.int32(ring[-step])
        for i in range(1, len(ring)):
            found = jnp.where(me == ring[i], ring[(i - step) % len(ring)], found)
        return found

    return owner


def gathered_stages(raw, replicas):
    everything = lax.all_gather(raw, "replica", axis=0, tiled=True)
    owners = [lambda me, n, at=at: jnp.where(me == at, -1, at) for at in range(replicas)]
    together = math.gcd(replicas, 4) * raw.shape[0]
    return [
        [everything[i : i + together]] for i in range(0, everything.shape[0], together)
    ], owners


def shards(replicas, queries, prefix_pool, page_table, suffix_kv, new_kv, suffix_len, counts):
    requests, head_count, width = queries.shape
    slots, page, unused, heads, width = prefix_pool.shape
    suffix = suffix_kv.shape[1]
    group = head_count // heads
    kinds = 2 * heads
    scale = width**-0.5 * math.log2(math.e)
    raw = prefix_pool.reshape(slots * page * kinds, width)
    batch = (-suffix * kinds) % lanes // kinds
    block_rows = 256
    rows = requests * head_count
    block_tokens = slots * page
    two_ways = replicas == 4
    if two_ways:
        ring = folded_ring(replicas)
        ahead, back = ring_step(raw, ring, -1), ring_step(raw, ring, 1)
        owners = [ring_owner(ring, step) for step in (-1, 1, 2)]
    else:
        stages, owners = gathered_stages(raw, replicas)
    suffix_rows = requests * suffix * kinds
    full = jax.ShapeDtypeStruct((rows, lanes), jnp.float32)
    params = pltpu.CompilerParams(vmem_limit_bytes=24 << 20)

    def cost(tokens):
        return pl.CostEstimate(
            flops=4 * rows * tokens * width, bytes_accessed=3 << 20, transcendentals=rows * tokens
        )

    def tables(tokens):
        return [pltpu.VMEM((tokens, heads * width), jnp.bfloat16)] * 2

    def low(*shape):
        return jax.ShapeDtypeStruct(shape, jnp.bfloat16)

    loaded = pl.pallas_call(
        functools.partial(load_body, (heads, group, page, suffix, batch, replicas), owners),
        out_shape=[
            low(rows, width),
            low(suffix_rows, width),
            low(requests * kinds, width),
            low(block_tokens, heads * width),
            low(block_tokens, heads * width),
            low(rows, heads * width),
            full,
            jax.ShapeDtypeStruct((8, (1 + len(owners)) * block_tokens), jnp.float32),
        ],
        in_specs=[hbm()] * 6,
        out_specs=[vmem()] * 8,
        scratch_shapes=[
            pltpu.SMEM(page_table.shape, jnp.int32),
            pltpu.SMEM(suffix_len.shape, jnp.int32),
            pltpu.VMEM(raw.shape, jnp.bfloat16),
            pltpu.SemaphoreType.DMA((6,)),
        ],
        compiler_params=params,
        cost_estimate=cost(block_tokens),
        name="load_part",
    )(
        *[
            pltpu.with_memory_space_constraint(value, pltpu.HBM)
            for value in (
                page_table,
                suffix_len,
                queries.reshape(rows, width),
                raw,
                suffix_kv.reshape(suffix_rows, width),
                new_kv.reshape(requests * kinds, width),
            )
        ]
    )
    q_wide, bias = loaded[5], loaded[7]
    if two_ways:
        ahead, bias = lax.optimization_barrier((ahead, bias))
        passed = ring_step(ahead, ring, -1)
    acc, row_max, part = pl.pallas_call(
        functools.partial(local_body, (heads, group, suffix, scale, batch)),
        out_shape=[full] * 3,
        in_specs=[vmem()] * 8,
        out_specs=[vmem()] * 3,
        compiler_params=params,
        cost_estimate=cost(2 * block_tokens),
        name="local_part",
    )(*loaded[:7], bias)
    if two_ways:
        stages = [[ahead, back], [passed]]
    sizes = (heads, group, page, scale, block_rows, replicas)
    place = block_tokens
    count = jnp.broadcast_to(counts, (8, lanes)) if len(stages) == 1 else counts.reshape(1, 1)
    for blocks in stages[:-1]:
        tokens = sum(block.shape[0] for block in blocks) // kinds
        count, acc, row_max, part = pl.pallas_call(
            functools.partial(fold_body, sizes, place),
            out_shape=[jax.ShapeDtypeStruct((8, lanes), jnp.int32)] + [full] * 3,
            in_specs=[vmem()] * (6 + len(blocks)),
            out_specs=[vmem()] * 4,
            scratch_shapes=tables(tokens),
            compiler_params=params,
            cost_estimate=cost(tokens),
            name="fold_part",
        )(count, q_wide, acc, row_max, part, bias, *blocks)
        place += tokens
    tokens = sum(block.shape[0] for block in stages[-1]) // kinds
    out = pl.pallas_call(
        functools.partial(finish_body, sizes, place),
        out_shape=jax.ShapeDtypeStruct((rows, width), jnp.bfloat16),
        in_specs=[vmem()] * (6 + len(stages[-1])),
        out_specs=hbm(),
        scratch_shapes=[
            pltpu.VMEM((rows, width), jnp.bfloat16),
            *tables(tokens),
            pltpu.SemaphoreType.DMA,
        ],
        compiler_params=params,
        cost_estimate=cost(tokens),
        name="finish_part",
    )(count, q_wide, acc, row_max, part, bias, *stages[-1])
    return out.reshape(requests, head_count, width)


def solution(mesh):
    placed = (
        P(("groups", "replica"), "tensor", None),
        P(("groups", "replica"), None, None, "tensor", None),
        P("groups"),
        P(("groups", "replica"), None, None, "tensor", None),
        P(("groups", "replica"), None, "tensor", None),
        P(("groups", "replica")),
        P(("groups", "replica")),
    )
    return jax.shard_map(
        functools.partial(shards, mesh.shape["replica"]),
        mesh=mesh,
        in_specs=placed,
        out_specs=P(("groups", "replica"), "tensor", None),
        check_vma=False,
    )
```

```python
import functools
import math

import jax
import jax.numpy as jnp
from jax import lax
from jax.experimental import pallas as pl
from jax.experimental.pallas import tpu as pltpu
from jax.sharding import PartitionSpec as P

masked_score = -1e30
lanes = 128


def one_hot(shape, condition):
    row = lax.broadcasted_iota(jnp.int32, shape, 0)
    column = lax.broadcasted_iota(jnp.int32, shape, 1)
    return jnp.where(condition(row, column), 1.0, 0.0).astype(jnp.bfloat16)


def head_concat(grouped, heads, group):
    row = lax.broadcasted_iota(jnp.int32, grouped.shape, 0)
    head = lax.rem(row, heads * group) // group
    values = grouped.astype(jnp.float32)
    parts = [jnp.where(head == g, values, 0.0).astype(jnp.bfloat16) for g in range(heads)]
    return jnp.concatenate(parts, axis=1)


def head_select(wide, heads, group):
    width = wide.shape[1] // heads
    shape = (wide.shape[0], width)
    head = lax.rem(lax.broadcasted_iota(jnp.int32, shape, 0), heads * group) // group
    result = wide[:, :width]
    for g in range(1, heads):
        result = jnp.where(head == g, wide[:, g * width : (g + 1) * width], result)
    return result


def split_page(raw, order, heads):
    sorted_rows = jnp.dot(order, raw, preferred_element_type=jnp.float32).astype(jnp.bfloat16)
    tokens = raw.shape[0] // (2 * heads)
    kinds = [sorted_rows[i * tokens : (i + 1) * tokens] for i in range(2 * heads)]
    return jnp.concatenate(kinds[:heads], axis=1), jnp.concatenate(kinds[heads:], axis=1)


def page_order(page_rows, kinds):
    tokens = page_rows // kinds
    return one_hot(
        (page_rows, page_rows),
        lambda row, column: column == lax.rem(row, tokens) * kinds + row // tokens,
    )


def slot_bias(table_ref, slot):
    size = table_ref.shape[0]

    def look(index, found):
        return jnp.maximum(found, (table_ref[index] == slot).astype(jnp.int32))

    found = lax.fori_loop(0, size, look, jnp.int32(0), unroll=size <= 16)
    return jnp.where(found > 0, 0.0, masked_score)


def live_bias(table_ref, slots, page, rows):
    column = lax.broadcasted_iota(jnp.int32, (rows, len(slots) * page), 1)
    bias = jnp.zeros(column.shape, jnp.float32)
    for place, slot in enumerate(slots):
        bias = jnp.where(column // page == place, slot_bias(table_ref, slot), bias)
    return bias


def fill_tables(raws, order, keys_ref, values_ref, heads, page):
    place = 0
    page_rows = page * 2 * heads
    for raw_ref in raws:
        for at in range(0, raw_ref.shape[0], page_rows):
            keys, values = split_page(raw_ref[at : at + page_rows], order, heads)
            keys_ref[place : place + page] = keys
            values_ref[place : place + page] = values
            place += page


def contract_last(a, b):
    return lax.dot_general(a, b, (((1,), (1,)), ((), ())), preferred_element_type=jnp.float32)


def load_body(sizes, owners, *refs):
    heads, group, page, suffix, batch, replicas = sizes
    table_hbm, lens_hbm, q_hbm, own_hbm, suffix_hbm, new_hbm = refs[:6]
    q_ref, suffix_ref, new_ref, keys_ref, values_ref, wide_ref, mask_ref, bias_ref = refs[6:14]
    table_ref, lens_ref, own_ref, sems = refs[14:]
    kinds = 2 * heads
    row_heads = heads * group
    cached = suffix * kinds
    width = cached + batch * kinds
    pairs = [
        (table_hbm, table_ref),
        (lens_hbm, lens_ref),
        (own_hbm, own_ref),
        (q_hbm, q_ref),
        (new_hbm, new_ref),
        (suffix_hbm, suffix_ref),
    ]
    copies = [
        pltpu.make_async_copy(source, target, sems.at[i])
        for i, (source, target) in enumerate(pairs)
    ]
    for copy in copies:
        copy.start()
    me = lax.axis_index("replica")
    slots = own_ref.shape[0] // (page * kinds)
    order = page_order(page * kinds, kinds)
    column = lax.broadcasted_iota(jnp.int32, (row_heads, width), 1)
    head = lax.broadcasted_iota(jnp.int32, (row_heads, width), 0) // group
    never = jnp.int32(1 << 20)
    token = jnp.where(
        (column < cached) & (lax.rem(column, kinds) == head), column // kinds, never
    )
    places = [
        jnp.where(column == cached + i * kinds + head, -1, token) for i in range(batch)
    ]
    for copy in copies[:2]:
        copy.wait()
    owners = [lambda me, n: me] + owners
    bias_ref[...] = live_bias(
        table_ref,
        [owner(me, replicas) * slots + s for owner in owners for s in range(slots)],
        page,
        8,
    )
    for request in range(lens_ref.shape[0]):
        mask_ref[request * row_heads : (request + 1) * row_heads] = jnp.where(
            places[request % batch] < lens_ref[request], 0.0, masked_score
        )
    for copy in copies[2:4]:
        copy.wait()
    fill_tables([own_ref], order, keys_ref, values_ref, heads, page)
    wide_ref[...] = head_concat(q_ref[...], heads, group)
    for copy in copies[4:]:
        copy.wait()


def local_body(sizes, *refs):
    heads, group, suffix, scale, batch = sizes
    q_ref, suffix_ref, new_ref, keys_ref, values_ref, wide_ref, mask_ref, bias_ref = refs[:8]
    acc_ref, max_ref, part_ref = refs[8:]
    kinds = 2 * heads
    row_heads = heads * group
    cached = suffix * kinds
    fresh = batch * kinds
    live = bias_ref[:1, : keys_ref.shape[0]]
    prefix = contract_last(wide_ref[...], keys_ref[...]) * scale + live
    pieces = []
    scores = []
    for request in range(q_ref.shape[0] // row_heads):
        kv = jnp.concatenate(
            [
                suffix_ref[request * cached : (request + 1) * cached],
                new_ref[request // batch * fresh : (request // batch + 1) * fresh],
            ],
            axis=0,
        )
        pieces.append(kv)
        rows = slice(request * row_heads, (request + 1) * row_heads)
        scores.append(contract_last(q_ref[rows], kv) * scale + mask_ref[rows])
    score = jnp.concatenate(scores, axis=0)
    row_max = jnp.max(jnp.maximum(prefix, score), axis=1, keepdims=True)
    weights = jnp.exp2(score - row_max)
    prefix_weights = jnp.exp2(prefix - row_max)
    part_ref[...] = weights + prefix_weights
    max_ref[...] = jnp.broadcast_to(row_max, weights.shape)
    rounded = pltpu.roll(weights, heads, 1).astype(jnp.bfloat16)
    wide = jnp.dot(
        prefix_weights.astype(jnp.bfloat16), values_ref[...], preferred_element_type=jnp.float32
    )
    attended = [
        jnp.dot(
            rounded[i * row_heads : (i + 1) * row_heads],
            piece,
            preferred_element_type=jnp.float32,
        )
        for i, piece in enumerate(pieces)
    ]
    acc_ref[...] = jnp.concatenate(attended, axis=0) + head_select(wide, heads, group)


def absorb(sizes, rows, wide_ref, acc_ref, max_ref, part_ref, keys, values, live):
    heads, group, scale = sizes
    score = contract_last(wide_ref[rows], keys) * scale + live
    chunks = [score[:, i : i + lanes] for i in range(0, score.shape[1], lanes)]
    top = functools.reduce(jnp.maximum, chunks)
    earlier = max_ref[rows]
    row_max = jnp.maximum(earlier, jnp.max(top, axis=1, keepdims=True))
    weights = [jnp.exp2(chunk - row_max) for chunk in chunks]
    factor = jnp.exp2(earlier - row_max)
    part = part_ref[rows] * factor + functools.reduce(jnp.add, weights)
    rounded = jnp.concatenate([w.astype(jnp.bfloat16) for w in weights], axis=1)
    wide = jnp.dot(rounded, values, preferred_element_type=jnp.float32)
    return acc_ref[rows] * factor + head_select(wide, heads, group), row_max, part


def fold_body(sizes, place, *refs):
    heads, group, page, scale, block_rows, replicas = sizes
    count_in, wide_ref, acc_in, max_in, part_in, bias_ref = refs[:6]
    raws = refs[6:-6]
    count_ref, acc_ref, max_ref, part_ref, keys_ref, values_ref = refs[-6:]
    count_ref[...] = jnp.broadcast_to(count_in[:1, :1], count_ref.shape)
    kinds = 2 * heads
    fill_tables(raws, page_order(page * kinds, kinds), keys_ref, values_ref, heads, page)
    keys = keys_ref[...]
    values = values_ref[...]
    live = bias_ref[:1, place : place + keys.shape[0]]
    for start in range(0, wide_ref.shape[0], block_rows):
        rows = pl.ds(start, block_rows)
        acc_ref[rows], max_ref[rows], part_ref[rows] = absorb(
            (heads, group, scale), rows, wide_ref, acc_in, max_in, part_in, keys, values, live
        )


def finish_body(sizes, place, *refs):
    heads, group, page, scale, block_rows, replicas = sizes
    count_ref, wide_ref, acc_in, max_in, part_in, bias_ref = refs[:6]
    raws = refs[6:-5]
    out_hbm, out_ref, keys_ref, values_ref, sem = refs[-5:]
    kinds = 2 * heads
    fill_tables(raws, page_order(page * kinds, kinds), keys_ref, values_ref, heads, page)
    keys = keys_ref[...]
    values = values_ref[...]
    live = bias_ref[:1, place : place + keys.shape[0]]
    live_rows = count_ref[:1, :] * (heads * group)
    for start in range(0, wide_ref.shape[0], block_rows):
        rows = pl.ds(start, block_rows)
        acc, row_max, part = absorb(
            (heads, group, scale), rows, wide_ref, acc_in, max_in, part_in, keys, values, live
        )
        total = jnp.broadcast_to(jnp.sum(part, axis=1, keepdims=True), part.shape)
        row = start + lax.broadcasted_iota(jnp.int32, part.shape, 0)
        share = jnp.where(row < live_rows, 1.0 / total, 0.0)
        out_ref[rows] = (acc * share).astype(jnp.bfloat16)
    copy = pltpu.make_async_copy(out_ref, out_hbm, sem)
    copy.start()
    copy.wait()


def vmem():
    return pl.BlockSpec(memory_space=pltpu.VMEM)


def hbm():
    return pl.BlockSpec(memory_space=pltpu.HBM)


def folded_ring(replicas):
    return list(range(0, replicas, 2)) + list(range(1, replicas, 2))[::-1]


def ring_step(values, ring, step):
    return lax.ppermute(
        values, "replica", [(ring[i], ring[(i + step) % len(ring)]) for i in range(len(ring))]
    )


def ring_owner(ring, step):
    def owner(me, n):
        found = jnp.int32(ring[-step])
        for i in range(1, len(ring)):
            found = jnp.where(me == ring[i], ring[(i - step) % len(ring)], found)
        return found

    return owner


def gathered_stages(raw, replicas):
    everything = lax.all_gather(raw, "replica", axis=0, tiled=True)
    owners = [lambda me, n, at=at: jnp.where(me == at, -1, at) for at in range(replicas)]
    together = math.gcd(replicas, 4) * raw.shape[0]
    return [
        [everything[i : i + together]] for i in range(0, everything.shape[0], together)
    ], owners


def shards(replicas, queries, prefix_pool, page_table, suffix_kv, new_kv, suffix_len, counts):
    requests, head_count, width = queries.shape
    slots, page, unused, heads, width = prefix_pool.shape
    suffix = suffix_kv.shape[1]
    group = head_count // heads
    kinds = 2 * heads
    scale = width**-0.5 * math.log2(math.e)
    raw = prefix_pool.reshape(slots * page * kinds, width)
    batch = (-suffix * kinds) % lanes // kinds
    block_rows = 256
    rows = requests * head_count
    block_tokens = slots * page
    two_ways = replicas == 4
    if two_ways:
        ring = folded_ring(replicas)
        ahead = ring_step(raw, ring, -1)
        owners = [ring_owner(ring, step) for step in (-1, 1, 2)]
    else:
        stages, owners = gathered_stages(raw, replicas)
    suffix_rows = requests * suffix * kinds
    full = jax.ShapeDtypeStruct((rows, lanes), jnp.float32)
    params = pltpu.CompilerParams(vmem_limit_bytes=24 << 20)

    def cost(tokens):
        return pl.CostEstimate(
            flops=4 * rows * tokens * width, bytes_accessed=3 << 20, transcendentals=rows * tokens
        )

    def tables(tokens):
        return [pltpu.VMEM((tokens, heads * width), jnp.bfloat16)] * 2

    def low(*shape):
        return jax.ShapeDtypeStruct(shape, jnp.bfloat16)

    loaded = pl.pallas_call(
        functools.partial(load_body, (heads, group, page, suffix, batch, replicas), owners),
        out_shape=[
            low(rows, width),
            low(suffix_rows, width),
            low(requests * kinds, width),
            low(block_tokens, heads * width),
            low(block_tokens, heads * width),
            low(rows, heads * width),
            full,
            jax.ShapeDtypeStruct((8, (1 + len(owners)) * block_tokens), jnp.float32),
        ],
        in_specs=[hbm()] * 6,
        out_specs=[vmem()] * 8,
        scratch_shapes=[
            pltpu.SMEM(page_table.shape, jnp.int32),
            pltpu.SMEM(suffix_len.shape, jnp.int32),
            pltpu.VMEM(raw.shape, jnp.bfloat16),
            pltpu.SemaphoreType.DMA((6,)),
        ],
        compiler_params=params,
        cost_estimate=cost(block_tokens),
        name="load_part",
    )(
        *[
            pltpu.with_memory_space_constraint(value, pltpu.HBM)
            for value in (
                page_table,
                suffix_len,
                queries.reshape(rows, width),
                raw,
                suffix_kv.reshape(suffix_rows, width),
                new_kv.reshape(requests * kinds, width),
            )
        ]
    )
    q_wide, bias = loaded[5], loaded[7]
    if two_ways:
        own, bias = lax.optimization_barrier((raw, bias))
        back = ring_step(own, ring, 1)
    acc, row_max, part = pl.pallas_call(
        functools.partial(local_body, (heads, group, suffix, scale, batch)),
        out_shape=[full] * 3,
        in_specs=[vmem()] * 8,
        out_specs=[vmem()] * 3,
        compiler_params=params,
        cost_estimate=cost(2 * block_tokens),
        name="local_part",
    )(*loaded[:7], bias)
    if two_ways:
        ahead, acc = lax.optimization_barrier((ahead, acc))
        stages = [[ahead, back], [ring_step(ahead, ring, -1)]]
    sizes = (heads, group, page, scale, block_rows, replicas)
    place = block_tokens
    count = jnp.broadcast_to(counts, (8, lanes)) if len(stages) == 1 else counts.reshape(1, 1)
    for blocks in stages[:-1]:
        tokens = sum(block.shape[0] for block in blocks) // kinds
        count, acc, row_max, part = pl.pallas_call(
            functools.partial(fold_body, sizes, place),
            out_shape=[jax.ShapeDtypeStruct((8, lanes), jnp.int32)] + [full] * 3,
            in_specs=[vmem()] * (6 + len(blocks)),
            out_specs=[vmem()] * 4,
            scratch_shapes=tables(tokens),
            compiler_params=params,
            cost_estimate=cost(tokens),
            name="fold_part",
        )(count, q_wide, acc, row_max, part, bias, *blocks)
        place += tokens
    tokens = sum(block.shape[0] for block in stages[-1]) // kinds
    out = pl.pallas_call(
        functools.partial(finish_body, sizes, place),
        out_shape=jax.ShapeDtypeStruct((rows, width), jnp.bfloat16),
        in_specs=[vmem()] * (6 + len(stages[-1])),
        out_specs=hbm(),
        scratch_shapes=[
            pltpu.VMEM((rows, width), jnp.bfloat16),
            *tables(tokens),
            pltpu.SemaphoreType.DMA,
        ],
        compiler_params=params,
        cost_estimate=cost(tokens),
        name="finish_part",
    )(count, q_wide, acc, row_max, part, bias, *stages[-1])
    return out.reshape(requests, head_count, width)


def solution(mesh):
    placed = (
        P(("groups", "replica"), "tensor", None),
        P(("groups", "replica"), None, None, "tensor", None),
        P("groups"),
        P(("groups", "replica"), None, None, "tensor", None),
        P(("groups", "replica"), None, "tensor", None),
        P(("groups", "replica")),
        P(("groups", "replica")),
    )
    return jax.shard_map(
        functools.partial(shards, mesh.shape["replica"]),
        mesh=mesh,
        in_specs=placed,
        out_specs=P(("groups", "replica"), "tensor", None),
        check_vma=False,
    )
```

```python
import functools
import math

import jax
import jax.numpy as jnp
from jax import lax
from jax.experimental import pallas as pl
from jax.experimental.pallas import tpu as pltpu
from jax.sharding import PartitionSpec as P

masked_score = -1e30
lanes = 128


def one_hot(shape, condition):
    row = lax.broadcasted_iota(jnp.int32, shape, 0)
    column = lax.broadcasted_iota(jnp.int32, shape, 1)
    return jnp.where(condition(row, column), 1.0, 0.0).astype(jnp.bfloat16)


def head_concat(grouped, heads, group):
    row = lax.broadcasted_iota(jnp.int32, grouped.shape, 0)
    head = lax.rem(row, heads * group) // group
    values = grouped.astype(jnp.float32)
    parts = [jnp.where(head == g, values, 0.0).astype(jnp.bfloat16) for g in range(heads)]
    return jnp.concatenate(parts, axis=1)


def head_select(wide, heads, group):
    width = wide.shape[1] // heads
    shape = (wide.shape[0], width)
    head = lax.rem(lax.broadcasted_iota(jnp.int32, shape, 0), heads * group) // group
    result = wide[:, :width]
    for g in range(1, heads):
        result = jnp.where(head == g, wide[:, g * width : (g + 1) * width], result)
    return result


def split_page(raw, order, heads):
    sorted_rows = jnp.dot(order, raw, preferred_element_type=jnp.float32).astype(jnp.bfloat16)
    tokens = raw.shape[0] // (2 * heads)
    kinds = [sorted_rows[i * tokens : (i + 1) * tokens] for i in range(2 * heads)]
    return jnp.concatenate(kinds[:heads], axis=1), jnp.concatenate(kinds[heads:], axis=1)


def page_order(page_rows, kinds):
    tokens = page_rows // kinds
    return one_hot(
        (page_rows, page_rows),
        lambda row, column: column == lax.rem(row, tokens) * kinds + row // tokens,
    )


def slot_bias(table_ref, slot):
    size = table_ref.shape[0]

    def look(index, found):
        return jnp.maximum(found, (table_ref[index] == slot).astype(jnp.int32))

    found = lax.fori_loop(0, size, look, jnp.int32(0), unroll=size <= 16)
    return jnp.where(found > 0, 0.0, masked_score)


def live_bias(table_ref, slots, page, rows):
    column = lax.broadcasted_iota(jnp.int32, (rows, len(slots) * page), 1)
    bias = jnp.zeros(column.shape, jnp.float32)
    for place, slot in enumerate(slots):
        bias = jnp.where(column // page == place, slot_bias(table_ref, slot), bias)
    return bias


def fill_tables(raws, order, keys_ref, values_ref, heads, page):
    place = 0
    page_rows = page * 2 * heads
    for raw_ref in raws:
        for at in range(0, raw_ref.shape[0], page_rows):
            keys, values = split_page(raw_ref[at : at + page_rows], order, heads)
            keys_ref[place : place + page] = keys
            values_ref[place : place + page] = values
            place += page


def contract_last(a, b):
    return lax.dot_general(a, b, (((1,), (1,)), ((), ())), preferred_element_type=jnp.float32)


def local_body(sizes, owners, *refs):
    heads, group, page, suffix, scale, batch, replicas, wave = sizes
    table_hbm, lens_hbm, q_hbm, own_hbm, suffix_hbm, new_hbm = refs[:6]
    acc_ref, max_ref, part_ref, wide_ref, bias_ref = refs[6:11]
    table_ref, lens_ref, q_ref, own_ref, suffix_ref, new_ref = refs[11:17]
    keys_ref, values_ref, sems = refs[17:]
    kinds = 2 * heads
    row_heads = heads * group
    cached = suffix * kinds
    fresh = batch * kinds
    width = cached + fresh
    batches = q_ref.shape[0] // (batch * row_heads)
    waves = batches // wave
    wave_rows = wave * batch * cached
    pairs = [
        (own_hbm, own_ref),
        (q_hbm, q_ref),
        (new_hbm, new_ref),
        (table_hbm, table_ref),
        (lens_hbm, lens_ref),
    ] + [
        (suffix_hbm.at[pl.ds(i * wave_rows, wave_rows)], suffix_ref.at[pl.ds(i * wave_rows, wave_rows)])
        for i in range(waves)
    ]
    copies = [
        pltpu.make_async_copy(source, target, sems.at[i])
        for i, (source, target) in enumerate(pairs)
    ]
    for copy in copies:
        copy.start()
    me = lax.axis_index("replica")
    slots = own_ref.shape[0] // (page * kinds)
    order = page_order(page * kinds, kinds)
    column = lax.broadcasted_iota(jnp.int32, (row_heads, width), 1)
    head = lax.broadcasted_iota(jnp.int32, (row_heads, width), 0) // group
    never = jnp.int32(1 << 20)
    token = jnp.where(
        (column < cached) & (lax.rem(column, kinds) == head), column // kinds, never
    )
    places = [
        jnp.where(column == cached + i * kinds + head, -1, token) for i in range(batch)
    ]
    for copy in copies[:5]:
        copy.wait()
    fill_tables([own_ref], order, keys_ref, values_ref, heads, page)
    live = live_bias(table_ref, [me * slots + s for s in range(slots)], page, 1)
    bias_ref[...] = live_bias(
        table_ref,
        [owner(me, replicas) * slots + s for owner in owners for s in range(slots)],
        page,
        8,
    )
    keys = keys_ref[...]
    values = values_ref[...]
    block_rows = wave * batch * row_heads
    for turn in range(waves):
        copies[5 + turn].wait()
        rows = pl.ds(turn * block_rows, block_rows)
        q = q_ref[rows]
        q_wide = head_concat(q, heads, group)
        wide_ref[rows] = q_wide
        prefix = contract_last(q_wide, keys) * scale + live
        pieces = []
        scores = []
        for i in range(wave * batch):
            request = turn * wave * batch + i
            kv = jnp.concatenate(
                [
                    suffix_ref[request * cached : (request + 1) * cached],
                    new_ref[request // batch * fresh : (request // batch + 1) * fresh],
                ],
                axis=0,
            )
            pieces.append(kv)
            score = contract_last(q[i * row_heads : (i + 1) * row_heads], kv) * scale
            scores.append(
                jnp.where(places[i % batch] < lens_ref[request], score, masked_score)
            )
        score = jnp.concatenate(scores, axis=0)
        row_max = jnp.max(jnp.maximum(prefix, score), axis=1, keepdims=True)
        weights = jnp.exp2(score - row_max)
        prefix_weights = jnp.exp2(prefix - row_max)
        part_ref[rows] = weights + prefix_weights
        max_ref[rows] = jnp.broadcast_to(row_max, weights.shape)
        rounded = pltpu.roll(weights, heads, 1).astype(jnp.bfloat16)
        wide = jnp.dot(
            prefix_weights.astype(jnp.bfloat16), values, preferred_element_type=jnp.float32
        )
        attended = [
            jnp.dot(
                rounded[i * row_heads : (i + 1) * row_heads],
                pieces[i],
                preferred_element_type=jnp.float32,
            )
            for i in range(wave * batch)
        ]
        acc_ref[rows] = jnp.concatenate(attended, axis=0) + head_select(wide, heads, group)


def early_body(sizes, owners, *refs):
    @pl.when(lax.rem(lax.axis_index("tensor"), 2) == 1)
    def work():
        local_body(sizes, owners, *refs)


def late_body(sizes, owners, *refs):
    inputs, done, others = refs[:6], refs[6:11], refs[11:]
    is_done = lax.rem(lax.axis_index("tensor"), 2) == 1

    @pl.when(is_done)
    def keep():
        for source, target in zip(done, others[:5]):
            target[...] = source[...]

    @pl.when(jnp.logical_not(is_done))
    def work():
        local_body(sizes, owners, *inputs, *others)


def absorb(sizes, rows, wide_ref, acc_ref, max_ref, part_ref, keys, values, live):
    heads, group, scale = sizes
    score = contract_last(wide_ref[rows], keys) * scale + live
    chunks = [score[:, i : i + lanes] for i in range(0, score.shape[1], lanes)]
    top = functools.reduce(jnp.maximum, chunks)
    earlier = max_ref[rows]
    row_max = jnp.maximum(earlier, jnp.max(top, axis=1, keepdims=True))
    weights = [jnp.exp2(chunk - row_max) for chunk in chunks]
    factor = jnp.exp2(earlier - row_max)
    part = part_ref[rows] * factor + functools.reduce(jnp.add, weights)
    rounded = jnp.concatenate([w.astype(jnp.bfloat16) for w in weights], axis=1)
    wide = jnp.dot(rounded, values, preferred_element_type=jnp.float32)
    return acc_ref[rows] * factor + head_select(wide, heads, group), row_max, part


def fold_body(sizes, place, *refs):
    heads, group, page, scale, block_rows, replicas = sizes
    count_in, wide_ref, acc_in, max_in, part_in, bias_ref = refs[:6]
    raws = refs[6:-6]
    count_ref, acc_ref, max_ref, part_ref, keys_ref, values_ref = refs[-6:]
    count_ref[...] = jnp.broadcast_to(count_in[:1, :1], count_ref.shape)
    kinds = 2 * heads
    fill_tables(raws, page_order(page * kinds, kinds), keys_ref, values_ref, heads, page)
    keys = keys_ref[...]
    values = values_ref[...]
    live = bias_ref[:1, place : place + keys.shape[0]]
    for start in range(0, wide_ref.shape[0], block_rows):
        rows = pl.ds(start, block_rows)
        acc_ref[rows], max_ref[rows], part_ref[rows] = absorb(
            (heads, group, scale), rows, wide_ref, acc_in, max_in, part_in, keys, values, live
        )


def finish_body(sizes, place, *refs):
    heads, group, page, scale, block_rows, replicas = sizes
    count_ref, wide_ref, acc_in, max_in, part_in, bias_ref = refs[:6]
    raws = refs[6:-5]
    out_hbm, out_ref, keys_ref, values_ref, sem = refs[-5:]
    kinds = 2 * heads
    fill_tables(raws, page_order(page * kinds, kinds), keys_ref, values_ref, heads, page)
    keys = keys_ref[...]
    values = values_ref[...]
    live = bias_ref[:1, place : place + keys.shape[0]]
    live_rows = count_ref[:1, :] * (heads * group)
    for start in range(0, wide_ref.shape[0], block_rows):
        rows = pl.ds(start, block_rows)
        acc, row_max, part = absorb(
            (heads, group, scale), rows, wide_ref, acc_in, max_in, part_in, keys, values, live
        )
        total = jnp.broadcast_to(jnp.sum(part, axis=1, keepdims=True), part.shape)
        row = start + lax.broadcasted_iota(jnp.int32, part.shape, 0)
        share = jnp.where(row < live_rows, 1.0 / total, 0.0)
        out_ref[rows] = (acc * share).astype(jnp.bfloat16)
    copy = pltpu.make_async_copy(out_ref, out_hbm, sem)
    copy.start()
    copy.wait()


def vmem():
    return pl.BlockSpec(memory_space=pltpu.VMEM)


def hbm():
    return pl.BlockSpec(memory_space=pltpu.HBM)


def folded_ring(replicas):
    return list(range(0, replicas, 2)) + list(range(1, replicas, 2))[::-1]


def ring_step(values, ring, step):
    return lax.ppermute(
        values, "replica", [(ring[i], ring[(i + step) % len(ring)]) for i in range(len(ring))]
    )


def ring_owner(ring, step):
    def owner(me, n):
        found = jnp.int32(ring[-step])
        for i in range(1, len(ring)):
            found = jnp.where(me == ring[i], ring[(i - step) % len(ring)], found)
        return found

    return owner


def gathered_stages(raw, replicas):
    everything = lax.all_gather(raw, "replica", axis=0, tiled=True)
    owners = [lambda me, n, at=at: jnp.where(me == at, -1, at) for at in range(replicas)]
    together = math.gcd(replicas, 4) * raw.shape[0]
    return [
        [everything[i : i + together]] for i in range(0, everything.shape[0], together)
    ], owners


def shards(replicas, queries, prefix_pool, page_table, suffix_kv, new_kv, suffix_len, counts):
    requests, head_count, width = queries.shape
    slots, page, unused, heads, width = prefix_pool.shape
    suffix = suffix_kv.shape[1]
    group = head_count // heads
    kinds = 2 * heads
    scale = width**-0.5 * math.log2(math.e)
    raw = prefix_pool.reshape(slots * page * kinds, width)
    batch = (-suffix * kinds) % lanes // kinds
    wave = requests // batch
    block_rows = 256
    rows = requests * head_count
    block_tokens = slots * page
    two_ways = replicas == 4
    if two_ways:
        ring = folded_ring(replicas)
        ahead = ring_step(raw, ring, 1)
        owners = [ring_owner(ring, step) for step in (1, -1, 2)]
    else:
        stages, owners = gathered_stages(raw, replicas)
    suffix_rows = requests * suffix * kinds
    full = jax.ShapeDtypeStruct((rows, lanes), jnp.float32)
    params = pltpu.CompilerParams(vmem_limit_bytes=24 << 20)

    def cost(tokens):
        return pl.CostEstimate(
            flops=4 * rows * tokens * width, bytes_accessed=3 << 20, transcendentals=rows * tokens
        )

    def tables(tokens):
        return [pltpu.VMEM((tokens, heads * width), jnp.bfloat16)] * 2

    operands = [
        pltpu.with_memory_space_constraint(value, pltpu.HBM)
        for value in (
            page_table,
            suffix_len,
            queries.reshape(rows, width),
            raw,
            suffix_kv.reshape(suffix_rows, width),
            new_kv.reshape(requests * kinds, width),
        )
    ]

    def local_part(body, done):
        return pl.pallas_call(
            functools.partial(
                body, (heads, group, page, suffix, scale, batch, replicas, wave), owners
            ),
            out_shape=[
                full,
                full,
                full,
                jax.ShapeDtypeStruct((rows, heads * width), jnp.bfloat16),
                jax.ShapeDtypeStruct((8, len(owners) * block_tokens), jnp.float32),
            ],
            in_specs=[hbm()] * 6 + [vmem()] * len(done),
            out_specs=[vmem()] * 5,
            scratch_shapes=[
                pltpu.SMEM(page_table.shape, jnp.int32),
                pltpu.SMEM(suffix_len.shape, jnp.int32),
                pltpu.VMEM((rows, width), jnp.bfloat16),
                pltpu.VMEM(raw.shape, jnp.bfloat16),
                pltpu.VMEM((suffix_rows, width), jnp.bfloat16),
                pltpu.VMEM((requests * kinds, width), jnp.bfloat16),
                *tables(block_tokens),
                pltpu.SemaphoreType.DMA((5 + requests // batch // wave,)),
            ],
            compiler_params=params,
            cost_estimate=cost(2 * block_tokens),
            name="local_part",
        )(*operands, *done)

    if two_ways:
        done = list(local_part(early_body, []))
        own, done[4] = lax.optimization_barrier((raw, done[4]))
        back = ring_step(own, ring, -1)
        acc, row_max, part, q_wide, bias = local_part(late_body, done)
        ahead, acc = lax.optimization_barrier((ahead, acc))
        stages = [[ahead, back], [ring_step(ahead, ring, 1)]]
    else:
        acc, row_max, part, q_wide, bias = local_part(local_body, [])
    sizes = (heads, group, page, scale, block_rows, replicas)
    place = 0
    count = jnp.broadcast_to(counts, (8, lanes)) if len(stages) == 1 else counts.reshape(1, 1)
    for blocks in stages[:-1]:
        tokens = sum(block.shape[0] for block in blocks) // kinds
        count, acc, row_max, part = pl.pallas_call(
            functools.partial(fold_body, sizes, place),
            out_shape=[jax.ShapeDtypeStruct((8, lanes), jnp.int32)] + [full] * 3,
            in_specs=[vmem()] * (6 + len(blocks)),
            out_specs=[vmem()] * 4,
            scratch_shapes=tables(tokens),
            compiler_params=params,
            cost_estimate=cost(tokens),
            name="fold_part",
        )(count, q_wide, acc, row_max, part, bias, *blocks)
        place += tokens
    tokens = sum(block.shape[0] for block in stages[-1]) // kinds
    out = pl.pallas_call(
        functools.partial(finish_body, sizes, place),
        out_shape=jax.ShapeDtypeStruct((rows, width), jnp.bfloat16),
        in_specs=[vmem()] * (6 + len(stages[-1])),
        out_specs=hbm(),
        scratch_shapes=[
            pltpu.VMEM((rows, width), jnp.bfloat16),
            *tables(tokens),
            pltpu.SemaphoreType.DMA,
        ],
        compiler_params=params,
        cost_estimate=cost(tokens),
        name="finish_part",
    )(count, q_wide, acc, row_max, part, bias, *stages[-1])
    return out.reshape(requests, head_count, width)


def solution(mesh):
    placed = (
        P(("groups", "replica"), "tensor", None),
        P(("groups", "replica"), None, None, "tensor", None),
        P("groups"),
        P(("groups", "replica"), None, None, "tensor", None),
        P(("groups", "replica"), None, "tensor", None),
        P(("groups", "replica")),
        P(("groups", "replica")),
    )
    return jax.shard_map(
        functools.partial(shards, mesh.shape["replica"]),
        mesh=mesh,
        in_specs=placed,
        out_specs=P(("groups", "replica"), "tensor", None),
        check_vma=False,
    )
```

```python
import functools
import math

import jax
import jax.numpy as jnp
from jax import lax
from jax.experimental import pallas as pl
from jax.experimental.pallas import tpu as pltpu
from jax.sharding import PartitionSpec as P

masked_score = -1e30
lanes = 128


def one_hot(shape, condition):
    row = lax.broadcasted_iota(jnp.int32, shape, 0)
    column = lax.broadcasted_iota(jnp.int32, shape, 1)
    return jnp.where(condition(row, column), 1.0, 0.0).astype(jnp.bfloat16)


def head_concat(grouped, heads, group):
    row = lax.broadcasted_iota(jnp.int32, grouped.shape, 0)
    head = lax.rem(row, heads * group) // group
    values = grouped.astype(jnp.float32)
    parts = [jnp.where(head == g, values, 0.0).astype(jnp.bfloat16) for g in range(heads)]
    return jnp.concatenate(parts, axis=1)


def head_select(wide, heads, group):
    width = wide.shape[1] // heads
    shape = (wide.shape[0], width)
    head = lax.rem(lax.broadcasted_iota(jnp.int32, shape, 0), heads * group) // group
    result = wide[:, :width]
    for g in range(1, heads):
        result = jnp.where(head == g, wide[:, g * width : (g + 1) * width], result)
    return result


def split_page(raw, order, heads):
    sorted_rows = jnp.dot(order, raw, preferred_element_type=jnp.float32).astype(jnp.bfloat16)
    tokens = raw.shape[0] // (2 * heads)
    kinds = [sorted_rows[i * tokens : (i + 1) * tokens] for i in range(2 * heads)]
    return jnp.concatenate(kinds[:heads], axis=1), jnp.concatenate(kinds[heads:], axis=1)


def page_order(page_rows, kinds):
    tokens = page_rows // kinds
    return one_hot(
        (page_rows, page_rows),
        lambda row, column: column == lax.rem(row, tokens) * kinds + row // tokens,
    )


def slot_bias(table_ref, slot):
    size = table_ref.shape[0]

    def look(index, found):
        return jnp.maximum(found, (table_ref[index] == slot).astype(jnp.int32))

    found = lax.fori_loop(0, size, look, jnp.int32(0), unroll=size <= 16)
    return jnp.where(found > 0, 0.0, masked_score)


def live_bias(table_ref, slots, page, rows):
    column = lax.broadcasted_iota(jnp.int32, (rows, len(slots) * page), 1)
    bias = jnp.zeros(column.shape, jnp.float32)
    for place, slot in enumerate(slots):
        bias = jnp.where(column // page == place, slot_bias(table_ref, slot), bias)
    return bias


def fill_tables(raws, order, keys_ref, values_ref, heads, page):
    place = 0
    page_rows = page * 2 * heads
    for raw_ref in raws:
        for at in range(0, raw_ref.shape[0], page_rows):
            keys, values = split_page(raw_ref[at : at + page_rows], order, heads)
            keys_ref[place : place + page] = keys
            values_ref[place : place + page] = values
            place += page


def contract_last(a, b):
    return lax.dot_general(a, b, (((1,), (1,)), ((), ())), preferred_element_type=jnp.float32)


def local_body(sizes, owners, *refs):
    heads, group, page, suffix, scale, batch, replicas, wave = sizes
    table_hbm, lens_hbm, q_hbm, own_hbm, suffix_hbm, new_hbm = refs[:6]
    acc_ref, max_ref, part_ref, wide_ref, bias_ref = refs[6:11]
    table_ref, lens_ref, q_ref, own_ref, suffix_ref, new_ref = refs[11:17]
    keys_ref, values_ref, sems = refs[17:]
    kinds = 2 * heads
    row_heads = heads * group
    cached = suffix * kinds
    fresh = batch * kinds
    width = cached + fresh
    batches = q_ref.shape[0] // (batch * row_heads)
    waves = batches // wave
    wave_rows = wave * batch * cached
    pairs = [
        (own_hbm, own_ref),
        (q_hbm, q_ref),
        (new_hbm, new_ref),
        (table_hbm, table_ref),
        (lens_hbm, lens_ref),
    ] + [
        (suffix_hbm.at[pl.ds(i * wave_rows, wave_rows)], suffix_ref.at[pl.ds(i * wave_rows, wave_rows)])
        for i in range(waves)
    ]
    copies = [
        pltpu.make_async_copy(source, target, sems.at[i])
        for i, (source, target) in enumerate(pairs)
    ]
    for copy in copies:
        copy.start()
    me = lax.axis_index("replica")
    slots = own_ref.shape[0] // (page * kinds)
    order = page_order(page * kinds, kinds)
    column = lax.broadcasted_iota(jnp.int32, (row_heads, width), 1)
    head = lax.broadcasted_iota(jnp.int32, (row_heads, width), 0) // group
    never = jnp.int32(1 << 20)
    token = jnp.where(
        (column < cached) & (lax.rem(column, kinds) == head), column // kinds, never
    )
    places = [
        jnp.where(column == cached + i * kinds + head, -1, token) for i in range(batch)
    ]
    for copy in copies[:5]:
        copy.wait()
    fill_tables([own_ref], order, keys_ref, values_ref, heads, page)
    live = live_bias(table_ref, [me * slots + s for s in range(slots)], page, 1)
    bias_ref[...] = live_bias(
        table_ref,
        [owner(me, replicas) * slots + s for owner in owners for s in range(slots)],
        page,
        8,
    )
    keys = keys_ref[...]
    values = values_ref[...]
    block_rows = wave * batch * row_heads
    for turn in range(waves):
        copies[5 + turn].wait()
        rows = pl.ds(turn * block_rows, block_rows)
        q = q_ref[rows]
        q_wide = head_concat(q, heads, group)
        wide_ref[rows] = q_wide
        prefix = contract_last(q_wide, keys) * scale + live
        pieces = []
        scores = []
        for i in range(wave * batch):
            request = turn * wave * batch + i
            kv = jnp.concatenate(
                [
                    suffix_ref[request * cached : (request + 1) * cached],
                    new_ref[request // batch * fresh : (request // batch + 1) * fresh],
                ],
                axis=0,
            )
            pieces.append(kv)
            score = contract_last(q[i * row_heads : (i + 1) * row_heads], kv) * scale
            scores.append(
                jnp.where(places[i % batch] < lens_ref[request], score, masked_score)
            )
        score = jnp.concatenate(scores, axis=0)
        row_max = jnp.max(jnp.maximum(prefix, score), axis=1, keepdims=True)
        weights = jnp.exp2(score - row_max)
        prefix_weights = jnp.exp2(prefix - row_max)
        part_ref[rows] = weights + prefix_weights
        max_ref[rows] = jnp.broadcast_to(row_max, weights.shape)
        rounded = pltpu.roll(weights, heads, 1).astype(jnp.bfloat16)
        wide = jnp.dot(
            prefix_weights.astype(jnp.bfloat16), values, preferred_element_type=jnp.float32
        )
        attended = [
            jnp.dot(
                rounded[i * row_heads : (i + 1) * row_heads],
                pieces[i],
                preferred_element_type=jnp.float32,
            )
            for i in range(wave * batch)
        ]
        acc_ref[rows] = jnp.concatenate(attended, axis=0) + head_select(wide, heads, group)


def my_turn():
    odd = lax.rem(lax.axis_index("tensor"), 2) == 1
    return jnp.where(odd, 0, jnp.where(lax.axis_index("replica") == 0, 1, 2))


def turn_body(turn, sizes, owners, *refs):
    mine = my_turn()
    inputs, refs = refs[:6], refs[6:]
    if turn > 0:
        done, refs = refs[:5], refs[5:]

        @pl.when(mine < turn)
        def keep():
            for source, target in zip(done, refs[:5]):
                target[...] = source[...]

    @pl.when(mine == turn)
    def work():
        local_body(sizes, owners, *inputs, *refs)


def absorb(sizes, rows, wide_ref, acc_ref, max_ref, part_ref, keys, values, live):
    heads, group, scale = sizes
    score = contract_last(wide_ref[rows], keys) * scale + live
    chunks = [score[:, i : i + lanes] for i in range(0, score.shape[1], lanes)]
    top = functools.reduce(jnp.maximum, chunks)
    earlier = max_ref[rows]
    row_max = jnp.maximum(earlier, jnp.max(top, axis=1, keepdims=True))
    weights = [jnp.exp2(chunk - row_max) for chunk in chunks]
    factor = jnp.exp2(earlier - row_max)
    part = part_ref[rows] * factor + functools.reduce(jnp.add, weights)
    rounded = jnp.concatenate([w.astype(jnp.bfloat16) for w in weights], axis=1)
    wide = jnp.dot(rounded, values, preferred_element_type=jnp.float32)
    return acc_ref[rows] * factor + head_select(wide, heads, group), row_max, part


def fold_body(sizes, place, *refs):
    heads, group, page, scale, block_rows, replicas = sizes
    count_in, wide_ref, acc_in, max_in, part_in, bias_ref = refs[:6]
    raws = refs[6:-6]
    count_ref, acc_ref, max_ref, part_ref, keys_ref, values_ref = refs[-6:]
    count_ref[...] = jnp.broadcast_to(count_in[:1, :1], count_ref.shape)
    kinds = 2 * heads
    fill_tables(raws, page_order(page * kinds, kinds), keys_ref, values_ref, heads, page)
    keys = keys_ref[...]
    values = values_ref[...]
    live = bias_ref[:1, place : place + keys.shape[0]]
    for start in range(0, wide_ref.shape[0], block_rows):
        rows = pl.ds(start, block_rows)
        acc_ref[rows], max_ref[rows], part_ref[rows] = absorb(
            (heads, group, scale), rows, wide_ref, acc_in, max_in, part_in, keys, values, live
        )


def finish_body(sizes, place, *refs):
    heads, group, page, scale, block_rows, replicas = sizes
    count_ref, wide_ref, acc_in, max_in, part_in, bias_ref = refs[:6]
    raws = refs[6:-5]
    out_hbm, out_ref, keys_ref, values_ref, sem = refs[-5:]
    kinds = 2 * heads
    fill_tables(raws, page_order(page * kinds, kinds), keys_ref, values_ref, heads, page)
    keys = keys_ref[...]
    values = values_ref[...]
    live = bias_ref[:1, place : place + keys.shape[0]]
    live_rows = count_ref[:1, :] * (heads * group)
    for start in range(0, wide_ref.shape[0], block_rows):
        rows = pl.ds(start, block_rows)
        acc, row_max, part = absorb(
            (heads, group, scale), rows, wide_ref, acc_in, max_in, part_in, keys, values, live
        )
        total = jnp.broadcast_to(jnp.sum(part, axis=1, keepdims=True), part.shape)
        row = start + lax.broadcasted_iota(jnp.int32, part.shape, 0)
        share = jnp.where(row < live_rows, 1.0 / total, 0.0)
        out_ref[rows] = (acc * share).astype(jnp.bfloat16)
    copy = pltpu.make_async_copy(out_ref, out_hbm, sem)
    copy.start()
    copy.wait()


def vmem():
    return pl.BlockSpec(memory_space=pltpu.VMEM)


def hbm():
    return pl.BlockSpec(memory_space=pltpu.HBM)


def folded_ring(replicas):
    return list(range(0, replicas, 2)) + list(range(1, replicas, 2))[::-1]


def ring_step(values, ring, step):
    return lax.ppermute(
        values, "replica", [(ring[i], ring[(i + step) % len(ring)]) for i in range(len(ring))]
    )


def ring_owner(ring, step):
    def owner(me, n):
        found = jnp.int32(ring[-step])
        for i in range(1, len(ring)):
            found = jnp.where(me == ring[i], ring[(i - step) % len(ring)], found)
        return found

    return owner


def gathered_stages(raw, replicas):
    everything = lax.all_gather(raw, "replica", axis=0, tiled=True)
    owners = [lambda me, n, at=at: jnp.where(me == at, -1, at) for at in range(replicas)]
    together = math.gcd(replicas, 4) * raw.shape[0]
    return [
        [everything[i : i + together]] for i in range(0, everything.shape[0], together)
    ], owners


def shards(replicas, queries, prefix_pool, page_table, suffix_kv, new_kv, suffix_len, counts):
    requests, head_count, width = queries.shape
    slots, page, unused, heads, width = prefix_pool.shape
    suffix = suffix_kv.shape[1]
    group = head_count // heads
    kinds = 2 * heads
    scale = width**-0.5 * math.log2(math.e)
    raw = prefix_pool.reshape(slots * page * kinds, width)
    batch = (-suffix * kinds) % lanes // kinds
    wave = requests // batch
    block_rows = 256
    rows = requests * head_count
    block_tokens = slots * page
    two_ways = replicas == 4
    if two_ways:
        ring = folded_ring(replicas)
        ahead = ring_step(raw, ring, 1)
        owners = [ring_owner(ring, step) for step in (1, -1, 2)]
    else:
        stages, owners = gathered_stages(raw, replicas)
    suffix_rows = requests * suffix * kinds
    full = jax.ShapeDtypeStruct((rows, lanes), jnp.float32)
    params = pltpu.CompilerParams(vmem_limit_bytes=24 << 20)

    def cost(tokens):
        return pl.CostEstimate(
            flops=4 * rows * tokens * width, bytes_accessed=3 << 20, transcendentals=rows * tokens
        )

    def tables(tokens):
        return [pltpu.VMEM((tokens, heads * width), jnp.bfloat16)] * 2

    operands = [
        pltpu.with_memory_space_constraint(value, pltpu.HBM)
        for value in (
            page_table,
            suffix_len,
            queries.reshape(rows, width),
            raw,
            suffix_kv.reshape(suffix_rows, width),
            new_kv.reshape(requests * kinds, width),
        )
    ]

    def local_part(body, done):
        return pl.pallas_call(
            functools.partial(
                body, (heads, group, page, suffix, scale, batch, replicas, wave), owners
            ),
            out_shape=[
                full,
                full,
                full,
                jax.ShapeDtypeStruct((rows, heads * width), jnp.bfloat16),
                jax.ShapeDtypeStruct((8, len(owners) * block_tokens), jnp.float32),
            ],
            in_specs=[hbm()] * 6 + [vmem()] * len(done),
            out_specs=[vmem()] * 5,
            scratch_shapes=[
                pltpu.SMEM(page_table.shape, jnp.int32),
                pltpu.SMEM(suffix_len.shape, jnp.int32),
                pltpu.VMEM((rows, width), jnp.bfloat16),
                pltpu.VMEM(raw.shape, jnp.bfloat16),
                pltpu.VMEM((suffix_rows, width), jnp.bfloat16),
                pltpu.VMEM((requests * kinds, width), jnp.bfloat16),
                *tables(block_tokens),
                pltpu.SemaphoreType.DMA((5 + requests // batch // wave,)),
            ],
            compiler_params=params,
            cost_estimate=cost(2 * block_tokens),
            name="local_part",
        )(*operands, *done)

    if two_ways:
        done = list(local_part(functools.partial(turn_body, 0), []))
        own, done[4] = lax.optimization_barrier((raw, done[4]))
        back = ring_step(own, ring, -1)
        done = list(local_part(functools.partial(turn_body, 1), done))
        ahead, done[4] = lax.optimization_barrier((ahead, done[4]))
        stages = [[ahead, back], [ring_step(ahead, ring, 1)]]
        acc, row_max, part, q_wide, bias = local_part(functools.partial(turn_body, 2), done)
    else:
        acc, row_max, part, q_wide, bias = local_part(local_body, [])
    sizes = (heads, group, page, scale, block_rows, replicas)
    place = 0
    count = jnp.broadcast_to(counts, (8, lanes)) if len(stages) == 1 else counts.reshape(1, 1)
    for blocks in stages[:-1]:
        tokens = sum(block.shape[0] for block in blocks) // kinds
        count, acc, row_max, part = pl.pallas_call(
            functools.partial(fold_body, sizes, place),
            out_shape=[jax.ShapeDtypeStruct((8, lanes), jnp.int32)] + [full] * 3,
            in_specs=[vmem()] * (6 + len(blocks)),
            out_specs=[vmem()] * 4,
            scratch_shapes=tables(tokens),
            compiler_params=params,
            cost_estimate=cost(tokens),
            name="fold_part",
        )(count, q_wide, acc, row_max, part, bias, *blocks)
        place += tokens
    tokens = sum(block.shape[0] for block in stages[-1]) // kinds
    out = pl.pallas_call(
        functools.partial(finish_body, sizes, place),
        out_shape=jax.ShapeDtypeStruct((rows, width), jnp.bfloat16),
        in_specs=[vmem()] * (6 + len(stages[-1])),
        out_specs=hbm(),
        scratch_shapes=[
            pltpu.VMEM((rows, width), jnp.bfloat16),
            *tables(tokens),
            pltpu.SemaphoreType.DMA,
        ],
        compiler_params=params,
        cost_estimate=cost(tokens),
        name="finish_part",
    )(count, q_wide, acc, row_max, part, bias, *stages[-1])
    return out.reshape(requests, head_count, width)


def solution(mesh):
    placed = (
        P(("groups", "replica"), "tensor", None),
        P(("groups", "replica"), None, None, "tensor", None),
        P("groups"),
        P(("groups", "replica"), None, None, "tensor", None),
        P(("groups", "replica"), None, "tensor", None),
        P(("groups", "replica")),
        P(("groups", "replica")),
    )
    return jax.shard_map(
        functools.partial(shards, mesh.shape["replica"]),
        mesh=mesh,
        in_specs=placed,
        out_specs=P(("groups", "replica"), "tensor", None),
        check_vma=False,
    )
```

```python
import functools
import math

import jax
import jax.numpy as jnp
from jax import lax
from jax.experimental import pallas as pl
from jax.experimental.pallas import tpu as pltpu
from jax.sharding import PartitionSpec as P

masked_score = -1e30
lanes = 128


def one_hot(shape, condition):
    row = lax.broadcasted_iota(jnp.int32, shape, 0)
    column = lax.broadcasted_iota(jnp.int32, shape, 1)
    return jnp.where(condition(row, column), 1.0, 0.0).astype(jnp.bfloat16)


def head_concat(grouped, heads, group):
    row = lax.broadcasted_iota(jnp.int32, grouped.shape, 0)
    head = lax.rem(row, heads * group) // group
    values = grouped.astype(jnp.float32)
    parts = [jnp.where(head == g, values, 0.0).astype(jnp.bfloat16) for g in range(heads)]
    return jnp.concatenate(parts, axis=1)


def head_select(wide, heads, group):
    width = wide.shape[1] // heads
    shape = (wide.shape[0], width)
    head = lax.rem(lax.broadcasted_iota(jnp.int32, shape, 0), heads * group) // group
    result = wide[:, :width]
    for g in range(1, heads):
        result = jnp.where(head == g, wide[:, g * width : (g + 1) * width], result)
    return result


def split_page(raw, order, heads):
    sorted_rows = jnp.dot(order, raw, preferred_element_type=jnp.float32).astype(jnp.bfloat16)
    tokens = raw.shape[0] // (2 * heads)
    kinds = [sorted_rows[i * tokens : (i + 1) * tokens] for i in range(2 * heads)]
    return jnp.concatenate(kinds[:heads], axis=1), jnp.concatenate(kinds[heads:], axis=1)


def page_order(page_rows, kinds):
    tokens = page_rows // kinds
    return one_hot(
        (page_rows, page_rows),
        lambda row, column: column == lax.rem(row, tokens) * kinds + row // tokens,
    )


def slot_bias(table_ref, slot):
    size = table_ref.shape[0]

    def look(index, found):
        return jnp.maximum(found, (table_ref[index] == slot).astype(jnp.int32))

    found = lax.fori_loop(0, size, look, jnp.int32(0), unroll=size <= 16)
    return jnp.where(found > 0, 0.0, masked_score)


def live_bias(table_ref, slots, page, rows):
    column = lax.broadcasted_iota(jnp.int32, (rows, len(slots) * page), 1)
    bias = jnp.zeros(column.shape, jnp.float32)
    for place, slot in enumerate(slots):
        bias = jnp.where(column // page == place, slot_bias(table_ref, slot), bias)
    return bias


def fill_tables(raws, order, keys_ref, values_ref, heads, page):
    place = 0
    page_rows = page * 2 * heads
    for raw_ref in raws:
        for at in range(0, raw_ref.shape[0], page_rows):
            keys, values = split_page(raw_ref[at : at + page_rows], order, heads)
            keys_ref[place : place + page] = keys
            values_ref[place : place + page] = values
            place += page


def contract_last(a, b):
    return lax.dot_general(a, b, (((1,), (1,)), ((), ())), preferred_element_type=jnp.float32)


def local_body(sizes, owners, *refs):
    heads, group, page, suffix, scale, batch, replicas, wave = sizes
    table_hbm, lens_hbm, q_hbm, own_hbm, suffix_hbm, new_hbm = refs[:6]
    acc_ref, max_ref, part_ref, wide_ref, bias_ref = refs[6:11]
    table_ref, lens_ref, q_ref, own_ref, suffix_ref, new_ref = refs[11:17]
    keys_ref, values_ref, sems = refs[17:]
    kinds = 2 * heads
    row_heads = heads * group
    cached = suffix * kinds
    fresh = batch * kinds
    width = cached + fresh
    batches = q_ref.shape[0] // (batch * row_heads)
    waves = batches // wave
    wave_rows = wave * batch * cached
    pairs = [
        (own_hbm, own_ref),
        (q_hbm, q_ref),
        (new_hbm, new_ref),
        (table_hbm, table_ref),
        (lens_hbm, lens_ref),
    ] + [
        (suffix_hbm.at[pl.ds(i * wave_rows, wave_rows)], suffix_ref.at[pl.ds(i * wave_rows, wave_rows)])
        for i in range(waves)
    ]
    copies = [
        pltpu.make_async_copy(source, target, sems.at[i])
        for i, (source, target) in enumerate(pairs)
    ]
    for copy in copies:
        copy.start()
    me = lax.axis_index("replica")
    slots = own_ref.shape[0] // (page * kinds)
    order = page_order(page * kinds, kinds)
    column = lax.broadcasted_iota(jnp.int32, (row_heads, width), 1)
    head = lax.broadcasted_iota(jnp.int32, (row_heads, width), 0) // group
    never = jnp.int32(1 << 20)
    token = jnp.where(
        (column < cached) & (lax.rem(column, kinds) == head), column // kinds, never
    )
    places = [
        jnp.where(column == cached + i * kinds + head, -1, token) for i in range(batch)
    ]
    for copy in copies[:5]:
        copy.wait()
    fill_tables([own_ref], order, keys_ref, values_ref, heads, page)
    live = live_bias(table_ref, [me * slots + s for s in range(slots)], page, 1)
    bias_ref[...] = live_bias(
        table_ref,
        [owner(me, replicas) * slots + s for owner in owners for s in range(slots)],
        page,
        8,
    )
    keys = keys_ref[...]
    values = values_ref[...]
    block_rows = wave * batch * row_heads
    for turn in range(waves):
        copies[5 + turn].wait()
        rows = pl.ds(turn * block_rows, block_rows)
        q = q_ref[rows]
        q_wide = head_concat(q, heads, group)
        wide_ref[rows] = q_wide
        prefix = contract_last(q_wide, keys) * scale + live
        pieces = []
        scores = []
        for i in range(wave * batch):
            request = turn * wave * batch + i
            kv = jnp.concatenate(
                [
                    suffix_ref[request * cached : (request + 1) * cached],
                    new_ref[request // batch * fresh : (request // batch + 1) * fresh],
                ],
                axis=0,
            )
            pieces.append(kv)
            score = contract_last(q[i * row_heads : (i + 1) * row_heads], kv) * scale
            scores.append(
                jnp.where(places[i % batch] < lens_ref[request], score, masked_score)
            )
        score = jnp.concatenate(scores, axis=0)
        row_max = jnp.max(jnp.maximum(prefix, score), axis=1, keepdims=True)
        weights = jnp.exp2(score - row_max)
        prefix_weights = jnp.exp2(prefix - row_max)
        part_ref[rows] = weights + prefix_weights
        max_ref[rows] = jnp.broadcast_to(row_max, weights.shape)
        rounded = pltpu.roll(weights, heads, 1).astype(jnp.bfloat16)
        wide = jnp.dot(
            prefix_weights.astype(jnp.bfloat16), values, preferred_element_type=jnp.float32
        )
        attended = [
            jnp.dot(
                rounded[i * row_heads : (i + 1) * row_heads],
                pieces[i],
                preferred_element_type=jnp.float32,
            )
            for i in range(wave * batch)
        ]
        acc_ref[rows] = jnp.concatenate(attended, axis=0) + head_select(wide, heads, group)


def my_turn():
    odd = lax.rem(lax.axis_index("tensor"), 2) == 1
    return jnp.where(odd, 0, jnp.where(lax.axis_index("replica") == 0, 1, 2))


def turn_body(turn, sizes, owners, *refs):
    mine = my_turn()
    inputs, refs = refs[:6], refs[6:]
    if turn > 0:
        done, refs = refs[:5], refs[5:]

        @pl.when(mine < turn)
        def keep():
            for source, target in zip(done, refs[:5]):
                target[...] = source[...]

    @pl.when(mine == turn)
    def work():
        local_body(sizes, owners, *inputs, *refs)


def absorb(sizes, rows, wide_ref, acc_ref, max_ref, part_ref, keys, values, live):
    heads, group, scale = sizes
    score = contract_last(wide_ref[rows], keys) * scale + live
    chunks = [score[:, i : i + lanes] for i in range(0, score.shape[1], lanes)]
    top = functools.reduce(jnp.maximum, chunks)
    earlier = max_ref[rows]
    row_max = jnp.maximum(earlier, jnp.max(top, axis=1, keepdims=True))
    weights = [jnp.exp2(chunk - row_max) for chunk in chunks]
    factor = jnp.exp2(earlier - row_max)
    part = part_ref[rows] * factor + functools.reduce(jnp.add, weights)
    rounded = jnp.concatenate([w.astype(jnp.bfloat16) for w in weights], axis=1)
    wide = jnp.dot(rounded, values, preferred_element_type=jnp.float32)
    return acc_ref[rows] * factor + head_select(wide, heads, group), row_max, part


def fold_body(sizes, place, *refs):
    heads, group, page, scale, block_rows, replicas = sizes
    count_in, wide_ref, acc_in, max_in, part_in, bias_ref = refs[:6]
    raws = refs[6:-6]
    count_ref, acc_ref, max_ref, part_ref, keys_ref, values_ref = refs[-6:]
    count_ref[...] = jnp.broadcast_to(count_in[:1, :1], count_ref.shape)
    kinds = 2 * heads
    fill_tables(raws, page_order(page * kinds, kinds), keys_ref, values_ref, heads, page)
    keys = keys_ref[...]
    values = values_ref[...]
    live = bias_ref[:1, place : place + keys.shape[0]]
    for start in range(0, wide_ref.shape[0], block_rows):
        rows = pl.ds(start, block_rows)
        acc_ref[rows], max_ref[rows], part_ref[rows] = absorb(
            (heads, group, scale), rows, wide_ref, acc_in, max_in, part_in, keys, values, live
        )


def finish_body(sizes, place, *refs):
    heads, group, page, scale, block_rows, replicas = sizes
    count_ref, wide_ref, acc_in, max_in, part_in, bias_ref = refs[:6]
    raws = refs[6:-5]
    out_hbm, out_ref, keys_ref, values_ref, sem = refs[-5:]
    kinds = 2 * heads
    fill_tables(raws, page_order(page * kinds, kinds), keys_ref, values_ref, heads, page)
    keys = keys_ref[...]
    values = values_ref[...]
    live = bias_ref[:1, place : place + keys.shape[0]]
    live_rows = count_ref[:1, :] * (heads * group)
    for start in range(0, wide_ref.shape[0], block_rows):
        rows = pl.ds(start, block_rows)
        acc, row_max, part = absorb(
            (heads, group, scale), rows, wide_ref, acc_in, max_in, part_in, keys, values, live
        )
        total = jnp.broadcast_to(jnp.sum(part, axis=1, keepdims=True), part.shape)
        row = start + lax.broadcasted_iota(jnp.int32, part.shape, 0)
        share = jnp.where(row < live_rows, 1.0 / total, 0.0)
        out_ref[rows] = (acc * share).astype(jnp.bfloat16)
    copy = pltpu.make_async_copy(out_ref, out_hbm, sem)
    copy.start()
    copy.wait()


def vmem():
    return pl.BlockSpec(memory_space=pltpu.VMEM)


def hbm():
    return pl.BlockSpec(memory_space=pltpu.HBM)


def folded_ring(replicas):
    return list(range(0, replicas, 2)) + list(range(1, replicas, 2))[::-1]


def ring_step(values, ring, step):
    return lax.ppermute(
        values, "replica", [(ring[i], ring[(i + step) % len(ring)]) for i in range(len(ring))]
    )


def ring_owner(ring, step):
    def owner(me, n):
        found = jnp.int32(ring[-step])
        for i in range(1, len(ring)):
            found = jnp.where(me == ring[i], ring[(i - step) % len(ring)], found)
        return found

    return owner


def gathered_stages(raw, replicas):
    everything = lax.all_gather(raw, "replica", axis=0, tiled=True)
    owners = [lambda me, n, at=at: jnp.where(me == at, -1, at) for at in range(replicas)]
    together = math.gcd(replicas, 4) * raw.shape[0]
    return [
        [everything[i : i + together]] for i in range(0, everything.shape[0], together)
    ], owners


def shards(replicas, queries, prefix_pool, page_table, suffix_kv, new_kv, suffix_len, counts):
    requests, head_count, width = queries.shape
    slots, page, unused, heads, width = prefix_pool.shape
    suffix = suffix_kv.shape[1]
    group = head_count // heads
    kinds = 2 * heads
    scale = width**-0.5 * math.log2(math.e)
    raw = prefix_pool.reshape(slots * page * kinds, width)
    batch = (-suffix * kinds) % lanes // kinds
    wave = requests // batch
    block_rows = 256
    rows = requests * head_count
    block_tokens = slots * page
    two_ways = replicas == 4
    if two_ways:
        ring = folded_ring(replicas)
        ahead = ring_step(raw, ring, -1)
        owners = [ring_owner(ring, step) for step in (-1, 1, 2)]
    else:
        stages, owners = gathered_stages(raw, replicas)
    suffix_rows = requests * suffix * kinds
    full = jax.ShapeDtypeStruct((rows, lanes), jnp.float32)
    params = pltpu.CompilerParams(vmem_limit_bytes=24 << 20)

    def cost(tokens):
        return pl.CostEstimate(
            flops=4 * rows * tokens * width, bytes_accessed=3 << 20, transcendentals=rows * tokens
        )

    def tables(tokens):
        return [pltpu.VMEM((tokens, heads * width), jnp.bfloat16)] * 2

    operands = [
        pltpu.with_memory_space_constraint(value, pltpu.HBM)
        for value in (
            page_table,
            suffix_len,
            queries.reshape(rows, width),
            raw,
            suffix_kv.reshape(suffix_rows, width),
            new_kv.reshape(requests * kinds, width),
        )
    ]

    def local_part(body, done):
        return pl.pallas_call(
            functools.partial(
                body, (heads, group, page, suffix, scale, batch, replicas, wave), owners
            ),
            out_shape=[
                full,
                full,
                full,
                jax.ShapeDtypeStruct((rows, heads * width), jnp.bfloat16),
                jax.ShapeDtypeStruct((8, len(owners) * block_tokens), jnp.float32),
            ],
            in_specs=[hbm()] * 6 + [vmem()] * len(done),
            out_specs=[vmem()] * 5,
            scratch_shapes=[
                pltpu.SMEM(page_table.shape, jnp.int32),
                pltpu.SMEM(suffix_len.shape, jnp.int32),
                pltpu.VMEM((rows, width), jnp.bfloat16),
                pltpu.VMEM(raw.shape, jnp.bfloat16),
                pltpu.VMEM((suffix_rows, width), jnp.bfloat16),
                pltpu.VMEM((requests * kinds, width), jnp.bfloat16),
                *tables(block_tokens),
                pltpu.SemaphoreType.DMA((5 + requests // batch // wave,)),
            ],
            compiler_params=params,
            cost_estimate=cost(2 * block_tokens),
            name="local_part",
        )(*operands, *done)

    if two_ways:
        done = list(local_part(functools.partial(turn_body, 0), []))
        own, done[4] = lax.optimization_barrier((raw, done[4]))
        back = ring_step(own, ring, 1)
        done = list(local_part(functools.partial(turn_body, 1), done))
        ahead, done[4] = lax.optimization_barrier((ahead, done[4]))
        stages = [[ahead, back], [ring_step(ahead, ring, -1)]]
        acc, row_max, part, q_wide, bias = local_part(functools.partial(turn_body, 2), done)
    else:
        acc, row_max, part, q_wide, bias = local_part(local_body, [])
    sizes = (heads, group, page, scale, block_rows, replicas)
    place = 0
    count = jnp.broadcast_to(counts, (8, lanes)) if len(stages) == 1 else counts.reshape(1, 1)
    for blocks in stages[:-1]:
        tokens = sum(block.shape[0] for block in blocks) // kinds
        count, acc, row_max, part = pl.pallas_call(
            functools.partial(fold_body, sizes, place),
            out_shape=[jax.ShapeDtypeStruct((8, lanes), jnp.int32)] + [full] * 3,
            in_specs=[vmem()] * (6 + len(blocks)),
            out_specs=[vmem()] * 4,
            scratch_shapes=tables(tokens),
            compiler_params=params,
            cost_estimate=cost(tokens),
            name="fold_part",
        )(count, q_wide, acc, row_max, part, bias, *blocks)
        place += tokens
    tokens = sum(block.shape[0] for block in stages[-1]) // kinds
    out = pl.pallas_call(
        functools.partial(finish_body, sizes, place),
        out_shape=jax.ShapeDtypeStruct((rows, width), jnp.bfloat16),
        in_specs=[vmem()] * (6 + len(stages[-1])),
        out_specs=hbm(),
        scratch_shapes=[
            pltpu.VMEM((rows, width), jnp.bfloat16),
            *tables(tokens),
            pltpu.SemaphoreType.DMA,
        ],
        compiler_params=params,
        cost_estimate=cost(tokens),
        name="finish_part",
    )(count, q_wide, acc, row_max, part, bias, *stages[-1])
    return out.reshape(requests, head_count, width)


def solution(mesh):
    placed = (
        P(("groups", "replica"), "tensor", None),
        P(("groups", "replica"), None, None, "tensor", None),
        P("groups"),
        P(("groups", "replica"), None, None, "tensor", None),
        P(("groups", "replica"), None, "tensor", None),
        P(("groups", "replica")),
        P(("groups", "replica")),
    )
    return jax.shard_map(
        functools.partial(shards, mesh.shape["replica"]),
        mesh=mesh,
        in_specs=placed,
        out_specs=P(("groups", "replica"), "tensor", None),
        check_vma=False,
    )
```

```python
import functools
import math

import jax
import jax.numpy as jnp
from jax import lax
from jax.experimental import pallas as pl
from jax.experimental.pallas import tpu as pltpu
from jax.sharding import PartitionSpec as P

masked_score = -1e30
lanes = 128


def one_hot(shape, condition):
    row = lax.broadcasted_iota(jnp.int32, shape, 0)
    column = lax.broadcasted_iota(jnp.int32, shape, 1)
    return jnp.where(condition(row, column), 1.0, 0.0).astype(jnp.bfloat16)


def head_concat(grouped, heads, group):
    row = lax.broadcasted_iota(jnp.int32, grouped.shape, 0)
    head = lax.rem(row, heads * group) // group
    values = grouped.astype(jnp.float32)
    parts = [jnp.where(head == g, values, 0.0).astype(jnp.bfloat16) for g in range(heads)]
    return jnp.concatenate(parts, axis=1)


def head_select(wide, heads, group):
    width = wide.shape[1] // heads
    shape = (wide.shape[0], width)
    head = lax.rem(lax.broadcasted_iota(jnp.int32, shape, 0), heads * group) // group
    result = wide[:, :width]
    for g in range(1, heads):
        result = jnp.where(head == g, wide[:, g * width : (g + 1) * width], result)
    return result


def split_page(raw, order, heads):
    sorted_rows = jnp.dot(order, raw, preferred_element_type=jnp.float32).astype(jnp.bfloat16)
    tokens = raw.shape[0] // (2 * heads)
    kinds = [sorted_rows[i * tokens : (i + 1) * tokens] for i in range(2 * heads)]
    return jnp.concatenate(kinds[:heads], axis=1), jnp.concatenate(kinds[heads:], axis=1)


def page_order(page_rows, kinds):
    tokens = page_rows // kinds
    return one_hot(
        (page_rows, page_rows),
        lambda row, column: column == lax.rem(row, tokens) * kinds + row // tokens,
    )


def slot_bias(table_ref, slot):
    size = table_ref.shape[0]

    def look(index, found):
        return jnp.maximum(found, (table_ref[index] == slot).astype(jnp.int32))

    found = lax.fori_loop(0, size, look, jnp.int32(0), unroll=size <= 16)
    return jnp.where(found > 0, 0.0, masked_score)


def live_bias(table_ref, slots, page, rows):
    column = lax.broadcasted_iota(jnp.int32, (rows, len(slots) * page), 1)
    bias = jnp.zeros(column.shape, jnp.float32)
    for place, slot in enumerate(slots):
        bias = jnp.where(column // page == place, slot_bias(table_ref, slot), bias)
    return bias


def fill_tables(raws, order, keys_ref, values_ref, heads, page):
    place = 0
    page_rows = page * 2 * heads
    for raw_ref in raws:
        for at in range(0, raw_ref.shape[0], page_rows):
            keys, values = split_page(raw_ref[at : at + page_rows], order, heads)
            keys_ref[place : place + page] = keys
            values_ref[place : place + page] = values
            place += page


def contract_last(a, b):
    return lax.dot_general(a, b, (((1,), (1,)), ((), ())), preferred_element_type=jnp.float32)


def local_body(sizes, owners, *refs):
    heads, group, page, suffix, scale, batch, replicas, wave = sizes
    table_hbm, lens_hbm, q_hbm, own_hbm, suffix_hbm, new_hbm = refs[:6]
    acc_ref, max_ref, part_ref, wide_ref, bias_ref = refs[6:11]
    table_ref, lens_ref, q_ref, own_ref, suffix_ref, new_ref = refs[11:17]
    keys_ref, values_ref, sems = refs[17:]
    kinds = 2 * heads
    row_heads = heads * group
    cached = suffix * kinds
    fresh = batch * kinds
    width = cached + fresh
    batches = q_ref.shape[0] // (batch * row_heads)
    waves = batches // wave
    wave_rows = wave * batch * cached
    pairs = [
        (own_hbm, own_ref),
        (q_hbm, q_ref),
        (new_hbm, new_ref),
        (table_hbm, table_ref),
        (lens_hbm, lens_ref),
    ] + [
        (suffix_hbm.at[pl.ds(i * wave_rows, wave_rows)], suffix_ref.at[pl.ds(i * wave_rows, wave_rows)])
        for i in range(waves)
    ]
    copies = [
        pltpu.make_async_copy(source, target, sems.at[i])
        for i, (source, target) in enumerate(pairs)
    ]
    for copy in copies:
        copy.start()
    me = lax.axis_index("replica")
    slots = own_ref.shape[0] // (page * kinds)
    order = page_order(page * kinds, kinds)
    column = lax.broadcasted_iota(jnp.int32, (row_heads, width), 1)
    head = lax.broadcasted_iota(jnp.int32, (row_heads, width), 0) // group
    never = jnp.int32(1 << 20)
    token = jnp.where(
        (column < cached) & (lax.rem(column, kinds) == head), column // kinds, never
    )
    places = [
        jnp.where(column == cached + i * kinds + head, -1, token) for i in range(batch)
    ]
    for copy in copies[:5]:
        copy.wait()
    fill_tables([own_ref], order, keys_ref, values_ref, heads, page)
    live = live_bias(table_ref, [me * slots + s for s in range(slots)], page, 1)
    bias_ref[...] = live_bias(
        table_ref,
        [owner(me, replicas) * slots + s for owner in owners for s in range(slots)],
        page,
        8,
    )
    keys = keys_ref[...]
    values = values_ref[...]
    block_rows = wave * batch * row_heads
    for turn in range(waves):
        copies[5 + turn].wait()
        rows = pl.ds(turn * block_rows, block_rows)
        q = q_ref[rows]
        q_wide = head_concat(q, heads, group)
        wide_ref[rows] = q_wide
        prefix = contract_last(q_wide, keys) * scale + live
        pieces = []
        scores = []
        for i in range(wave * batch):
            request = turn * wave * batch + i
            kv = jnp.concatenate(
                [
                    suffix_ref[request * cached : (request + 1) * cached],
                    new_ref[request // batch * fresh : (request // batch + 1) * fresh],
                ],
                axis=0,
            )
            pieces.append(kv)
            score = contract_last(q[i * row_heads : (i + 1) * row_heads], kv) * scale
            scores.append(
                jnp.where(places[i % batch] < lens_ref[request], score, masked_score)
            )
        score = jnp.concatenate(scores, axis=0)
        row_max = jnp.max(jnp.maximum(prefix, score), axis=1, keepdims=True)
        weights = jnp.exp2(score - row_max)
        prefix_weights = jnp.exp2(prefix - row_max)
        part_ref[rows] = weights + prefix_weights
        max_ref[rows] = jnp.broadcast_to(row_max, weights.shape)
        rounded = pltpu.roll(weights, heads, 1).astype(jnp.bfloat16)
        wide = jnp.dot(
            prefix_weights.astype(jnp.bfloat16), values, preferred_element_type=jnp.float32
        )
        attended = [
            jnp.dot(
                rounded[i * row_heads : (i + 1) * row_heads],
                pieces[i],
                preferred_element_type=jnp.float32,
            )
            for i in range(wave * batch)
        ]
        acc_ref[rows] = jnp.concatenate(attended, axis=0) + head_select(wide, heads, group)


def absorb(sizes, rows, wide_ref, acc_ref, max_ref, part_ref, keys, values, live):
    heads, group, scale = sizes
    score = contract_last(wide_ref[rows], keys) * scale + live
    chunks = [score[:, i : i + lanes] for i in range(0, score.shape[1], lanes)]
    top = functools.reduce(jnp.maximum, chunks)
    earlier = max_ref[rows]
    row_max = jnp.maximum(earlier, jnp.max(top, axis=1, keepdims=True))
    weights = [jnp.exp2(chunk - row_max) for chunk in chunks]
    factor = jnp.exp2(earlier - row_max)
    part = part_ref[rows] * factor + functools.reduce(jnp.add, weights)
    rounded = jnp.concatenate([w.astype(jnp.bfloat16) for w in weights], axis=1)
    wide = jnp.dot(rounded, values, preferred_element_type=jnp.float32)
    return acc_ref[rows] * factor + head_select(wide, heads, group), row_max, part


def fold_body(sizes, place, *refs):
    heads, group, page, scale, block_rows, replicas = sizes
    count_in, wide_ref, acc_in, max_in, part_in, bias_ref = refs[:6]
    raws = refs[6:-6]
    count_ref, acc_ref, max_ref, part_ref, keys_ref, values_ref = refs[-6:]
    count_ref[...] = jnp.broadcast_to(count_in[:1, :1], count_ref.shape)
    kinds = 2 * heads
    fill_tables(raws, page_order(page * kinds, kinds), keys_ref, values_ref, heads, page)
    keys = keys_ref[...]
    values = values_ref[...]
    live = bias_ref[:1, place : place + keys.shape[0]]
    for start in range(0, wide_ref.shape[0], block_rows):
        rows = pl.ds(start, block_rows)
        acc_ref[rows], max_ref[rows], part_ref[rows] = absorb(
            (heads, group, scale), rows, wide_ref, acc_in, max_in, part_in, keys, values, live
        )


def finish_body(sizes, place, *refs):
    heads, group, page, scale, block_rows, replicas = sizes
    count_ref, wide_ref, acc_in, max_in, part_in, bias_ref = refs[:6]
    raws = refs[6:-5]
    out_hbm, out_ref, keys_ref, values_ref, sems = refs[-5:]
    kinds = 2 * heads
    fill_tables(raws, page_order(page * kinds, kinds), keys_ref, values_ref, heads, page)
    keys = keys_ref[...]
    values = values_ref[...]
    live = bias_ref[:1, place : place + keys.shape[0]]
    live_rows = count_ref[:1, :] * (heads * group)
    half = wide_ref.shape[0] // 2
    copies = []
    for start in range(0, wide_ref.shape[0], block_rows):
        rows = pl.ds(start, block_rows)
        acc, row_max, part = absorb(
            (heads, group, scale), rows, wide_ref, acc_in, max_in, part_in, keys, values, live
        )
        total = jnp.broadcast_to(jnp.sum(part, axis=1, keepdims=True), part.shape)
        row = start + lax.broadcasted_iota(jnp.int32, part.shape, 0)
        share = jnp.where(row < live_rows, 1.0 / total, 0.0)
        out_ref[rows] = (acc * share).astype(jnp.bfloat16)
        if (start + block_rows) % half == 0:
            ready = pl.ds(start + block_rows - half, half)
            place = len(copies)
            copies.append(
                pltpu.make_async_copy(out_ref.at[ready], out_hbm.at[ready], sems.at[place])
            )
            copies[-1].start()
    for copy in copies:
        copy.wait()


def vmem():
    return pl.BlockSpec(memory_space=pltpu.VMEM)


def hbm():
    return pl.BlockSpec(memory_space=pltpu.HBM)


def folded_ring(replicas):
    return list(range(0, replicas, 2)) + list(range(1, replicas, 2))[::-1]


def ring_step(values, ring, step):
    return lax.ppermute(
        values, "replica", [(ring[i], ring[(i + step) % len(ring)]) for i in range(len(ring))]
    )


def ring_owner(ring, step):
    def owner(me, n):
        found = jnp.int32(ring[-step])
        for i in range(1, len(ring)):
            found = jnp.where(me == ring[i], ring[(i - step) % len(ring)], found)
        return found

    return owner


def ring_start(raw, replicas):
    ring = folded_ring(replicas)
    owners = [ring_owner(ring, step) for step in (1, -1, 2)]
    return ring_step(raw, ring, 1), ring_step(raw, ring, -1), owners


def ring_finish(ahead, back, replicas, anchor):
    ahead, anchor = lax.optimization_barrier((ahead, anchor))
    return [[ahead, back], [ring_step(ahead, folded_ring(replicas), 1)]], anchor


def gathered_stages(raw, replicas):
    everything = lax.all_gather(raw, "replica", axis=0, tiled=True)
    owners = [lambda me, n, at=at: jnp.where(me == at, -1, at) for at in range(replicas)]
    together = math.gcd(replicas, 4) * raw.shape[0]
    return [
        [everything[i : i + together]] for i in range(0, everything.shape[0], together)
    ], owners


def shards(replicas, queries, prefix_pool, page_table, suffix_kv, new_kv, suffix_len, counts):
    requests, head_count, width = queries.shape
    slots, page, unused, heads, width = prefix_pool.shape
    suffix = suffix_kv.shape[1]
    group = head_count // heads
    kinds = 2 * heads
    scale = width**-0.5 * math.log2(math.e)
    raw = prefix_pool.reshape(slots * page * kinds, width)
    batch = (-suffix * kinds) % lanes // kinds
    wave = requests // batch
    block_rows = 256
    rows = requests * head_count
    block_tokens = slots * page
    two_ways = replicas == 4
    if two_ways:
        ahead, back, owners = ring_start(raw, replicas)
    else:
        stages, owners = gathered_stages(raw, replicas)
    suffix_rows = requests * suffix * kinds
    full = jax.ShapeDtypeStruct((rows, lanes), jnp.float32)
    params = pltpu.CompilerParams(vmem_limit_bytes=24 << 20)

    def cost(tokens):
        return pl.CostEstimate(
            flops=4 * rows * tokens * width, bytes_accessed=3 << 20, transcendentals=rows * tokens
        )

    def tables(tokens):
        return [pltpu.VMEM((tokens, heads * width), jnp.bfloat16)] * 2

    acc, row_max, part, q_wide, bias = pl.pallas_call(
        functools.partial(
            local_body, (heads, group, page, suffix, scale, batch, replicas, wave), owners
        ),
        out_shape=[
            full,
            full,
            full,
            jax.ShapeDtypeStruct((rows, heads * width), jnp.bfloat16),
            jax.ShapeDtypeStruct((8, len(owners) * block_tokens), jnp.float32),
        ],
        in_specs=[hbm()] * 6,
        out_specs=[vmem()] * 5,
        scratch_shapes=[
            pltpu.SMEM(page_table.shape, jnp.int32),
            pltpu.SMEM(suffix_len.shape, jnp.int32),
            pltpu.VMEM((rows, width), jnp.bfloat16),
            pltpu.VMEM(raw.shape, jnp.bfloat16),
            pltpu.VMEM((suffix_rows, width), jnp.bfloat16),
            pltpu.VMEM((requests * kinds, width), jnp.bfloat16),
            *tables(block_tokens),
            pltpu.SemaphoreType.DMA((5 + requests // batch // wave,)),
        ],
        compiler_params=params,
        cost_estimate=cost(2 * block_tokens),
        name="local_part",
    )(
        *[
            pltpu.with_memory_space_constraint(value, pltpu.HBM)
            for value in (
                page_table,
                suffix_len,
                queries.reshape(rows, width),
                raw,
                suffix_kv.reshape(suffix_rows, width),
                new_kv.reshape(requests * kinds, width),
            )
        ]
    )
    if two_ways:
        stages, acc = ring_finish(ahead, back, replicas, acc)
    sizes = (heads, group, page, scale, block_rows, replicas)
    place = 0
    count = jnp.broadcast_to(counts, (8, lanes)) if len(stages) == 1 else counts.reshape(1, 1)
    for blocks in stages[:-1]:
        tokens = sum(block.shape[0] for block in blocks) // kinds
        count, acc, row_max, part = pl.pallas_call(
            functools.partial(fold_body, sizes, place),
            out_shape=[jax.ShapeDtypeStruct((8, lanes), jnp.int32)] + [full] * 3,
            in_specs=[vmem()] * (6 + len(blocks)),
            out_specs=[vmem()] * 4,
            scratch_shapes=tables(tokens),
            compiler_params=params,
            cost_estimate=cost(tokens),
            name="fold_part",
        )(count, q_wide, acc, row_max, part, bias, *blocks)
        place += tokens
    tokens = sum(block.shape[0] for block in stages[-1]) // kinds
    out = pl.pallas_call(
        functools.partial(finish_body, sizes, place),
        out_shape=jax.ShapeDtypeStruct((rows, width), jnp.bfloat16),
        in_specs=[vmem()] * (6 + len(stages[-1])),
        out_specs=hbm(),
        scratch_shapes=[
            pltpu.VMEM((rows, width), jnp.bfloat16),
            *tables(tokens),
            pltpu.SemaphoreType.DMA((2,)),
        ],
        compiler_params=params,
        cost_estimate=cost(tokens),
        name="finish_part",
    )(count, q_wide, acc, row_max, part, bias, *stages[-1])
    return out.reshape(requests, head_count, width)


def solution(mesh):
    placed = (
        P(("groups", "replica"), "tensor", None),
        P(("groups", "replica"), None, None, "tensor", None),
        P("groups"),
        P(("groups", "replica"), None, None, "tensor", None),
        P(("groups", "replica"), None, "tensor", None),
        P(("groups", "replica")),
        P(("groups", "replica")),
    )
    return jax.shard_map(
        functools.partial(shards, mesh.shape["replica"]),
        mesh=mesh,
        in_specs=placed,
        out_specs=P(("groups", "replica"), "tensor", None),
        check_vma=False,
    )
```

```python
import functools
import math

import jax
import jax.numpy as jnp
from jax import lax
from jax.experimental import pallas as pl
from jax.experimental.pallas import tpu as pltpu
from jax.sharding import PartitionSpec as P

masked_score = -1e30
lanes = 128


def one_hot(shape, condition):
    row = lax.broadcasted_iota(jnp.int32, shape, 0)
    column = lax.broadcasted_iota(jnp.int32, shape, 1)
    return jnp.where(condition(row, column), 1.0, 0.0).astype(jnp.bfloat16)


def head_concat(grouped, heads, group):
    row = lax.broadcasted_iota(jnp.int32, grouped.shape, 0)
    head = lax.rem(row, heads * group) // group
    values = grouped.astype(jnp.float32)
    parts = [jnp.where(head == g, values, 0.0).astype(jnp.bfloat16) for g in range(heads)]
    return jnp.concatenate(parts, axis=1)


def head_select(wide, heads, group):
    width = wide.shape[1] // heads
    shape = (wide.shape[0], width)
    head = lax.rem(lax.broadcasted_iota(jnp.int32, shape, 0), heads * group) // group
    result = wide[:, :width]
    for g in range(1, heads):
        result = jnp.where(head == g, wide[:, g * width : (g + 1) * width], result)
    return result


def split_page(raw, order, heads):
    sorted_rows = jnp.dot(order, raw, preferred_element_type=jnp.float32).astype(jnp.bfloat16)
    tokens = raw.shape[0] // (2 * heads)
    kinds = [sorted_rows[i * tokens : (i + 1) * tokens] for i in range(2 * heads)]
    return jnp.concatenate(kinds[:heads], axis=1), jnp.concatenate(kinds[heads:], axis=1)


def page_order(page_rows, kinds):
    tokens = page_rows // kinds
    return one_hot(
        (page_rows, page_rows),
        lambda row, column: column == lax.rem(row, tokens) * kinds + row // tokens,
    )


def slot_bias(table_ref, slot):
    size = table_ref.shape[0]

    def look(index, found):
        return jnp.maximum(found, (table_ref[index] == slot).astype(jnp.int32))

    found = lax.fori_loop(0, size, look, jnp.int32(0), unroll=size <= 16)
    return jnp.where(found > 0, 0.0, masked_score)


def live_bias(table_ref, slots, page, rows):
    column = lax.broadcasted_iota(jnp.int32, (rows, len(slots) * page), 1)
    bias = jnp.zeros(column.shape, jnp.float32)
    for place, slot in enumerate(slots):
        bias = jnp.where(column // page == place, slot_bias(table_ref, slot), bias)
    return bias


def fill_tables(raws, order, keys_ref, values_ref, heads, page):
    place = 0
    page_rows = page * 2 * heads
    for raw_ref in raws:
        for at in range(0, raw_ref.shape[0], page_rows):
            keys, values = split_page(raw_ref[at : at + page_rows], order, heads)
            keys_ref[place : place + page] = keys
            values_ref[place : place + page] = values
            place += page


def contract_last(a, b):
    return lax.dot_general(a, b, (((1,), (1,)), ((), ())), preferred_element_type=jnp.float32)


def local_body(sizes, owners, *refs):
    heads, group, page, suffix, scale, batch, replicas, wave = sizes
    table_hbm, lens_hbm, q_hbm, own_hbm, suffix_hbm, new_hbm = refs[:6]
    acc_ref, max_ref, part_ref, wide_ref, bias_ref = refs[6:11]
    table_ref, lens_ref, q_ref, own_ref, suffix_ref, new_ref = refs[11:17]
    keys_ref, values_ref, sems = refs[17:]
    kinds = 2 * heads
    row_heads = heads * group
    cached = suffix * kinds
    fresh = batch * kinds
    width = cached + fresh
    batches = q_ref.shape[0] // (batch * row_heads)
    waves = batches // wave
    wave_rows = wave * batch * cached
    pairs = [
        (own_hbm, own_ref),
        (q_hbm, q_ref),
        (new_hbm, new_ref),
        (table_hbm, table_ref),
        (lens_hbm, lens_ref),
    ] + [
        (suffix_hbm.at[pl.ds(i * wave_rows, wave_rows)], suffix_ref.at[pl.ds(i * wave_rows, wave_rows)])
        for i in range(waves)
    ]
    copies = [
        pltpu.make_async_copy(source, target, sems.at[i])
        for i, (source, target) in enumerate(pairs)
    ]
    for copy in copies:
        copy.start()
    me = lax.axis_index("replica")
    slots = own_ref.shape[0] // (page * kinds)
    order = page_order(page * kinds, kinds)
    column = lax.broadcasted_iota(jnp.int32, (row_heads, width), 1)
    head = lax.broadcasted_iota(jnp.int32, (row_heads, width), 0) // group
    never = jnp.int32(1 << 20)
    token = jnp.where(
        (column < cached) & (lax.rem(column, kinds) == head), column // kinds, never
    )
    places = [
        jnp.where(column == cached + i * kinds + head, -1, token) for i in range(batch)
    ]
    for copy in copies[:5]:
        copy.wait()
    fill_tables([own_ref], order, keys_ref, values_ref, heads, page)
    live = live_bias(table_ref, [me * slots + s for s in range(slots)], page, 1)
    bias_ref[...] = live_bias(
        table_ref,
        [owner(me, replicas) * slots + s for owner in owners for s in range(slots)],
        page,
        8,
    )
    keys = keys_ref[...]
    values = values_ref[...]
    block_rows = wave * batch * row_heads
    for turn in range(waves):
        copies[5 + turn].wait()
        rows = pl.ds(turn * block_rows, block_rows)
        q = q_ref[rows]
        q_wide = head_concat(q, heads, group)
        wide_ref[rows] = q_wide
        prefix = contract_last(q_wide, keys) * scale + live
        pieces = []
        scores = []
        for i in range(wave * batch):
            request = turn * wave * batch + i
            kv = jnp.concatenate(
                [
                    suffix_ref[request * cached : (request + 1) * cached],
                    new_ref[request // batch * fresh : (request // batch + 1) * fresh],
                ],
                axis=0,
            )
            pieces.append(kv)
            score = contract_last(q[i * row_heads : (i + 1) * row_heads], kv) * scale
            scores.append(
                jnp.where(places[i % batch] < lens_ref[request], score, masked_score)
            )
        score = jnp.concatenate(scores, axis=0)
        row_max = jnp.max(jnp.maximum(prefix, score), axis=1, keepdims=True)
        weights = jnp.exp2(score - row_max)
        prefix_weights = jnp.exp2(prefix - row_max)
        part_ref[rows] = weights + prefix_weights
        max_ref[rows] = jnp.broadcast_to(row_max, weights.shape)
        rounded = pltpu.roll(weights, heads, 1).astype(jnp.bfloat16)
        wide = jnp.dot(
            prefix_weights.astype(jnp.bfloat16), values, preferred_element_type=jnp.float32
        )
        attended = [
            jnp.dot(
                rounded[i * row_heads : (i + 1) * row_heads],
                pieces[i],
                preferred_element_type=jnp.float32,
            )
            for i in range(wave * batch)
        ]
        acc_ref[rows] = jnp.concatenate(attended, axis=0) + head_select(wide, heads, group)


def my_turn():
    odd = lax.rem(lax.axis_index("tensor"), 2) == 1
    replica = lax.axis_index("replica")
    first = lax.rem(replica, 2) == 1
    return jnp.where(
        odd, jnp.where(first, 0, 1), jnp.where(replica == 0, 1, 2)
    )


def turn_body(turn, sizes, owners, *refs):
    mine = my_turn()
    inputs, refs = refs[:6], refs[6:]
    if turn > 0:
        done, refs = refs[:5], refs[5:]

        @pl.when(mine < turn)
        def keep():
            for source, target in zip(done, refs[:5]):
                target[...] = source[...]

    @pl.when(mine == turn)
    def work():
        local_body(sizes, owners, *inputs, *refs)


def absorb(sizes, rows, wide_ref, acc_ref, max_ref, part_ref, keys, values, live):
    heads, group, scale = sizes
    score = contract_last(wide_ref[rows], keys) * scale + live
    chunks = [score[:, i : i + lanes] for i in range(0, score.shape[1], lanes)]
    top = functools.reduce(jnp.maximum, chunks)
    earlier = max_ref[rows]
    row_max = jnp.maximum(earlier, jnp.max(top, axis=1, keepdims=True))
    weights = [jnp.exp2(chunk - row_max) for chunk in chunks]
    factor = jnp.exp2(earlier - row_max)
    part = part_ref[rows] * factor + functools.reduce(jnp.add, weights)
    rounded = jnp.concatenate([w.astype(jnp.bfloat16) for w in weights], axis=1)
    wide = jnp.dot(rounded, values, preferred_element_type=jnp.float32)
    return acc_ref[rows] * factor + head_select(wide, heads, group), row_max, part


def fold_body(sizes, place, *refs):
    heads, group, page, scale, block_rows, replicas = sizes
    count_in, wide_ref, acc_in, max_in, part_in, bias_ref = refs[:6]
    raws = refs[6:-6]
    count_ref, acc_ref, max_ref, part_ref, keys_ref, values_ref = refs[-6:]
    count_ref[...] = jnp.broadcast_to(count_in[:1, :1], count_ref.shape)
    kinds = 2 * heads
    fill_tables(raws, page_order(page * kinds, kinds), keys_ref, values_ref, heads, page)
    keys = keys_ref[...]
    values = values_ref[...]
    live = bias_ref[:1, place : place + keys.shape[0]]
    for start in range(0, wide_ref.shape[0], block_rows):
        rows = pl.ds(start, block_rows)
        acc_ref[rows], max_ref[rows], part_ref[rows] = absorb(
            (heads, group, scale), rows, wide_ref, acc_in, max_in, part_in, keys, values, live
        )


def finish_body(sizes, place, *refs):
    heads, group, page, scale, block_rows, replicas = sizes
    count_ref, wide_ref, acc_in, max_in, part_in, bias_ref = refs[:6]
    raws = refs[6:-5]
    out_hbm, out_ref, keys_ref, values_ref, sem = refs[-5:]
    kinds = 2 * heads
    fill_tables(raws, page_order(page * kinds, kinds), keys_ref, values_ref, heads, page)
    keys = keys_ref[...]
    values = values_ref[...]
    live = bias_ref[:1, place : place + keys.shape[0]]
    live_rows = count_ref[:1, :] * (heads * group)
    for start in range(0, wide_ref.shape[0], block_rows):
        rows = pl.ds(start, block_rows)
        acc, row_max, part = absorb(
            (heads, group, scale), rows, wide_ref, acc_in, max_in, part_in, keys, values, live
        )
        total = jnp.broadcast_to(jnp.sum(part, axis=1, keepdims=True), part.shape)
        row = start + lax.broadcasted_iota(jnp.int32, part.shape, 0)
        share = jnp.where(row < live_rows, 1.0 / total, 0.0)
        out_ref[rows] = (acc * share).astype(jnp.bfloat16)
    copy = pltpu.make_async_copy(out_ref, out_hbm, sem)
    copy.start()
    copy.wait()


def vmem():
    return pl.BlockSpec(memory_space=pltpu.VMEM)


def hbm():
    return pl.BlockSpec(memory_space=pltpu.HBM)


def folded_ring(replicas):
    return list(range(0, replicas, 2)) + list(range(1, replicas, 2))[::-1]


def ring_step(values, ring, step):
    return lax.ppermute(
        values, "replica", [(ring[i], ring[(i + step) % len(ring)]) for i in range(len(ring))]
    )


def ring_owner(ring, step):
    def owner(me, n):
        found = jnp.int32(ring[-step])
        for i in range(1, len(ring)):
            found = jnp.where(me == ring[i], ring[(i - step) % len(ring)], found)
        return found

    return owner


def gathered_stages(raw, replicas):
    everything = lax.all_gather(raw, "replica", axis=0, tiled=True)
    owners = [lambda me, n, at=at: jnp.where(me == at, -1, at) for at in range(replicas)]
    together = math.gcd(replicas, 4) * raw.shape[0]
    return [
        [everything[i : i + together]] for i in range(0, everything.shape[0], together)
    ], owners


def shards(replicas, queries, prefix_pool, page_table, suffix_kv, new_kv, suffix_len, counts):
    requests, head_count, width = queries.shape
    slots, page, unused, heads, width = prefix_pool.shape
    suffix = suffix_kv.shape[1]
    group = head_count // heads
    kinds = 2 * heads
    scale = width**-0.5 * math.log2(math.e)
    raw = prefix_pool.reshape(slots * page * kinds, width)
    batch = (-suffix * kinds) % lanes // kinds
    wave = requests // batch
    block_rows = 256
    rows = requests * head_count
    block_tokens = slots * page
    two_ways = replicas == 4
    if two_ways:
        ring = folded_ring(replicas)
        ahead = ring_step(raw, ring, 1)
        owners = [ring_owner(ring, step) for step in (1, -1, 2)]
    else:
        stages, owners = gathered_stages(raw, replicas)
    suffix_rows = requests * suffix * kinds
    full = jax.ShapeDtypeStruct((rows, lanes), jnp.float32)
    params = pltpu.CompilerParams(vmem_limit_bytes=24 << 20)

    def cost(tokens):
        return pl.CostEstimate(
            flops=4 * rows * tokens * width, bytes_accessed=3 << 20, transcendentals=rows * tokens
        )

    def tables(tokens):
        return [pltpu.VMEM((tokens, heads * width), jnp.bfloat16)] * 2

    operands = [
        pltpu.with_memory_space_constraint(value, pltpu.HBM)
        for value in (
            page_table,
            suffix_len,
            queries.reshape(rows, width),
            raw,
            suffix_kv.reshape(suffix_rows, width),
            new_kv.reshape(requests * kinds, width),
        )
    ]

    def local_part(body, done):
        return pl.pallas_call(
            functools.partial(
                body, (heads, group, page, suffix, scale, batch, replicas, wave), owners
            ),
            out_shape=[
                full,
                full,
                full,
                jax.ShapeDtypeStruct((rows, heads * width), jnp.bfloat16),
                jax.ShapeDtypeStruct((8, len(owners) * block_tokens), jnp.float32),
            ],
            in_specs=[hbm()] * 6 + [vmem()] * len(done),
            out_specs=[vmem()] * 5,
            scratch_shapes=[
                pltpu.SMEM(page_table.shape, jnp.int32),
                pltpu.SMEM(suffix_len.shape, jnp.int32),
                pltpu.VMEM((rows, width), jnp.bfloat16),
                pltpu.VMEM(raw.shape, jnp.bfloat16),
                pltpu.VMEM((suffix_rows, width), jnp.bfloat16),
                pltpu.VMEM((requests * kinds, width), jnp.bfloat16),
                *tables(block_tokens),
                pltpu.SemaphoreType.DMA((5 + requests // batch // wave,)),
            ],
            compiler_params=params,
            cost_estimate=cost(2 * block_tokens),
            name="local_part",
        )(*operands, *done)

    if two_ways:
        done = list(local_part(functools.partial(turn_body, 0), []))
        own, done[4] = lax.optimization_barrier((raw, done[4]))
        back = ring_step(own, ring, -1)
        done = list(local_part(functools.partial(turn_body, 1), done))
        ahead, done[4] = lax.optimization_barrier((ahead, done[4]))
        stages = [[ahead, back], [ring_step(ahead, ring, 1)]]
        acc, row_max, part, q_wide, bias = local_part(functools.partial(turn_body, 2), done)
    else:
        acc, row_max, part, q_wide, bias = local_part(local_body, [])
    sizes = (heads, group, page, scale, block_rows, replicas)
    place = 0
    count = jnp.broadcast_to(counts, (8, lanes)) if len(stages) == 1 else counts.reshape(1, 1)
    for blocks in stages[:-1]:
        tokens = sum(block.shape[0] for block in blocks) // kinds
        count, acc, row_max, part = pl.pallas_call(
            functools.partial(fold_body, sizes, place),
            out_shape=[jax.ShapeDtypeStruct((8, lanes), jnp.int32)] + [full] * 3,
            in_specs=[vmem()] * (6 + len(blocks)),
            out_specs=[vmem()] * 4,
            scratch_shapes=tables(tokens),
            compiler_params=params,
            cost_estimate=cost(tokens),
            name="fold_part",
        )(count, q_wide, acc, row_max, part, bias, *blocks)
        place += tokens
    tokens = sum(block.shape[0] for block in stages[-1]) // kinds
    out = pl.pallas_call(
        functools.partial(finish_body, sizes, place),
        out_shape=jax.ShapeDtypeStruct((rows, width), jnp.bfloat16),
        in_specs=[vmem()] * (6 + len(stages[-1])),
        out_specs=hbm(),
        scratch_shapes=[
            pltpu.VMEM((rows, width), jnp.bfloat16),
            *tables(tokens),
            pltpu.SemaphoreType.DMA,
        ],
        compiler_params=params,
        cost_estimate=cost(tokens),
        name="finish_part",
    )(count, q_wide, acc, row_max, part, bias, *stages[-1])
    return out.reshape(requests, head_count, width)


def solution(mesh):
    placed = (
        P(("groups", "replica"), "tensor", None),
        P(("groups", "replica"), None, None, "tensor", None),
        P("groups"),
        P(("groups", "replica"), None, None, "tensor", None),
        P(("groups", "replica"), None, "tensor", None),
        P(("groups", "replica")),
        P(("groups", "replica")),
    )
    return jax.shard_map(
        functools.partial(shards, mesh.shape["replica"]),
        mesh=mesh,
        in_specs=placed,
        out_specs=P(("groups", "replica"), "tensor", None),
        check_vma=False,
    )
```

```python
import functools
import math

import jax
import jax.numpy as jnp
from jax import lax
from jax.experimental import pallas as pl
from jax.experimental.pallas import tpu as pltpu
from jax.sharding import PartitionSpec as P

masked_score = -1e30
lanes = 128


def one_hot(shape, condition):
    row = lax.broadcasted_iota(jnp.int32, shape, 0)
    column = lax.broadcasted_iota(jnp.int32, shape, 1)
    return jnp.where(condition(row, column), 1.0, 0.0).astype(jnp.bfloat16)


def head_concat(grouped, heads, group):
    row = lax.broadcasted_iota(jnp.int32, grouped.shape, 0)
    head = lax.rem(row, heads * group) // group
    values = grouped.astype(jnp.float32)
    parts = [jnp.where(head == g, values, 0.0).astype(jnp.bfloat16) for g in range(heads)]
    return jnp.concatenate(parts, axis=1)


def head_select(wide, heads, group):
    width = wide.shape[1] // heads
    shape = (wide.shape[0], width)
    head = lax.rem(lax.broadcasted_iota(jnp.int32, shape, 0), heads * group) // group
    result = wide[:, :width]
    for g in range(1, heads):
        result = jnp.where(head == g, wide[:, g * width : (g + 1) * width], result)
    return result


def split_page(raw, order, heads):
    sorted_rows = jnp.dot(order, raw, preferred_element_type=jnp.float32).astype(jnp.bfloat16)
    tokens = raw.shape[0] // (2 * heads)
    kinds = [sorted_rows[i * tokens : (i + 1) * tokens] for i in range(2 * heads)]
    return jnp.concatenate(kinds[:heads], axis=1), jnp.concatenate(kinds[heads:], axis=1)


def page_order(page_rows, kinds):
    tokens = page_rows // kinds
    return one_hot(
        (page_rows, page_rows),
        lambda row, column: column == lax.rem(row, tokens) * kinds + row // tokens,
    )


def slot_bias(table_ref, slot):
    size = table_ref.shape[0]

    def look(index, found):
        return jnp.maximum(found, (table_ref[index] == slot).astype(jnp.int32))

    found = lax.fori_loop(0, size, look, jnp.int32(0), unroll=size <= 16)
    return jnp.where(found > 0, 0.0, masked_score)


def live_bias(table_ref, slots, page, rows):
    column = lax.broadcasted_iota(jnp.int32, (rows, len(slots) * page), 1)
    bias = jnp.zeros(column.shape, jnp.float32)
    for place, slot in enumerate(slots):
        bias = jnp.where(column // page == place, slot_bias(table_ref, slot), bias)
    return bias


def fill_tables(raws, order, keys_ref, values_ref, heads, page):
    place = 0
    page_rows = page * 2 * heads
    for raw_ref in raws:
        for at in range(0, raw_ref.shape[0], page_rows):
            keys, values = split_page(raw_ref[at : at + page_rows], order, heads)
            keys_ref[place : place + page] = keys
            values_ref[place : place + page] = values
            place += page


def contract_last(a, b):
    return lax.dot_general(a, b, (((1,), (1,)), ((), ())), preferred_element_type=jnp.float32)


def local_body(sizes, owners, *refs):
    heads, group, page, suffix, scale, batch, replicas, wave = sizes
    table_hbm, lens_hbm, q_hbm, own_hbm, suffix_hbm, new_hbm = refs[:6]
    acc_ref, max_ref, part_ref, wide_ref, bias_ref = refs[6:11]
    table_ref, lens_ref, q_ref, own_ref, suffix_ref, new_ref = refs[11:17]
    keys_ref, values_ref, sems = refs[17:]
    kinds = 2 * heads
    row_heads = heads * group
    cached = suffix * kinds
    fresh = batch * kinds
    width = cached + fresh
    batches = q_ref.shape[0] // (batch * row_heads)
    waves = batches // wave
    wave_rows = wave * batch * cached
    pairs = [
        (own_hbm, own_ref),
        (q_hbm, q_ref),
        (new_hbm, new_ref),
        (table_hbm, table_ref),
        (lens_hbm, lens_ref),
    ] + [
        (suffix_hbm.at[pl.ds(i * wave_rows, wave_rows)], suffix_ref.at[pl.ds(i * wave_rows, wave_rows)])
        for i in range(waves)
    ]
    copies = [
        pltpu.make_async_copy(source, target, sems.at[i])
        for i, (source, target) in enumerate(pairs)
    ]
    for copy in copies:
        copy.start()
    me = lax.axis_index("replica")
    slots = own_ref.shape[0] // (page * kinds)
    order = page_order(page * kinds, kinds)
    column = lax.broadcasted_iota(jnp.int32, (row_heads, width), 1)
    head = lax.broadcasted_iota(jnp.int32, (row_heads, width), 0) // group
    never = jnp.int32(1 << 20)
    token = jnp.where(
        (column < cached) & (lax.rem(column, kinds) == head), column // kinds, never
    )
    places = [
        jnp.where(column == cached + i * kinds + head, -1, token) for i in range(batch)
    ]
    for copy in copies[:5]:
        copy.wait()
    fill_tables([own_ref], order, keys_ref, values_ref, heads, page)
    live = live_bias(table_ref, [me * slots + s for s in range(slots)], page, 1)
    bias_ref[...] = live_bias(
        table_ref,
        [owner(me, replicas) * slots + s for owner in owners for s in range(slots)],
        page,
        8,
    )
    keys = keys_ref[...]
    values = values_ref[...]
    block_rows = wave * batch * row_heads
    for turn in range(waves):
        copies[5 + turn].wait()
        rows = pl.ds(turn * block_rows, block_rows)
        q = q_ref[rows]
        q_wide = head_concat(q, heads, group)
        wide_ref[rows] = q_wide
        prefix = contract_last(q_wide, keys) * scale + live
        pieces = []
        scores = []
        for i in range(wave * batch):
            request = turn * wave * batch + i
            kv = jnp.concatenate(
                [
                    suffix_ref[request * cached : (request + 1) * cached],
                    new_ref[request // batch * fresh : (request // batch + 1) * fresh],
                ],
                axis=0,
            )
            pieces.append(kv)
            score = contract_last(q[i * row_heads : (i + 1) * row_heads], kv) * scale
            scores.append(
                jnp.where(places[i % batch] < lens_ref[request], score, masked_score)
            )
        score = jnp.concatenate(scores, axis=0)
        row_max = jnp.max(jnp.maximum(prefix, score), axis=1, keepdims=True)
        weights = jnp.exp2(score - row_max)
        prefix_weights = jnp.exp2(prefix - row_max)
        part_ref[rows] = weights + prefix_weights
        max_ref[rows] = jnp.broadcast_to(row_max, weights.shape)
        rounded = pltpu.roll(weights, heads, 1).astype(jnp.bfloat16)
        wide = jnp.dot(
            prefix_weights.astype(jnp.bfloat16), values, preferred_element_type=jnp.float32
        )
        attended = [
            jnp.dot(
                rounded[i * row_heads : (i + 1) * row_heads],
                pieces[i],
                preferred_element_type=jnp.float32,
            )
            for i in range(wave * batch)
        ]
        acc_ref[rows] = jnp.concatenate(attended, axis=0) + head_select(wide, heads, group)


def my_turn():
    odd = lax.rem(lax.axis_index("tensor"), 2) == 1
    replica = lax.axis_index("replica")
    first = lax.rem(replica, 2) == 1
    return jnp.where(
        odd, jnp.where(first, 0, 2), jnp.where(replica == 0, 1, 2)
    )


def turn_body(turn, sizes, owners, *refs):
    mine = my_turn()
    inputs, refs = refs[:6], refs[6:]
    if turn > 0:
        done, refs = refs[:5], refs[5:]

        @pl.when(mine < turn)
        def keep():
            for source, target in zip(done, refs[:5]):
                target[...] = source[...]

    @pl.when(mine == turn)
    def work():
        local_body(sizes, owners, *inputs, *refs)


def absorb(sizes, rows, wide_ref, acc_ref, max_ref, part_ref, keys, values, live):
    heads, group, scale = sizes
    score = contract_last(wide_ref[rows], keys) * scale + live
    chunks = [score[:, i : i + lanes] for i in range(0, score.shape[1], lanes)]
    top = functools.reduce(jnp.maximum, chunks)
    earlier = max_ref[rows]
    row_max = jnp.maximum(earlier, jnp.max(top, axis=1, keepdims=True))
    weights = [jnp.exp2(chunk - row_max) for chunk in chunks]
    factor = jnp.exp2(earlier - row_max)
    part = part_ref[rows] * factor + functools.reduce(jnp.add, weights)
    rounded = jnp.concatenate([w.astype(jnp.bfloat16) for w in weights], axis=1)
    wide = jnp.dot(rounded, values, preferred_element_type=jnp.float32)
    return acc_ref[rows] * factor + head_select(wide, heads, group), row_max, part


def fold_body(sizes, place, *refs):
    heads, group, page, scale, block_rows, replicas = sizes
    count_in, wide_ref, acc_in, max_in, part_in, bias_ref = refs[:6]
    raws = refs[6:-6]
    count_ref, acc_ref, max_ref, part_ref, keys_ref, values_ref = refs[-6:]
    count_ref[...] = jnp.broadcast_to(count_in[:1, :1], count_ref.shape)
    kinds = 2 * heads
    fill_tables(raws, page_order(page * kinds, kinds), keys_ref, values_ref, heads, page)
    keys = keys_ref[...]
    values = values_ref[...]
    live = bias_ref[:1, place : place + keys.shape[0]]
    for start in range(0, wide_ref.shape[0], block_rows):
        rows = pl.ds(start, block_rows)
        acc_ref[rows], max_ref[rows], part_ref[rows] = absorb(
            (heads, group, scale), rows, wide_ref, acc_in, max_in, part_in, keys, values, live
        )


def finish_body(sizes, place, *refs):
    heads, group, page, scale, block_rows, replicas = sizes
    count_ref, wide_ref, acc_in, max_in, part_in, bias_ref = refs[:6]
    raws = refs[6:-5]
    out_hbm, out_ref, keys_ref, values_ref, sem = refs[-5:]
    kinds = 2 * heads
    fill_tables(raws, page_order(page * kinds, kinds), keys_ref, values_ref, heads, page)
    keys = keys_ref[...]
    values = values_ref[...]
    live = bias_ref[:1, place : place + keys.shape[0]]
    live_rows = count_ref[:1, :] * (heads * group)
    for start in range(0, wide_ref.shape[0], block_rows):
        rows = pl.ds(start, block_rows)
        acc, row_max, part = absorb(
            (heads, group, scale), rows, wide_ref, acc_in, max_in, part_in, keys, values, live
        )
        total = jnp.broadcast_to(jnp.sum(part, axis=1, keepdims=True), part.shape)
        row = start + lax.broadcasted_iota(jnp.int32, part.shape, 0)
        share = jnp.where(row < live_rows, 1.0 / total, 0.0)
        out_ref[rows] = (acc * share).astype(jnp.bfloat16)
    copy = pltpu.make_async_copy(out_ref, out_hbm, sem)
    copy.start()
    copy.wait()


def vmem():
    return pl.BlockSpec(memory_space=pltpu.VMEM)


def hbm():
    return pl.BlockSpec(memory_space=pltpu.HBM)


def folded_ring(replicas):
    return list(range(0, replicas, 2)) + list(range(1, replicas, 2))[::-1]


def ring_step(values, ring, step):
    return lax.ppermute(
        values, "replica", [(ring[i], ring[(i + step) % len(ring)]) for i in range(len(ring))]
    )


def ring_owner(ring, step):
    def owner(me, n):
        found = jnp.int32(ring[-step])
        for i in range(1, len(ring)):
            found = jnp.where(me == ring[i], ring[(i - step) % len(ring)], found)
        return found

    return owner


def gathered_stages(raw, replicas):
    everything = lax.all_gather(raw, "replica", axis=0, tiled=True)
    owners = [lambda me, n, at=at: jnp.where(me == at, -1, at) for at in range(replicas)]
    together = math.gcd(replicas, 4) * raw.shape[0]
    return [
        [everything[i : i + together]] for i in range(0, everything.shape[0], together)
    ], owners


def shards(replicas, queries, prefix_pool, page_table, suffix_kv, new_kv, suffix_len, counts):
    requests, head_count, width = queries.shape
    slots, page, unused, heads, width = prefix_pool.shape
    suffix = suffix_kv.shape[1]
    group = head_count // heads
    kinds = 2 * heads
    scale = width**-0.5 * math.log2(math.e)
    raw = prefix_pool.reshape(slots * page * kinds, width)
    batch = (-suffix * kinds) % lanes // kinds
    wave = requests // batch
    block_rows = 256
    rows = requests * head_count
    block_tokens = slots * page
    two_ways = replicas == 4
    if two_ways:
        ring = folded_ring(replicas)
        ahead = ring_step(raw, ring, 1)
        owners = [ring_owner(ring, step) for step in (1, -1, 2)]
    else:
        stages, owners = gathered_stages(raw, replicas)
    suffix_rows = requests * suffix * kinds
    full = jax.ShapeDtypeStruct((rows, lanes), jnp.float32)
    params = pltpu.CompilerParams(vmem_limit_bytes=24 << 20)

    def cost(tokens):
        return pl.CostEstimate(
            flops=4 * rows * tokens * width, bytes_accessed=3 << 20, transcendentals=rows * tokens
        )

    def tables(tokens):
        return [pltpu.VMEM((tokens, heads * width), jnp.bfloat16)] * 2

    operands = [
        pltpu.with_memory_space_constraint(value, pltpu.HBM)
        for value in (
            page_table,
            suffix_len,
            queries.reshape(rows, width),
            raw,
            suffix_kv.reshape(suffix_rows, width),
            new_kv.reshape(requests * kinds, width),
        )
    ]

    def local_part(body, done):
        return pl.pallas_call(
            functools.partial(
                body, (heads, group, page, suffix, scale, batch, replicas, wave), owners
            ),
            out_shape=[
                full,
                full,
                full,
                jax.ShapeDtypeStruct((rows, heads * width), jnp.bfloat16),
                jax.ShapeDtypeStruct((8, len(owners) * block_tokens), jnp.float32),
            ],
            in_specs=[hbm()] * 6 + [vmem()] * len(done),
            out_specs=[vmem()] * 5,
            scratch_shapes=[
                pltpu.SMEM(page_table.shape, jnp.int32),
                pltpu.SMEM(suffix_len.shape, jnp.int32),
                pltpu.VMEM((rows, width), jnp.bfloat16),
                pltpu.VMEM(raw.shape, jnp.bfloat16),
                pltpu.VMEM((suffix_rows, width), jnp.bfloat16),
                pltpu.VMEM((requests * kinds, width), jnp.bfloat16),
                *tables(block_tokens),
                pltpu.SemaphoreType.DMA((5 + requests // batch // wave,)),
            ],
            compiler_params=params,
            cost_estimate=cost(2 * block_tokens),
            name="local_part",
        )(*operands, *done)

    if two_ways:
        done = list(local_part(functools.partial(turn_body, 0), []))
        own, done[4] = lax.optimization_barrier((raw, done[4]))
        back = ring_step(own, ring, -1)
        done = list(local_part(functools.partial(turn_body, 1), done))
        ahead, done[4] = lax.optimization_barrier((ahead, done[4]))
        stages = [[ahead, back], [ring_step(ahead, ring, 1)]]
        acc, row_max, part, q_wide, bias = local_part(functools.partial(turn_body, 2), done)
    else:
        acc, row_max, part, q_wide, bias = local_part(local_body, [])
    sizes = (heads, group, page, scale, block_rows, replicas)
    place = 0
    count = jnp.broadcast_to(counts, (8, lanes)) if len(stages) == 1 else counts.reshape(1, 1)
    for blocks in stages[:-1]:
        tokens = sum(block.shape[0] for block in blocks) // kinds
        count, acc, row_max, part = pl.pallas_call(
            functools.partial(fold_body, sizes, place),
            out_shape=[jax.ShapeDtypeStruct((8, lanes), jnp.int32)] + [full] * 3,
            in_specs=[vmem()] * (6 + len(blocks)),
            out_specs=[vmem()] * 4,
            scratch_shapes=tables(tokens),
            compiler_params=params,
            cost_estimate=cost(tokens),
            name="fold_part",
        )(count, q_wide, acc, row_max, part, bias, *blocks)
        place += tokens
    tokens = sum(block.shape[0] for block in stages[-1]) // kinds
    out = pl.pallas_call(
        functools.partial(finish_body, sizes, place),
        out_shape=jax.ShapeDtypeStruct((rows, width), jnp.bfloat16),
        in_specs=[vmem()] * (6 + len(stages[-1])),
        out_specs=hbm(),
        scratch_shapes=[
            pltpu.VMEM((rows, width), jnp.bfloat16),
            *tables(tokens),
            pltpu.SemaphoreType.DMA,
        ],
        compiler_params=params,
        cost_estimate=cost(tokens),
        name="finish_part",
    )(count, q_wide, acc, row_max, part, bias, *stages[-1])
    return out.reshape(requests, head_count, width)


def solution(mesh):
    placed = (
        P(("groups", "replica"), "tensor", None),
        P(("groups", "replica"), None, None, "tensor", None),
        P("groups"),
        P(("groups", "replica"), None, None, "tensor", None),
        P(("groups", "replica"), None, "tensor", None),
        P(("groups", "replica")),
        P(("groups", "replica")),
    )
    return jax.shard_map(
        functools.partial(shards, mesh.shape["replica"]),
        mesh=mesh,
        in_specs=placed,
        out_specs=P(("groups", "replica"), "tensor", None),
        check_vma=False,
    )
```

```python
import functools
import math

import jax
import jax.numpy as jnp
from jax import lax
from jax.experimental import pallas as pl
from jax.experimental.pallas import tpu as pltpu
from jax.sharding import PartitionSpec as P

masked_score = -1e30
lanes = 128


def one_hot(shape, condition):
    row = lax.broadcasted_iota(jnp.int32, shape, 0)
    column = lax.broadcasted_iota(jnp.int32, shape, 1)
    return jnp.where(condition(row, column), 1.0, 0.0).astype(jnp.bfloat16)


def head_concat(grouped, heads, group):
    row = lax.broadcasted_iota(jnp.int32, grouped.shape, 0)
    head = lax.rem(row, heads * group) // group
    values = grouped.astype(jnp.float32)
    parts = [jnp.where(head == g, values, 0.0).astype(jnp.bfloat16) for g in range(heads)]
    return jnp.concatenate(parts, axis=1)


def head_select(wide, heads, group):
    width = wide.shape[1] // heads
    shape = (wide.shape[0], width)
    head = lax.rem(lax.broadcasted_iota(jnp.int32, shape, 0), heads * group) // group
    result = wide[:, :width]
    for g in range(1, heads):
        result = jnp.where(head == g, wide[:, g * width : (g + 1) * width], result)
    return result


def split_page(raw, order, heads):
    sorted_rows = jnp.dot(order, raw, preferred_element_type=jnp.float32).astype(jnp.bfloat16)
    tokens = raw.shape[0] // (2 * heads)
    kinds = [sorted_rows[i * tokens : (i + 1) * tokens] for i in range(2 * heads)]
    return jnp.concatenate(kinds[:heads], axis=1), jnp.concatenate(kinds[heads:], axis=1)


def page_order(page_rows, kinds):
    tokens = page_rows // kinds
    return one_hot(
        (page_rows, page_rows),
        lambda row, column: column == lax.rem(row, tokens) * kinds + row // tokens,
    )


def slot_bias(table_ref, slot):
    size = table_ref.shape[0]

    def look(index, found):
        return jnp.maximum(found, (table_ref[index] == slot).astype(jnp.int32))

    found = lax.fori_loop(0, size, look, jnp.int32(0), unroll=size <= 16)
    return jnp.where(found > 0, 0.0, masked_score)


def live_bias(table_ref, slots, page, rows):
    column = lax.broadcasted_iota(jnp.int32, (rows, len(slots) * page), 1)
    bias = jnp.zeros(column.shape, jnp.float32)
    for place, slot in enumerate(slots):
        bias = jnp.where(column // page == place, slot_bias(table_ref, slot), bias)
    return bias


def fill_tables(raws, order, keys_ref, values_ref, heads, page):
    place = 0
    page_rows = page * 2 * heads
    for raw_ref in raws:
        for at in range(0, raw_ref.shape[0], page_rows):
            keys, values = split_page(raw_ref[at : at + page_rows], order, heads)
            keys_ref[place : place + page] = keys
            values_ref[place : place + page] = values
            place += page


def contract_last(a, b):
    return lax.dot_general(a, b, (((1,), (1,)), ((), ())), preferred_element_type=jnp.float32)


def local_body(sizes, owners, *refs):
    heads, group, page, suffix, scale, batch, replicas, wave = sizes
    table_hbm, lens_hbm, q_hbm, own_hbm, suffix_hbm, new_hbm = refs[:6]
    acc_ref, max_ref, part_ref, wide_ref, bias_ref = refs[6:11]
    table_ref, lens_ref, q_ref, own_ref, suffix_ref, new_ref = refs[11:17]
    keys_ref, values_ref, sems = refs[17:]
    kinds = 2 * heads
    row_heads = heads * group
    cached = suffix * kinds
    fresh = batch * kinds
    width = cached + fresh
    batches = q_ref.shape[0] // (batch * row_heads)
    waves = batches // wave
    wave_rows = wave * batch * cached
    pairs = [
        (own_hbm, own_ref),
        (q_hbm, q_ref),
        (new_hbm, new_ref),
        (table_hbm, table_ref),
        (lens_hbm, lens_ref),
    ] + [
        (suffix_hbm.at[pl.ds(i * wave_rows, wave_rows)], suffix_ref.at[pl.ds(i * wave_rows, wave_rows)])
        for i in range(waves)
    ]
    copies = [
        pltpu.make_async_copy(source, target, sems.at[i])
        for i, (source, target) in enumerate(pairs)
    ]
    for copy in copies:
        copy.start()
    me = lax.axis_index("replica")
    slots = own_ref.shape[0] // (page * kinds)
    order = page_order(page * kinds, kinds)
    column = lax.broadcasted_iota(jnp.int32, (row_heads, width), 1)
    head = lax.broadcasted_iota(jnp.int32, (row_heads, width), 0) // group
    never = jnp.int32(1 << 20)
    token = jnp.where(
        (column < cached) & (lax.rem(column, kinds) == head), column // kinds, never
    )
    places = [
        jnp.where(column == cached + i * kinds + head, -1, token) for i in range(batch)
    ]
    for copy in copies[:5]:
        copy.wait()
    fill_tables([own_ref], order, keys_ref, values_ref, heads, page)
    live = live_bias(table_ref, [me * slots + s for s in range(slots)], page, 1)
    bias_ref[...] = live_bias(
        table_ref,
        [owner(me, replicas) * slots + s for owner in owners for s in range(slots)],
        page,
        8,
    )
    keys = keys_ref[...]
    values = values_ref[...]
    block_rows = wave * batch * row_heads
    for turn in range(waves):
        copies[5 + turn].wait()
        rows = pl.ds(turn * block_rows, block_rows)
        q = q_ref[rows]
        q_wide = head_concat(q, heads, group)
        wide_ref[rows] = q_wide
        prefix = contract_last(q_wide, keys) * scale + live
        pieces = []
        scores = []
        for i in range(wave * batch):
            request = turn * wave * batch + i
            kv = jnp.concatenate(
                [
                    suffix_ref[request * cached : (request + 1) * cached],
                    new_ref[request // batch * fresh : (request // batch + 1) * fresh],
                ],
                axis=0,
            )
            pieces.append(kv)
            score = contract_last(q[i * row_heads : (i + 1) * row_heads], kv) * scale
            scores.append(
                jnp.where(places[i % batch] < lens_ref[request], score, masked_score)
            )
        score = jnp.concatenate(scores, axis=0)
        row_max = jnp.max(jnp.maximum(prefix, score), axis=1, keepdims=True)
        weights = jnp.exp2(score - row_max)
        prefix_weights = jnp.exp2(prefix - row_max)
        part_ref[rows] = weights + prefix_weights
        max_ref[rows] = jnp.broadcast_to(row_max, weights.shape)
        rounded = pltpu.roll(weights, heads, 1).astype(jnp.bfloat16)
        wide = jnp.dot(
            prefix_weights.astype(jnp.bfloat16), values, preferred_element_type=jnp.float32
        )
        attended = [
            jnp.dot(
                rounded[i * row_heads : (i + 1) * row_heads],
                pieces[i],
                preferred_element_type=jnp.float32,
            )
            for i in range(wave * batch)
        ]
        acc_ref[rows] = jnp.concatenate(attended, axis=0) + head_select(wide, heads, group)


def my_turn():
    odd = lax.rem(lax.axis_index("tensor"), 2) == 1
    replica = lax.axis_index("replica")
    first = replica != 2
    return jnp.where(
        odd, jnp.where(first, 0, 2), jnp.where(replica == 0, 1, 2)
    )


def turn_body(turn, sizes, owners, *refs):
    mine = my_turn()
    inputs, refs = refs[:6], refs[6:]
    if turn > 0:
        done, refs = refs[:5], refs[5:]

        @pl.when(mine < turn)
        def keep():
            for source, target in zip(done, refs[:5]):
                target[...] = source[...]

    @pl.when(mine == turn)
    def work():
        local_body(sizes, owners, *inputs, *refs)


def absorb(sizes, rows, wide_ref, acc_ref, max_ref, part_ref, keys, values, live):
    heads, group, scale = sizes
    score = contract_last(wide_ref[rows], keys) * scale + live
    chunks = [score[:, i : i + lanes] for i in range(0, score.shape[1], lanes)]
    top = functools.reduce(jnp.maximum, chunks)
    earlier = max_ref[rows]
    row_max = jnp.maximum(earlier, jnp.max(top, axis=1, keepdims=True))
    weights = [jnp.exp2(chunk - row_max) for chunk in chunks]
    factor = jnp.exp2(earlier - row_max)
    part = part_ref[rows] * factor + functools.reduce(jnp.add, weights)
    rounded = jnp.concatenate([w.astype(jnp.bfloat16) for w in weights], axis=1)
    wide = jnp.dot(rounded, values, preferred_element_type=jnp.float32)
    return acc_ref[rows] * factor + head_select(wide, heads, group), row_max, part


def fold_body(sizes, place, *refs):
    heads, group, page, scale, block_rows, replicas = sizes
    count_in, wide_ref, acc_in, max_in, part_in, bias_ref = refs[:6]
    raws = refs[6:-6]
    count_ref, acc_ref, max_ref, part_ref, keys_ref, values_ref = refs[-6:]
    count_ref[...] = jnp.broadcast_to(count_in[:1, :1], count_ref.shape)
    kinds = 2 * heads
    fill_tables(raws, page_order(page * kinds, kinds), keys_ref, values_ref, heads, page)
    keys = keys_ref[...]
    values = values_ref[...]
    live = bias_ref[:1, place : place + keys.shape[0]]
    for start in range(0, wide_ref.shape[0], block_rows):
        rows = pl.ds(start, block_rows)
        acc_ref[rows], max_ref[rows], part_ref[rows] = absorb(
            (heads, group, scale), rows, wide_ref, acc_in, max_in, part_in, keys, values, live
        )


def finish_body(sizes, place, *refs):
    heads, group, page, scale, block_rows, replicas = sizes
    count_ref, wide_ref, acc_in, max_in, part_in, bias_ref = refs[:6]
    raws = refs[6:-5]
    out_hbm, out_ref, keys_ref, values_ref, sem = refs[-5:]
    kinds = 2 * heads
    fill_tables(raws, page_order(page * kinds, kinds), keys_ref, values_ref, heads, page)
    keys = keys_ref[...]
    values = values_ref[...]
    live = bias_ref[:1, place : place + keys.shape[0]]
    live_rows = count_ref[:1, :] * (heads * group)
    for start in range(0, wide_ref.shape[0], block_rows):
        rows = pl.ds(start, block_rows)
        acc, row_max, part = absorb(
            (heads, group, scale), rows, wide_ref, acc_in, max_in, part_in, keys, values, live
        )
        total = jnp.broadcast_to(jnp.sum(part, axis=1, keepdims=True), part.shape)
        row = start + lax.broadcasted_iota(jnp.int32, part.shape, 0)
        share = jnp.where(row < live_rows, 1.0 / total, 0.0)
        out_ref[rows] = (acc * share).astype(jnp.bfloat16)
    copy = pltpu.make_async_copy(out_ref, out_hbm, sem)
    copy.start()
    copy.wait()


def vmem():
    return pl.BlockSpec(memory_space=pltpu.VMEM)


def hbm():
    return pl.BlockSpec(memory_space=pltpu.HBM)


def folded_ring(replicas):
    return list(range(0, replicas, 2)) + list(range(1, replicas, 2))[::-1]


def ring_step(values, ring, step):
    return lax.ppermute(
        values, "replica", [(ring[i], ring[(i + step) % len(ring)]) for i in range(len(ring))]
    )


def ring_owner(ring, step):
    def owner(me, n):
        found = jnp.int32(ring[-step])
        for i in range(1, len(ring)):
            found = jnp.where(me == ring[i], ring[(i - step) % len(ring)], found)
        return found

    return owner


def gathered_stages(raw, replicas):
    everything = lax.all_gather(raw, "replica", axis=0, tiled=True)
    owners = [lambda me, n, at=at: jnp.where(me == at, -1, at) for at in range(replicas)]
    together = math.gcd(replicas, 4) * raw.shape[0]
    return [
        [everything[i : i + together]] for i in range(0, everything.shape[0], together)
    ], owners


def shards(replicas, queries, prefix_pool, page_table, suffix_kv, new_kv, suffix_len, counts):
    requests, head_count, width = queries.shape
    slots, page, unused, heads, width = prefix_pool.shape
    suffix = suffix_kv.shape[1]
    group = head_count // heads
    kinds = 2 * heads
    scale = width**-0.5 * math.log2(math.e)
    raw = prefix_pool.reshape(slots * page * kinds, width)
    batch = (-suffix * kinds) % lanes // kinds
    wave = requests // batch
    block_rows = 256
    rows = requests * head_count
    block_tokens = slots * page
    two_ways = replicas == 4
    if two_ways:
        ring = folded_ring(replicas)
        ahead = ring_step(raw, ring, 1)
        owners = [ring_owner(ring, step) for step in (1, -1, 2)]
    else:
        stages, owners = gathered_stages(raw, replicas)
    suffix_rows = requests * suffix * kinds
    full = jax.ShapeDtypeStruct((rows, lanes), jnp.float32)
    params = pltpu.CompilerParams(vmem_limit_bytes=24 << 20)

    def cost(tokens):
        return pl.CostEstimate(
            flops=4 * rows * tokens * width, bytes_accessed=3 << 20, transcendentals=rows * tokens
        )

    def tables(tokens):
        return [pltpu.VMEM((tokens, heads * width), jnp.bfloat16)] * 2

    operands = [
        pltpu.with_memory_space_constraint(value, pltpu.HBM)
        for value in (
            page_table,
            suffix_len,
            queries.reshape(rows, width),
            raw,
            suffix_kv.reshape(suffix_rows, width),
            new_kv.reshape(requests * kinds, width),
        )
    ]

    def local_part(body, done):
        return pl.pallas_call(
            functools.partial(
                body, (heads, group, page, suffix, scale, batch, replicas, wave), owners
            ),
            out_shape=[
                full,
                full,
                full,
                jax.ShapeDtypeStruct((rows, heads * width), jnp.bfloat16),
                jax.ShapeDtypeStruct((8, len(owners) * block_tokens), jnp.float32),
            ],
            in_specs=[hbm()] * 6 + [vmem()] * len(done),
            out_specs=[vmem()] * 5,
            scratch_shapes=[
                pltpu.SMEM(page_table.shape, jnp.int32),
                pltpu.SMEM(suffix_len.shape, jnp.int32),
                pltpu.VMEM((rows, width), jnp.bfloat16),
                pltpu.VMEM(raw.shape, jnp.bfloat16),
                pltpu.VMEM((suffix_rows, width), jnp.bfloat16),
                pltpu.VMEM((requests * kinds, width), jnp.bfloat16),
                *tables(block_tokens),
                pltpu.SemaphoreType.DMA((5 + requests // batch // wave,)),
            ],
            compiler_params=params,
            cost_estimate=cost(2 * block_tokens),
            name="local_part",
        )(*operands, *done)

    if two_ways:
        done = list(local_part(functools.partial(turn_body, 0), []))
        own, done[4] = lax.optimization_barrier((raw, done[4]))
        back = ring_step(own, ring, -1)
        done = list(local_part(functools.partial(turn_body, 1), done))
        ahead, done[4] = lax.optimization_barrier((ahead, done[4]))
        stages = [[ahead, back], [ring_step(ahead, ring, 1)]]
        acc, row_max, part, q_wide, bias = local_part(functools.partial(turn_body, 2), done)
    else:
        acc, row_max, part, q_wide, bias = local_part(local_body, [])
    sizes = (heads, group, page, scale, block_rows, replicas)
    place = 0
    count = jnp.broadcast_to(counts, (8, lanes)) if len(stages) == 1 else counts.reshape(1, 1)
    for blocks in stages[:-1]:
        tokens = sum(block.shape[0] for block in blocks) // kinds
        count, acc, row_max, part = pl.pallas_call(
            functools.partial(fold_body, sizes, place),
            out_shape=[jax.ShapeDtypeStruct((8, lanes), jnp.int32)] + [full] * 3,
            in_specs=[vmem()] * (6 + len(blocks)),
            out_specs=[vmem()] * 4,
            scratch_shapes=tables(tokens),
            compiler_params=params,
            cost_estimate=cost(tokens),
            name="fold_part",
        )(count, q_wide, acc, row_max, part, bias, *blocks)
        place += tokens
    tokens = sum(block.shape[0] for block in stages[-1]) // kinds
    out = pl.pallas_call(
        functools.partial(finish_body, sizes, place),
        out_shape=jax.ShapeDtypeStruct((rows, width), jnp.bfloat16),
        in_specs=[vmem()] * (6 + len(stages[-1])),
        out_specs=hbm(),
        scratch_shapes=[
            pltpu.VMEM((rows, width), jnp.bfloat16),
            *tables(tokens),
            pltpu.SemaphoreType.DMA,
        ],
        compiler_params=params,
        cost_estimate=cost(tokens),
        name="finish_part",
    )(count, q_wide, acc, row_max, part, bias, *stages[-1])
    return out.reshape(requests, head_count, width)


def solution(mesh):
    placed = (
        P(("groups", "replica"), "tensor", None),
        P(("groups", "replica"), None, None, "tensor", None),
        P("groups"),
        P(("groups", "replica"), None, None, "tensor", None),
        P(("groups", "replica"), None, "tensor", None),
        P(("groups", "replica")),
        P(("groups", "replica")),
    )
    return jax.shard_map(
        functools.partial(shards, mesh.shape["replica"]),
        mesh=mesh,
        in_specs=placed,
        out_specs=P(("groups", "replica"), "tensor", None),
        check_vma=False,
    )
```
